256 devices in a mesh: gx: 4 (over x), gy: 8 (over y, core), gz: 8 (over z).
Axes of the slice: x: 4, y: 4, z: 8, core: 2. Of those that a mesh axis runs over, the one named last changes fastest.
Arguments:
- source: float32 [64, 128, 1024], P('gx', 'gy', 'gz'), may hold values from -8 to 8
- conductivity: float32 [64, 128, 1024], P('gx', 'gy', 'gz'), may hold values from 0.25 to 3
Outputs:
- solution: float32 [64, 128, 1024], P('gx', 'gy', 'gz')
- residual: float32 [64, 128, 1024], P('gx', 'gy', 'gz')
The draws below stay inside these ranges and needn't reach their ends.
All inputs are finite; a program needn't handle non-finite values.
Results may differ from the reference program's by a relative error of at most 0.0003.
Values sent between devices are 32-bit elements; how exact they have to be, the bound alone decides.
No kernel may reach another device: no remote copies, remote signals or barrier semaphores. Data moves between devices by JAX's collectives and lax.ppermute only.
A program may use at most 192 MiB of HBM per device.

```python
import math
from functools import partial
import jax
import jax.numpy as jnp
import numpy as np
from jax import lax

LEVELS = 5
DEGREE = 4
CSWEEPS = 32
NX = 64
NY = 128
NZ = 1024


def draw_source(key, part):
    key = jax.random.fold_in(key, 11)
    values = jnp.clip(4.0 * jax.random.normal(key, (NX, NY, NZ), jnp.float32), -8.0, 8.0)
    return values


def draw_conductivity(key, part):
    key = jax.random.fold_in(key, 23)
    pos_x = (jnp.arange(NX, dtype=jnp.float32) + 0.5) / NX
    pos_y = (jnp.arange(NY, dtype=jnp.float32) + 0.5) / NY
    pos_z = (jnp.arange(NZ, dtype=jnp.float32) + 0.5) / NZ
    wave = jnp.sin(2.0 * math.pi * pos_x)[:, None, None] * jnp.sin(2.0 * math.pi * pos_y)[None, :, None]
    wave = wave * jnp.sin(2.0 * math.pi * pos_z)[None, None, :]
    rough = jnp.exp(jax.random.uniform(key, (NX, NY, NZ), jnp.float32, math.log(0.5), math.log(2.0)))
    return (1.0 + 0.5 * wave) * rough


def setup_inputs(seed: int = 0) -> dict:
    seeds = jax.random.split(jax.random.key(seed), 3)
    return {
        "source": draw_source(jax.random.fold_in(seeds[2], 71), 0),
        "conductivity": draw_conductivity(jax.random.fold_in(seeds[2], 71), 0),
    }


smooth_low = 0.6
smooth_high = 2.0
coarse_low = 0.05
coarse_high = 2.0


def harmonic(own_value, other_value):
    return 2.0 * own_value * other_value / (own_value + other_value)


def face_coefficients(conductivity):
    padded = jnp.pad(conductivity, 1, mode="edge")
    return (harmonic(conductivity, padded[:-2, 1:-1, 1:-1]), harmonic(conductivity, padded[2:, 1:-1, 1:-1]),
            harmonic(conductivity, padded[1:-1, :-2, 1:-1]), harmonic(conductivity, padded[1:-1, 2:, 1:-1]),
            harmonic(conductivity, padded[1:-1, 1:-1, :-2]), harmonic(conductivity, padded[1:-1, 1:-1, 2:]))


def stencil(values, padded, coeffs, h_scale):
    summed = coeffs[0] * (values - padded[:-2, 1:-1, 1:-1]) + coeffs[1] * (values - padded[2:, 1:-1, 1:-1])
    summed = summed + coeffs[2] * (values - padded[1:-1, :-2, 1:-1]) + coeffs[3] * (values - padded[1:-1, 2:, 1:-1])
    summed = summed + coeffs[4] * (values - padded[1:-1, 1:-1, :-2]) + coeffs[5] * (values - padded[1:-1, 1:-1, 2:])
    return h_scale * summed


def inverse_diagonal(coeffs, h_scale):
    summed = coeffs[0] + coeffs[1] + coeffs[2] + coeffs[3] + coeffs[4] + coeffs[5]
    return 1.0 / (h_scale * summed)


def cell_mean(values):
    size_x, size_y, size_z = values.shape
    return jnp.mean(values.reshape(size_x // 2, 2, size_y // 2, 2, size_z // 2, 2), axis=(1, 3, 5))


def face_mean(coeff, axis_id, offset):
    size_x, size_y, size_z = coeff.shape
    blocks = coeff.reshape(size_x // 2, 2, size_y // 2, 2, size_z // 2, 2)
    blocks = lax.index_in_dim(blocks, offset, axis=2 * axis_id + 1, keepdims=False)
    kept_dims = [dim_at for dim_at in (1, 3, 5) if dim_at != 2 * axis_id + 1]
    kept_dims = [dim_at - 1 if dim_at > 2 * axis_id + 1 else dim_at for dim_at in kept_dims]
    return jnp.mean(blocks, axis=tuple(kept_dims))


def coarse_coefficients(coeffs):
    return lax.optimization_barrier(tuple(face_mean(coeffs[which], which // 2, which % 2) for which in range(6)))


def prolong(values):
    size_x, size_y, size_z = values.shape
    spread = jnp.broadcast_to(values[:, None, :, None, :, None], (size_x, 2, size_y, 2, size_z, 2))
    return spread.reshape(2 * size_x, 2 * size_y, 2 * size_z)


def chebyshev_terms(sweep_count, lower_bound, upper_bound):
    center = (upper_bound + lower_bound) / 2.0
    half_width = (upper_bound - lower_bound) / 2.0
    sigma_ratio = center / half_width
    rho_now = 1.0 / sigma_ratio
    momentum = []
    push_terms = []
    for sweep_at in range(sweep_count - 1):
        rho_next = 1.0 / (2.0 * sigma_ratio - rho_now)
        momentum.append(rho_next * rho_now)
        push_terms.append(2.0 * rho_next / half_width)
        rho_now = rho_next
    return 1.0 / center, momentum, push_terms


def smooth(operator_fn, inv_diag, right_side, initial, sweep_count, lower_bound, upper_bound):
    first_coef, momentum, push_terms = chebyshev_terms(sweep_count, lower_bound, upper_bound)
    if initial is None:
        update = first_coef * (inv_diag * right_side)
        iterate = update
    else:
        update = first_coef * (inv_diag * (right_side - operator_fn(initial)))
        iterate = initial + update
    iterate, update = lax.optimization_barrier((iterate, update))
    for sweep_at in range(sweep_count - 1):
        update = momentum[sweep_at] * update + push_terms[sweep_at] * (inv_diag * (right_side - operator_fn(iterate)))
        iterate = iterate + update
        iterate, update = lax.optimization_barrier((iterate, update))
    return iterate


def coarse_solve(operator_fn, inv_diag, right_side):
    first_coef, momentum, push_terms = chebyshev_terms(CSWEEPS, coarse_low, coarse_high)
    momentum_table = jnp.asarray(np.array(momentum, dtype=np.float32))
    push_table = jnp.asarray(np.array(push_terms, dtype=np.float32))
    update = first_coef * (inv_diag * right_side)

    def sweep_step(sweep_at, state_pair):
        iterate, update = state_pair
        update = momentum_table[sweep_at] * update + push_table[sweep_at] * (inv_diag * (right_side - operator_fn(iterate)))
        return (iterate + update, update)

    iterate, update = lax.fori_loop(0, CSWEEPS - 1, sweep_step, (update, update))
    return iterate


def apply_level(coeffs, h_scale, values):
    return stencil(values, jnp.pad(values, 1), coeffs, h_scale)


def reference(source, conductivity):
    coeff_list = [lax.optimization_barrier(face_coefficients(conductivity))]
    for level_at in range(1, LEVELS):
        coeff_list.append(coarse_coefficients(coeff_list[-1]))
    scales = [4.0 ** (-level_at) for level_at in range(LEVELS)]
    diags = [inverse_diagonal(coeff_list[level_at], scales[level_at]) for level_at in range(LEVELS)]
    appliers = [partial(apply_level, coeff_list[level_at], scales[level_at]) for level_at in range(LEVELS)]
    rhs_list = [source]
    pre_list = []
    for level_at in range(LEVELS - 1):
        presmooth = smooth(appliers[level_at], diags[level_at], rhs_list[level_at], None, DEGREE, smooth_low, smooth_high)
        pre_list.append(presmooth)
        rhs_list.append(lax.optimization_barrier(cell_mean(rhs_list[level_at] - appliers[level_at](presmooth))))
    current = coarse_solve(appliers[LEVELS - 1], diags[LEVELS - 1], rhs_list[LEVELS - 1])
    for level_at in range(LEVELS - 2, -1, -1):
        current = smooth(appliers[level_at], diags[level_at], rhs_list[level_at], pre_list[level_at] + prolong(current), DEGREE, smooth_low, smooth_high)
    return current, source - appliers[0](current)
```

```python
import functools

import jax
import jax.numpy as jnp
import numpy as np
from jax import lax
from jax.experimental import pallas as pl
from jax.experimental.pallas import tpu as pltpu
from jax.sharding import PartitionSpec as P

F32 = jnp.float32
CSWEEPS = 32
BUDGET = 48 * 1024 * 1024


def chebyshev_terms(sweep_count, lower_bound, upper_bound):
    center = (upper_bound + lower_bound) / 2.0
    half_width = (upper_bound - lower_bound) / 2.0
    sigma_ratio = center / half_width
    rho_now = 1.0 / sigma_ratio
    terms = []
    for _ in range(sweep_count - 1):
        rho_next = 1.0 / (2.0 * sigma_ratio - rho_now)
        terms.append((rho_next * rho_now, 2.0 * rho_next / half_width))
        rho_now = rho_next
    return 1.0 / center, terms


FIRST, TERMS = chebyshev_terms(4, 0.6, 2.0)
CFIRST, CTERMS = chebyshev_terms(CSWEEPS, 0.05, 2.0)


def harmonic(a, b):
    return 2.0 * a * b / (a + b)


def roll(a, shift, axis):
    return pltpu.roll(a, shift % a.shape[axis], axis)


def iota(shape, dim):
    return lax.broadcasted_iota(jnp.int32, shape, dim)


def exact_dot(a, m):
    return jnp.dot(a, m, precision=lax.Precision.HIGHEST, preferred_element_type=F32)


def signed(index, size, cut):
    return jnp.where(index < cut, index, index - size)


def loop(lo, hi, unroll, body):
    count = hi - lo
    assert count % unroll == 0

    def step(t, carry):
        for u in range(unroll):
            body(lo + t * unroll + u)
        return carry

    lax.fori_loop(0, count // unroll, step, 0)


class Level:
    def __init__(self, cx, cy, cz, inv, rhs, wrap):
        self.cx, self.cy, self.cz, self.inv, self.rhs, self.wrap = cx, cy, cz, inv, rhs, wrap

    def around(self, i):
        if self.wrap:
            return (i + self.wrap - 1) & (self.wrap - 1), (i + 1) & (self.wrap - 1)
        return i - 1, i + 1

    def defect(self, v, i):
        below, above = self.around(i)
        here = v[i]
        cy, cz = self.cy[i], self.cz[i]
        total = self.cx[i] * v[below] + self.cx[above] * v[above]
        total = total + (cy * roll(here, 1, 0) + roll(cy * here, -1, 0))
        total = total + (cz * roll(here, 1, 1) + roll(cz * here, -1, 1))
        return here, self.rhs[i] - here + self.inv[i] * total


def sweep(level, src, dst, upd, lo, hi, unroll, momentum, push, store_update=True):
    def body(i):
        here, d = level.defect(src, i)
        e = push * d
        if momentum is not None:
            e = momentum * upd[i] + e
        if store_update:
            upd[i] = e
        dst[i] = here + e

    loop(lo, hi, unroll, body)


def z_pack(get, planes, rows, starts, width, per):
    lane = iota((rows, 128), 1)
    out = []
    for start in starts:
        tiles = []
        for g in range(0, planes, per):
            acc = jnp.zeros((rows, 128), F32)
            for p in range(g, min(g + per, planes)):
                plane, base = get(p)
                at = (p - g) * width
                moved = roll(plane, at - start - base, 1)
                acc = jnp.where((lane >= at) & (lane < at + width), moved, acc)
            tiles.append(acc)
        out.append(tiles)
    return out


def pack0(f_ref, b_ref, up_ref, down_ref):
    for ref, start_f, start_b in ((up_ref, 120, 119), (down_ref, 0, 0)):
        (tiles,) = z_pack(lambda p: (f_ref[p], 0), 32, 32, (start_f,), 8, 16)
        for g, t in enumerate(tiles):
            ref[g] = t
        (tiles,) = z_pack(lambda p: (b_ref[p + 1], 0), 32, 32, (start_b,), 9, 14)
        for g, t in enumerate(tiles):
            ref[2 + g] = t


def fine_down(
    f_ref, b_ref, ylo_ref, yhi_ref, zlo_ref, zhi_ref,
    u_ref, cx_ref, cy_ref, cz_ref, inv_ref, rhs_ref, diag_ref, xp_ref,
    bw, ew, va, vb, upd, cxw, dw, scr,
):
    px, py, pz = lax.axis_index("gx"), lax.axis_index("gy"), lax.axis_index("gz")
    lane1 = iota((32, 128), 1)
    lane = iota((32, 256), 1)
    row = iota((32, 256), 0)
    for i in range(34):
        q = min(max(i - 1, 0), 31)
        g, at = q // 14, (q % 14) * 9
        right = roll(zhi_ref[2 + g], -at, 1)
        left = roll(zlo_ref[2 + g], 119 - at, 1)
        bw[i, :, 0:128] = b_ref[i]
        bw[i, :, 128:256] = jnp.where(lane1 < 9, right, jnp.where(lane1 >= 119, left, 1.0))
    for i in range(32):
        g, at = i // 16, (i % 16) * 8
        right = roll(zhi_ref[g], -at, 1)
        left = roll(zlo_ref[g], 120 - at, 1)
        va[i, :, 0:128] = f_ref[i]
        va[i, :, 128:256] = jnp.where(lane1 < 8, right, jnp.where(lane1 >= 120, left, 0.0))
    y_at = (16 * py + signed(row, 32, 24)) & 127
    z_at = (128 * pz + signed(lane, 256, 192)) & 1023
    y_open = jnp.where(y_at == 0, 0.0, 1.0)
    z_open = jnp.where(z_at == 0, 0.0, 1.0)
    y_edge = jnp.where((y_at == 0) | (y_at == 127), 1.0, 0.0)
    z_edge = jnp.where((z_at == 0) | (z_at == 1023), 1.0, 0.0)

    def x_at(i):
        return (16 * px + (i + 56)) & 63

    def face_x(i):
        open_x = jnp.where(x_at(i) == 0, 0.0, 1.0).astype(F32)
        cxw[i] = open_x * harmonic(bw[i + 1], bw[i])

    loop(0, 33, 1, face_x)

    def coefficients(i):
        b = bw[i + 1]
        e_at = jnp.clip(i - 8, 0, 15)
        below = ylo_ref[pl.ds(e_at, 1), :]
        above = yhi_ref[pl.ds(e_at, 1), :]
        below = jnp.concatenate([below, below], axis=1)
        above = jnp.concatenate([above, above], axis=1)
        before = jnp.where(row == 24, jnp.broadcast_to(below, (32, 256)), roll(b, 1, 0))
        cy = y_open * harmonic(b, before)
        outer = harmonic(b[16:24], jnp.broadcast_to(above, (8, 256))) * y_open_next
        after = roll(cy, -1, 0)
        after = jnp.concatenate(
            [after[0:16], jnp.where(row[16:24] == 23, outer, after[16:24]), after[24:32]], axis=0
        )
        cz = z_open * harmonic(b, roll(b, 1, 1))
        own = harmonic(b, b)
        x_edge = jnp.where((x_at(i) == 0) | (x_at(i) == 63), 1.0, 0.0).astype(F32)
        e = own * (y_edge + z_edge + x_edge)
        d = cxw[i] + cxw[i + 1] + (cy + after) + (cz + roll(cz, -1, 1)) + e
        inv = 1.0 / d
        cx_ref[i] = cxw[i]
        cy_ref[i] = cy
        cz_ref[i] = cz
        inv_ref[i] = inv
        ew[i] = e
        dw[i] = d
        g = va[i] * inv
        rhs_ref[i] = g
        first = FIRST * g
        upd[i] = first
        va[i] = first

    y_next = (16 * py + 24) & 127
    y_open_next = jnp.where(y_next == 0, 0.0, 1.0).astype(F32)
    loop(0, 32, 2, coefficients)
    level = Level(cx_ref, cy_ref, cz_ref, inv_ref, rhs_ref, 0)
    sweep(level, va, vb, upd, 1, 31, 2, *TERMS[0])
    sweep(level, vb, va, upd, 2, 30, 2, *TERMS[1])
    sweep(level, va, u_ref, upd, 3, 29, 2, *TERMS[2], store_update=False)

    def save_diag(i):
        diag_ref[i] = dw[i + 8, 0:16, 0:128]

    loop(0, 16, 4, save_diag)

    def put(a, p, value):
        scr[a, 0, p * 32 : p * 32 + 32, :] = value[:, 0:128]
        scr[a, 1, p * 32 : p * 32 + 32, :] = value[:, 128:256]

    for p in range(8):
        i = 8 + 2 * p
        total = None
        for k in (i, i + 1):
            _, d = level.defect(u_ref, k)
            r = dw[k] * d
            total = r if total is None else total + r
        put(0, p, 0.125 * total)
        put(1, p, 0.25 * cx_ref[i])
        put(2, p, 0.25 * (cy_ref[i] + cy_ref[i + 1]))
        put(3, p, 0.25 * (cz_ref[i] + cz_ref[i + 1]))
        put(4, p, 0.25 * (ew[i] + ew[i + 1]))
    fine_lane = iota((256, 128), 0)
    coarse_lane = iota((256, 128), 1)
    both = jnp.where((fine_lane >> 1) == coarse_lane, 1.0, 0.0)
    even = jnp.where(fine_lane == 2 * coarse_lane, 1.0, 0.0)
    half = iota((8, 128), 1) < 64
    for a in range(5):
        def rows_of(offset):
            return jnp.concatenate(
                [scr[a, t, pl.ds(offset, 128, stride=2), :] for t in range(2)], axis=1
            )

        folded = rows_of(0)
        if a != 2:
            folded = folded + rows_of(1)
        res = exact_dot(folded, even if a == 3 else both)
        for j in range(4):
            for t in range(2):
                lo = res[j * 16 + t * 8 : j * 16 + t * 8 + 8]
                hi = res[(j + 4) * 16 + t * 8 : (j + 4) * 16 + t * 8 + 8]
                xp_ref[a, j, t * 8 : t * 8 + 8, :] = jnp.where(half, lo, roll(hi, 64, 1))


def pack1(w_ref, up_ref, down_ref):
    for a in range(5):
        def get(p):
            k, j = p // 8, p % 8
            return w_ref[a, 4 * k + j % 4], 64 * (j // 4)

        ups, downs = z_pack(get, 32, 32, (53, 0), 11, 11)
        for g in range(3):
            up_ref[a, g] = ups[g]
            down_ref[a, g] = downs[g]


def pair_matrices(cut, size_in=128):
    fine = iota((size_in, 128), 0)
    coarse = iota((size_in, 128), 1)
    at = signed(fine, size_in, cut)
    both = jnp.where(((at >> 1) & 127) == coarse, 1.0, 0.0)
    even = jnp.where((((at >> 1) & 127) == coarse) & ((at & 1) == 0), 1.0, 0.0)
    return both, even


def restrict(scr, both, even, count):
    out = []
    for a in range(5):
        folded = scr[a, pl.ds(0, count, stride=2), :]
        if a != 2:
            folded = folded + scr[a, pl.ds(1, count, stride=2), :]
        out.append(exact_dot(folded, even if a == 3 else both))
    return out


def mid_down(
    w_ref, zlo_ref, zhi_ref,
    u_ref, cx_ref, cy_ref, cz_ref, inv_ref, rhs_ref, own_ref, ym_ref, yp_ref,
    va, vb, upd, ew, dw, scr,
):
    lane = iota((32, 128), 1)
    targets = (va, cx_ref, cy_ref, cz_ref, ew)
    for a in range(5):
        fill = 1.0 if a == 4 else 0.0
        for p in range(32):
            k, j = p // 8, p % 8
            base = w_ref[a, 4 * k + j % 4]
            if j >= 4:
                base = roll(base, 64, 1)
            g, at = p // 11, (p % 11) * 11
            right = roll(zhi_ref[a, g], 64 - at, 1)
            left = roll(zlo_ref[a, g], 117 - at, 1)
            halo = jnp.where(lane < 75, right, jnp.where(lane >= 117, left, fill))
            targets[a][p] = jnp.where(lane < 64, base, halo)

    def coefficients(i):
        above = (i + 1) & 31
        cy, cz = cy_ref[i], cz_ref[i]
        d = cx_ref[i] + cx_ref[above] + (cy + roll(cy, -1, 0)) + (cz + roll(cz, -1, 1)) + ew[i]
        inv = 1.0 / d
        inv_ref[i] = inv
        dw[i] = d
        g = 4.0 * va[i] * inv
        rhs_ref[i] = g
        first = FIRST * g
        upd[i] = first
        va[i] = first

    loop(0, 32, 4, coefficients)
    level = Level(cx_ref, cy_ref, cz_ref, inv_ref, rhs_ref, 32)
    sweep(level, va, vb, upd, 0, 32, 4, *TERMS[0])
    sweep(level, vb, va, upd, 0, 32, 4, *TERMS[1])
    sweep(level, va, u_ref, upd, 0, 32, 4, *TERMS[2], store_update=False)
    for p in range(16):
        i = 2 * p
        _, d0 = level.defect(u_ref, i)
        _, d1 = level.defect(u_ref, i + 1)
        at = slice(32 * p, 32 * p + 32)
        scr[0, at, :] = 0.03125 * (dw[i] * d0 + dw[i + 1] * d1)
        scr[1, at, :] = 0.25 * cx_ref[i]
        scr[2, at, :] = 0.25 * (cy_ref[i] + cy_ref[i + 1])
        scr[3, at, :] = 0.25 * (cz_ref[i] + cz_ref[i + 1])
        scr[4, at, :] = 0.25 * (ew[i] + ew[i + 1])
    both, even = pair_matrices(96)
    f, cx, cy, cz, e = [r.reshape(16, 16, 128) for r in restrict(scr, both, even, 256)]
    cx_next = jnp.concatenate([cx[1:], cx[:1]], axis=0)
    planes = []
    for p in range(16):
        d = cx[p] + cx_next[p] + (cy[p] + roll(cy[p], -1, 0)) + (cz[p] + roll(cz[p], -1, 1)) + e[p]
        planes.append((f[p], cx[p], cy[p], cz[p], d))
    lane8 = iota((16, 128), 1)
    for a in range(5):
        for j in range(4):
            packed = planes[j][a]
            for k in range(1, 4):
                packed = jnp.where(lane8 >= 32 * k, roll(planes[4 * k + j][a], 32 * k, 1), packed)
            own_ref[a, j] = packed
            ym_ref[a, j] = roll(packed, 1, 0)[0:8]
            yp_ref[a, j] = roll(packed, 3, 0)[0:8]


def pack2(w_ref, up_ref, down_ref):
    for a in range(5):
        def get(p):
            return w_ref[a, p % 4], 32 * (p // 4)

        ups, downs = z_pack(get, 16, 32, (21, 0), 11, 11)
        for g in range(2):
            up_ref[a, g] = ups[g]
            down_ref[a, g] = downs[g]


def low_down(
    w_ref, zlo_ref, zhi_ref,
    u_ref, cx_ref, cy_ref, cz_ref, inv_ref, rhs_ref, own_ref,
    va, vb, upd, dw, scr,
):
    lane = iota((32, 128), 1)
    targets = (va, cx_ref, cy_ref, cz_ref, dw)
    for a in range(5):
        fill = 1.0 if a == 4 else 0.0
        for p in range(16):
            base = roll(w_ref[a, p % 4], -32 * (p // 4), 1)
            g, at = p // 11, (p % 11) * 11
            right = roll(zhi_ref[a, g], 32 - at, 1)
            left = roll(zlo_ref[a, g], 117 - at, 1)
            halo = jnp.where(lane < 43, right, jnp.where(lane >= 117, left, fill))
            targets[a][p] = jnp.where(lane < 32, base, halo)

    def coefficients(i):
        inv = 1.0 / dw[i]
        inv_ref[i] = inv
        g = 16.0 * va[i] * inv
        rhs_ref[i] = g
        first = FIRST * g
        upd[i] = first
        va[i] = first

    loop(0, 16, 4, coefficients)
    level = Level(cx_ref, cy_ref, cz_ref, inv_ref, rhs_ref, 16)
    sweep(level, va, vb, upd, 0, 16, 4, *TERMS[0])
    sweep(level, vb, va, upd, 0, 16, 4, *TERMS[1])
    sweep(level, va, u_ref, upd, 0, 16, 4, *TERMS[2], store_update=False)

    def edge(i):
        above = (i + 1) & 15
        cy, cz = cy_ref[i], cz_ref[i]
        inner = cx_ref[i] + cx_ref[above] + (cy + roll(cy, -1, 0)) + (cz + roll(cz, -1, 1))
        return dw[i] - inner

    for p in range(8):
        i = 2 * p
        _, d0 = level.defect(u_ref, i)
        _, d1 = level.defect(u_ref, i + 1)
        at = slice(32 * p, 32 * p + 32)
        scr[0, at, :] = 0.0078125 * (dw[i] * d0 + dw[i + 1] * d1)
        scr[1, at, :] = 0.25 * cx_ref[i]
        scr[2, at, :] = 0.25 * (cy_ref[i] + cy_ref[i + 1])
        scr[3, at, :] = 0.25 * (cz_ref[i] + cz_ref[i + 1])
        scr[4, at, :] = 0.25 * (edge(i) + edge(i + 1))
    both, even = pair_matrices(96)
    f, cx, cy, cz, e = [r.reshape(8, 16, 128) for r in restrict(scr, both, even, 128)]
    planes = []
    for p in range(8):
        inner = cx[p] + cx[(p + 1) % 8] + (cy[p] + roll(cy[p], -1, 0))
        d = inner + (cz[p] + roll(cz[p], -1, 1)) + e[p]
        planes.append((f[p], cx[p], cy[p], cz[p], d))
    lane16 = iota((16, 128), 1)
    for a in range(5):
        packed = planes[0][a]
        for p in range(1, 8):
            packed = jnp.where(lane16 >= 16 * p, roll(planes[p][a], 16 * p, 1), packed)
        own_ref[a] = roll(packed, 3, 0)[0:8]


def spread(dup, w, rows, matrix):
    count = w.shape[0]
    dup[pl.ds(0, count, stride=2), :] = w
    dup[pl.ds(1, count, stride=2), :] = w
    return exact_dot(dup[0 : 2 * count, :], matrix)


def spread_matrix(cut, size):
    coarse = iota((128, size), 0)
    at = signed(iota((128, size), 1), size, cut)
    return jnp.where(((at >> 1) & 127) == coarse, 1.0, 0.0)


def post(level, va, vb, upd, ranges, unroll):
    lo, hi = ranges[0]
    sweep(level, va, vb, upd, lo, hi, unroll, None, FIRST)
    src, dst = vb, va
    for n in range(3):
        lo, hi = ranges[n + 1]
        sweep(level, src, dst, upd, lo, hi, unroll, *TERMS[n], store_update=n < 2)
        src, dst = dst, src


def up(
    g_ref,
    u2, cx2, cy2, cz2, inv2, rhs2,
    u1, cx1, cy1, cz1, inv1, rhs1,
    u0, cx0, cy0, cz0, inv0, rhs0, diag0,
    sol_ref, res_ref,
    l3, inv3, rhs3, u3, va3, vb3, upd3, scr3,
    va2, vb2, upd2, dup2, va1, vb1, upd1, dup1, va0, vb0, upd0, dup0,
):
    me = lax.axis_index("gz")
    lane = iota((16, 128), 1)
    for a in range(5):
        tiles = [roll(g_ref[(me + k) & 7, a], -3, 0) for k in range(8)]
        for p in range(8):
            plane = roll(tiles[0], -16 * p, 1)
            for k in range(1, 8):
                plane = jnp.where(lane >= 16 * k, roll(tiles[k], 16 * (k - p), 1), plane)
            l3[a, p] = plane
    f3, cx3, cy3, cz3, d3 = [l3.at[a] for a in range(5)]
    level = Level(cx3, cy3, cz3, inv3, rhs3, 8)

    def start3(i):
        inv = 1.0 / d3[i]
        inv3[i] = inv
        g = 64.0 * f3[i] * inv
        rhs3[i] = g
        first = FIRST * g
        upd3[i] = first
        va3[i] = first

    loop(0, 8, 8, start3)
    sweep(level, va3, vb3, upd3, 0, 8, 8, *TERMS[0])
    sweep(level, vb3, va3, upd3, 0, 8, 8, *TERMS[1])
    sweep(level, va3, u3, upd3, 0, 8, 8, *TERMS[2], store_update=False)
    for p in range(4):
        i = 2 * p
        _, r0 = level.defect(u3, i)
        _, r1 = level.defect(u3, i + 1)
        at = slice(16 * p, 16 * p + 16)
        scr3[0, at, :] = (0.125 / 64.0) * (d3[i] * r0 + d3[i + 1] * r1)
        scr3[1, at, :] = 0.25 * cx3[i]
        scr3[2, at, :] = 0.25 * (cy3[i] + cy3[i + 1])
        scr3[3, at, :] = 0.25 * (cz3[i] + cz3[i + 1])
        total = None
        for k in (i, i + 1):
            cy, cz = cy3[k], cz3[k]
            inner = cx3[k] + cx3[(k + 1) % 8] + (cy + roll(cy, -1, 0))
            inner = inner + (cz + roll(cz, -1, 1))
            total = d3[k] - inner if total is None else total + (d3[k] - inner)
        scr3[4, at, :] = 0.25 * total
    fine = iota((128, 128), 0)
    coarse = iota((128, 128), 1) & 63
    both = jnp.where((fine >> 1) == coarse, 1.0, 0.0)
    even = jnp.where(fine == 2 * coarse, 1.0, 0.0)
    f, cx, cy, cz, e = restrict(scr3, both, even, 32)

    def cut(a, p):
        return a[8 * p : 8 * p + 8]

    fs, cxs, cys, czs = [[cut(a, p) for p in range(4)] for a in (f, cx, cy, cz)]
    invs, gs, vs, es = [], [], [], []
    for p in range(4):
        d = cxs[p] + cxs[(p + 1) % 4] + (cys[p] + roll(cys[p], -1, 0))
        d = d + (czs[p] + roll(czs[p], -1, 1)) + cut(e, p)
        invs.append(1.0 / d)
        gs.append(256.0 * fs[p] * invs[p])
        es.append(CFIRST * gs[p])
        vs.append(es[p])
    xlo = [invs[p] * cxs[p] for p in range(4)]
    xhi = [invs[p] * cxs[(p + 1) % 4] for p in range(4)]
    ylo = [invs[p] * cys[p] for p in range(4)]
    yhi = [invs[p] * roll(cys[p], -1, 0) for p in range(4)]
    zlo = [invs[p] * czs[p] for p in range(4)]
    zhi = [invs[p] * roll(czs[p], -1, 1) for p in range(4)]
    for momentum, push in CTERMS:
        momentum, push = float(np.float32(momentum)), float(np.float32(push))
        new_v, new_e = [], []
        for p in range(4):
            v = vs[p]
            total = xlo[p] * vs[(p + 3) % 4] + xhi[p] * vs[(p + 1) % 4]
            total = total + (ylo[p] * roll(v, 1, 0) + yhi[p] * roll(v, -1, 0))
            total = total + (zlo[p] * roll(v, 1, 1) + zhi[p] * roll(v, -1, 1))
            ne = momentum * es[p] + push * ((gs[p] - v) + total)
            new_e.append(ne)
            new_v.append(v + ne)
        vs, es = new_v, new_e
    w4 = jnp.concatenate(vs, axis=0)
    fine = iota((128, 128), 1)
    coarse = iota((128, 128), 0)
    m = jnp.where((fine >> 1) == coarse, 1.0, 0.0)
    wide = spread(dup2, w4, 8, m)
    for i in range(8):
        p = i // 2
        va3[i] = u3[i] + wide[16 * p : 16 * p + 16]
    post(level, va3, vb3, upd3, [(0, 8)] * 4, 8)
    w3 = va3[...].reshape(128, 128)
    wide = spread(dup2, w3, 16, spread_matrix(96, 128))
    for i in range(16):
        p = i // 2
        va2[i] = u2[i] + wide[32 * p : 32 * p + 32]
    level = Level(cx2, cy2, cz2, inv2, rhs2, 16)
    post(level, va2, vb2, upd2, [(0, 16)] * 4, 4)
    w2 = jnp.concatenate([va2[:, 0:8, :], va2[:, 24:32, :]], axis=1).reshape(256, 128)
    wide = spread(dup1, w2, 16, spread_matrix(96, 128))
    for i in range(32):
        p = i // 2
        va1[i] = u1[i] + wide[32 * p : 32 * p + 32]
    level = Level(cx1, cy1, cz1, inv1, rhs1, 32)
    post(level, va1, vb1, upd1, [(0, 32)] * 4, 4)
    rows = [
        jnp.concatenate([va1[i % 32, 0:8, :], mix_rows(va1, i % 32)], axis=0) for i in range(-4, 12)
    ]
    w1 = jnp.concatenate(rows, axis=0)
    wide = spread(dup0, w1, 16, spread_matrix(192, 256))
    for i in range(3, 29):
        p = i // 2
        va0[i] = u0[i] + wide[32 * p : 32 * p + 32]
    level = Level(cx0, cy0, cz0, inv0, rhs0, 0)
    post(level, va0, vb0, upd0, [(4, 28), (5, 27), (6, 26), (7, 25)], 2)

    def finish(i):
        here, d = level.defect(va0, i)
        sol_ref[i - 8] = here[0:16, 0:128]
        res_ref[i - 8] = diag0[i - 8] * d[0:16, 0:128]

    loop(8, 24, 2, finish)


def mix_rows(ref, i):
    low = iota((8, 128), 0) < 4
    return jnp.where(low, ref[i, 8:16, :], ref[i, 24:32, :])


def call(body, args, outs, scratch=()):
    return pl.pallas_call(
        body,
        out_shape=[jax.ShapeDtypeStruct(s, F32) for s in outs],
        scratch_shapes=[pltpu.VMEM(s, F32) for s in scratch],
        compiler_params=pltpu.CompilerParams(vmem_limit_bytes=BUDGET),
        name=body.__name__,
    )(*args)


def move(values, axis, shift):
    size = lax.axis_size(axis)
    return lax.ppermute(values, axis, [((i + shift) % size, i) for i in range(size)])


def local(source, conductivity):
    f, b = source, conductivity
    from_lo = move(jnp.concatenate([f[8:16], b[7:16]]), "gx", -1)
    from_hi = move(jnp.concatenate([f[0:8], b[0:9]]), "gx", 1)
    fx = jnp.concatenate([from_lo[:8], f, from_hi[:8]])
    bx = jnp.concatenate([from_lo[8:], b, from_hi[8:]])

    def y_slab(at, edge):
        return jnp.concatenate(
            [fx[:, at : at + 8], bx[1:33, at : at + 8], bx[9:25, edge].reshape(2, 8, 128)]
        )

    from_lo = move(y_slab(8, 7), "gy", -1)
    from_hi = move(y_slab(0, 8), "gy", 1)
    fw = jnp.concatenate([fx, from_hi[:32], from_lo[:32]], axis=1)
    inner = jnp.concatenate([bx[1:33], from_hi[32:64], from_lo[32:64]], axis=1)
    first = jnp.concatenate([bx[:1], bx[:1]], axis=1)
    last = jnp.concatenate([bx[33:], bx[33:]], axis=1)
    bw = jnp.concatenate([first, inner, last])
    ylo, yhi = from_lo[64:].reshape(16, 128), from_hi[64:].reshape(16, 128)
    up0, down0 = call(pack0, (fw, bw), [(5, 32, 128)] * 2)
    zlo, zhi = move(up0, "gz", -1), move(down0, "gz", 1)
    big = (32, 32, 256)
    u0, cx0, cy0, cz0, inv0, rhs0, diag0, xp = call(
        fine_down,
        (fw, bw, ylo, yhi, zlo, zhi),
        [big] * 6 + [(16, 16, 128), (5, 4, 16, 128)],
        [(34, 32, 256), big, big, big, big, (33, 32, 256), big, (5, 2, 256, 128)],
    )
    x_all = jnp.concatenate([xp] + [move(xp, "gx", k) for k in (1, 2, 3)], axis=1)
    own, halo = x_all[:, :, 0:8], x_all[:, :, 8:16]

    def with_rows(at):
        part = halo[:, :, at : at + 4]
        return jnp.concatenate(
            [own, jnp.concatenate([part[:, :8], part[:, 8:]], axis=2)], axis=1
        )

    from_hi = move(with_rows(0), "gy", 1)
    from_lo = move(with_rows(4), "gy", -1)

    def unfold(got):
        part = got[:, 16:]
        return jnp.concatenate([part[:, :, 0:4], part[:, :, 4:8]], axis=1)

    w1 = jnp.concatenate(
        [own, from_hi[:, :16], unfold(from_hi), unfold(from_lo), from_lo[:, :16]], axis=2
    )
    up1, down1 = call(pack1, (w1,), [(5, 3, 32, 128)] * 2)
    zlo, zhi = move(up1, "gz", -1), move(down1, "gz", 1)
    mid = (32, 32, 128)
    u1, cx1, cy1, cz1, inv1, rhs1, own2, ym, yp = call(
        mid_down,
        (w1, zlo, zhi),
        [mid] * 6 + [(5, 4, 16, 128), (5, 4, 8, 128), (5, 4, 8, 128)],
        [mid] * 5 + [(5, 512, 128)],
    )
    from_hi, from_lo = move(ym, "gy", 2), move(yp, "gy", -2)
    w2 = jnp.concatenate(
        [own2[:, :, 0:7], from_hi, own2[:, :, 7:13], from_lo, own2[:, :, 13:16]], axis=2
    )
    up2, down2 = call(pack2, (w2,), [(5, 2, 32, 128)] * 2)
    zlo, zhi = move(up2, "gz", -1), move(down2, "gz", 1)
    low = (16, 32, 128)
    u2, cx2, cy2, cz2, inv2, rhs2, own3 = call(
        low_down,
        (w2, zlo, zhi),
        [low] * 6 + [(5, 8, 128)],
        [low] * 4 + [(5, 256, 128)],
    )
    both = jnp.concatenate([own3, move(own3, "gy", 4)], axis=1)
    everyone = jnp.broadcast_to(both[None], (8, 5, 16, 128))
    gathered = lax.all_to_all(everyone, "gz", 0, 0)
    tiny = (8, 16, 128)
    return tuple(
        call(
            up,
            (
                gathered,
                u2, cx2, cy2, cz2, inv2, rhs2,
                u1, cx1, cy1, cz1, inv1, rhs1,
                u0, cx0, cy0, cz0, inv0, rhs0, diag0,
            ),
            [(16, 16, 128)] * 2,
            [(5,) + tiny] + [tiny] * 6 + [(5, 64, 128)]
            + [low] * 3 + [(256, 128)] + [mid] * 3 + [(512, 128)] + [big] * 3 + [(512, 128)],
        )
    )


def solution(mesh):
    spec = P("gx", "gy", "gz")
    return jax.shard_map(
        local, mesh=mesh, in_specs=(spec, spec), out_specs=(spec, spec), check_vma=False
    )
```

```python
import functools

import jax
import jax.numpy as jnp
import numpy as np
from jax import lax
from jax.experimental import pallas as pl
from jax.experimental.pallas import tpu as pltpu
from jax.sharding import PartitionSpec as P

F32 = jnp.float32
CSWEEPS = 32
MIB = 1024 * 1024
WIDE = 4


def chebyshev_terms(sweep_count, lower_bound, upper_bound):
    center = (upper_bound + lower_bound) / 2.0
    half_width = (upper_bound - lower_bound) / 2.0
    sigma_ratio = center / half_width
    rho_now = 1.0 / sigma_ratio
    terms = []
    for _ in range(sweep_count - 1):
        rho_next = 1.0 / (2.0 * sigma_ratio - rho_now)
        terms.append((rho_next * rho_now, 2.0 * rho_next / half_width))
        rho_now = rho_next
    return 1.0 / center, terms


FIRST, TERMS = chebyshev_terms(4, 0.6, 2.0)
CFIRST, CTERMS = chebyshev_terms(CSWEEPS, 0.05, 2.0)


def harmonic(a, b):
    return 2.0 * a * b / (a + b)


def roll(a, shift, axis):
    return pltpu.roll(a, shift % a.shape[axis], axis)


def iota(shape, dim):
    return lax.broadcasted_iota(jnp.int32, shape, dim)


def exact_dot(a, m):
    return jnp.dot(a, m, precision=lax.Precision.HIGHEST, preferred_element_type=F32)


def signed(index, size, cut):
    return jnp.where(index < cut, index, index - size)


def loop(lo, hi, unroll, body):
    count = hi - lo
    unroll = max(u for u in range(1, unroll * WIDE + 1) if count % u == 0)

    def step(t, carry):
        for u in range(unroll):
            body(lo + t * unroll + u)
        return carry

    lax.fori_loop(0, count // unroll, step, 0)


def copies_of(sources, targets, sems):
    return [pltpu.make_async_copy(a, b, s) for a, b, s in zip(sources, targets, sems)]


class Level:
    def __init__(self, cx, cy, cz, inv, rhs, wrap):
        self.cx, self.cy, self.cz, self.inv, self.rhs, self.wrap = cx, cy, cz, inv, rhs, wrap

    def around(self, i):
        if self.wrap:
            return (i + self.wrap - 1) & (self.wrap - 1), (i + 1) & (self.wrap - 1)
        return i - 1, i + 1

    def defect(self, v, i):
        below, above = self.around(i)
        here = v[i]
        cy, cz = self.cy[i], self.cz[i]
        total = self.cx[i] * v[below] + self.cx[above] * v[above]
        total = total + (cy * roll(here, 1, 0) + roll(cy * here, -1, 0))
        total = total + (cz * roll(here, 1, 1) + roll(cz * here, -1, 1))
        return here, self.rhs[i] - here + self.inv[i] * total


def sweep(level, src, dst, upd, lo, hi, unroll, momentum, push, store_update=True):
    def body(i):
        here, d = level.defect(src, i)
        e = push * d
        if momentum is not None:
            e = momentum * upd[i] + e
        if store_update:
            upd[i] = e
        dst[i] = here + e

    loop(lo, hi, unroll, body)


def z_pack(get, planes, rows, starts, width, per):
    lane = iota((rows, 128), 1)
    out = []
    for start in starts:
        tiles = []
        for g in range(0, planes, per):
            acc = jnp.zeros((rows, 128), F32)
            for p in range(g, min(g + per, planes)):
                plane, base = get(p)
                at = (p - g) * width
                moved = roll(plane, at - start - base, 1)
                acc = jnp.where((lane >= at) & (lane < at + width), moved, acc)
            tiles.append(acc)
        out.append(tiles)
    return out


def packx0(f_ref, b_ref, up_ref, down_ref, *sems):
    pairs = (
        (f_ref.at[8:16], up_ref.at[0:8]),
        (b_ref.at[7:16], up_ref.at[8:17]),
        (f_ref.at[0:8], down_ref.at[0:8]),
        (b_ref.at[0:9], down_ref.at[8:17]),
    )
    moves = [pltpu.make_async_copy(a, b, s) for (a, b), s in zip(pairs, sems)]
    for m in moves:
        m.start()
    for m in moves:
        m.wait()


def pack0(f_ref, b_ref, up_ref, down_ref):
    for ref, start_f, start_b in ((up_ref, 120, 119), (down_ref, 0, 0)):
        (tiles,) = z_pack(lambda p: (f_ref[p], 0), 32, 32, (start_f,), 8, 16)
        for g, t in enumerate(tiles):
            ref[g] = t
        (tiles,) = z_pack(lambda p: (b_ref[p + 1], 0), 32, 32, (start_b,), 9, 14)
        for g, t in enumerate(tiles):
            ref[2 + g] = t


def fine_down(
    f_ref, b_ref, ylo_ref, yhi_ref, zlo_ref, zhi_ref,
    u_far, cx_far, cy_far, cz_far, inv_far, rhs_far, diag_ref, xp_ref,
    u_ref, cx_ref, cy_ref, cz_ref, inv_ref, rhs_ref,
    bw, ew, va, vb, upd, cxw, dw, scr, *sems,
):
    saves = copies_of(
        (cx_ref, cy_ref, cz_ref, inv_ref, rhs_ref, u_ref),
        (cx_far, cy_far, cz_far, inv_far, rhs_far, u_far),
        sems,
    )
    px, py, pz = lax.axis_index("gx"), lax.axis_index("gy"), lax.axis_index("gz")
    lane1 = iota((32, 128), 1)
    lane = iota((32, 256), 1)
    row = iota((32, 256), 0)
    for i in range(34):
        q = min(max(i - 1, 0), 31)
        g, at = q // 14, (q % 14) * 9
        right = roll(zhi_ref[2 + g], -at, 1)
        left = roll(zlo_ref[2 + g], 119 - at, 1)
        bw[i, :, 0:128] = b_ref[i]
        bw[i, :, 128:256] = jnp.where(lane1 < 9, right, jnp.where(lane1 >= 119, left, 1.0))
    for i in range(32):
        g, at = i // 16, (i % 16) * 8
        right = roll(zhi_ref[g], -at, 1)
        left = roll(zlo_ref[g], 120 - at, 1)
        va[i, :, 0:128] = f_ref[i]
        va[i, :, 128:256] = jnp.where(lane1 < 8, right, jnp.where(lane1 >= 120, left, 0.0))
    y_at = (16 * py + signed(row, 32, 24)) & 127
    z_at = (128 * pz + signed(lane, 256, 192)) & 1023
    y_open = jnp.where(y_at == 0, 0.0, 1.0)
    z_open = jnp.where(z_at == 0, 0.0, 1.0)
    y_edge = jnp.where((y_at == 0) | (y_at == 127), 1.0, 0.0)
    z_edge = jnp.where((z_at == 0) | (z_at == 1023), 1.0, 0.0)

    def x_at(i):
        return (16 * px + (i + 56)) & 63

    def face_x(i):
        open_x = jnp.where(x_at(i) == 0, 0.0, 1.0).astype(F32)
        cxw[i] = open_x * harmonic(bw[i + 1], bw[i])

    loop(0, 33, 1, face_x)

    def coefficients(i):
        b = bw[i + 1]
        e_at = jnp.clip(i - 8, 0, 15)
        below = ylo_ref[pl.ds(e_at, 1), :]
        above = yhi_ref[pl.ds(e_at, 1), :]
        below = jnp.concatenate([below, below], axis=1)
        above = jnp.concatenate([above, above], axis=1)
        before = jnp.where(row == 24, jnp.broadcast_to(below, (32, 256)), roll(b, 1, 0))
        cy = y_open * harmonic(b, before)
        outer = harmonic(b[16:24], jnp.broadcast_to(above, (8, 256))) * y_open_next
        after = roll(cy, -1, 0)
        after = jnp.concatenate(
            [after[0:16], jnp.where(row[16:24] == 23, outer, after[16:24]), after[24:32]], axis=0
        )
        cz = z_open * harmonic(b, roll(b, 1, 1))
        own = harmonic(b, b)
        x_edge = jnp.where((x_at(i) == 0) | (x_at(i) == 63), 1.0, 0.0).astype(F32)
        e = own * (y_edge + z_edge + x_edge)
        d = cxw[i] + cxw[i + 1] + (cy + after) + (cz + roll(cz, -1, 1)) + e
        inv = 1.0 / d
        cx_ref[i] = cxw[i]
        cy_ref[i] = cy
        cz_ref[i] = cz
        inv_ref[i] = inv
        ew[i] = e
        dw[i] = d
        g = va[i] * inv
        rhs_ref[i] = g
        first = FIRST * g
        upd[i] = first
        va[i] = first

    y_next = (16 * py + 24) & 127
    y_open_next = jnp.where(y_next == 0, 0.0, 1.0).astype(F32)
    loop(0, 32, 2, coefficients)
    for m in saves[:5]:
        m.start()
    level = Level(cx_ref, cy_ref, cz_ref, inv_ref, rhs_ref, 0)
    sweep(level, va, vb, upd, 1, 31, 2, *TERMS[0])
    sweep(level, vb, va, upd, 2, 30, 2, *TERMS[1])
    sweep(level, va, u_ref, upd, 3, 29, 2, *TERMS[2], store_update=False)
    saves[5].start()

    def save_diag(i):
        diag_ref[i] = dw[i + 8, 0:16, 0:128]

    loop(0, 16, 4, save_diag)

    def put(a, p, value):
        scr[a, 0, p * 32 : p * 32 + 32, :] = value[:, 0:128]
        scr[a, 1, p * 32 : p * 32 + 32, :] = value[:, 128:256]

    for p in range(8):
        i = 8 + 2 * p
        total = None
        for k in (i, i + 1):
            _, d = level.defect(u_ref, k)
            r = dw[k] * d
            total = r if total is None else total + r
        put(0, p, 0.125 * total)
        put(1, p, 0.25 * cx_ref[i])
        put(2, p, 0.25 * (cy_ref[i] + cy_ref[i + 1]))
        put(3, p, 0.25 * (cz_ref[i] + cz_ref[i + 1]))
        put(4, p, 0.25 * (ew[i] + ew[i + 1]))
    fine_lane = iota((256, 128), 0)
    coarse_lane = iota((256, 128), 1)
    both = jnp.where((fine_lane >> 1) == coarse_lane, 1.0, 0.0)
    even = jnp.where(fine_lane == 2 * coarse_lane, 1.0, 0.0)
    half = iota((8, 128), 1) < 64
    for a in range(5):
        def rows_of(offset):
            return jnp.concatenate(
                [scr[a, t, pl.ds(offset, 128, stride=2), :] for t in range(2)], axis=1
            )

        folded = rows_of(0)
        if a != 2:
            folded = folded + rows_of(1)
        res = exact_dot(folded, even if a == 3 else both)
        for j in range(4):
            for t in range(2):
                lo = res[j * 16 + t * 8 : j * 16 + t * 8 + 8]
                hi = res[(j + 4) * 16 + t * 8 : (j + 4) * 16 + t * 8 + 8]
                xp_ref[a, j, t * 8 : t * 8 + 8, :] = jnp.where(half, lo, roll(hi, 64, 1))
    for m in saves:
        m.wait()


def packy1(x0, x1, x2, x3, up_ref, down_ref):
    low = iota((8, 128), 0) < 4
    xs = (x0, x1, x2, x3)
    for a in range(5):
        for q in range(16):
            own = xs[q // 4][a, q % 4, 0:8, :]
            up_ref[a, q] = own
            down_ref[a, q] = own
        for q in range(8):
            one = xs[q // 4][a, q % 4, 8:16, :]
            two = xs[2 + q // 4][a, q % 4, 8:16, :]
            up_ref[a, 16 + q] = jnp.where(low, roll(one, 4, 0), two)
            down_ref[a, 16 + q] = jnp.where(low, one, roll(two, 4, 0))


def pack1(x0, x1, x2, x3, lo_ref, hi_ref, up_ref, down_ref, w_ref):
    low = iota((8, 128), 0) < 4
    xs = (x0, x1, x2, x3)
    for a in range(5):
        for q in range(16):
            right, left = hi_ref[a, 16 + q % 8], lo_ref[a, 16 + q % 8]
            if q < 8:
                edge = jnp.where(low, right, roll(left, 4, 0))
            else:
                edge = jnp.where(low, roll(right, 4, 0), left)
            w_ref[a, q, 0:8, :] = xs[q // 4][a, q % 4, 0:8, :]
            w_ref[a, q, 8:16, :] = hi_ref[a, q]
            w_ref[a, q, 16:24, :] = edge
            w_ref[a, q, 24:32, :] = lo_ref[a, q]

        def get(p):
            k, j = p // 8, p % 8
            return w_ref[a, 4 * k + j % 4], 64 * (j // 4)

        ups, downs = z_pack(get, 32, 32, (53, 0), 11, 11)
        for g in range(3):
            up_ref[a, g] = ups[g]
            down_ref[a, g] = downs[g]


def pair_matrices(cut, size_in=128):
    fine = iota((size_in, 128), 0)
    coarse = iota((size_in, 128), 1)
    at = signed(fine, size_in, cut)
    both = jnp.where(((at >> 1) & 127) == coarse, 1.0, 0.0)
    even = jnp.where((((at >> 1) & 127) == coarse) & ((at & 1) == 0), 1.0, 0.0)
    return both, even


def restrict(scr, both, even, count):
    out = []
    for a in range(5):
        folded = scr[a, pl.ds(0, count, stride=2), :]
        if a != 2:
            folded = folded + scr[a, pl.ds(1, count, stride=2), :]
        out.append(exact_dot(folded, even if a == 3 else both))
    return out


def mid_down(
    w_ref, zlo_ref, zhi_ref,
    u_far, cx_far, cy_far, cz_far, inv_far, rhs_far, own_ref, ym_ref, yp_ref,
    u_ref, cx_ref, cy_ref, cz_ref, inv_ref, rhs_ref,
    va, vb, upd, ew, dw, scr, *sems,
):
    saves = copies_of(
        (cx_ref, cy_ref, cz_ref, inv_ref, rhs_ref, u_ref),
        (cx_far, cy_far, cz_far, inv_far, rhs_far, u_far),
        sems,
    )
    lane = iota((32, 128), 1)
    targets = (va, cx_ref, cy_ref, cz_ref, ew)
    for a in range(5):
        fill = 1.0 if a == 4 else 0.0
        for p in range(32):
            k, j = p // 8, p % 8
            base = w_ref[a, 4 * k + j % 4]
            if j >= 4:
                base = roll(base, 64, 1)
            g, at = p // 11, (p % 11) * 11
            right = roll(zhi_ref[a, g], 64 - at, 1)
            left = roll(zlo_ref[a, g], 117 - at, 1)
            halo = jnp.where(lane < 75, right, jnp.where(lane >= 117, left, fill))
            targets[a][p] = jnp.where(lane < 64, base, halo)

    def coefficients(i):
        above = (i + 1) & 31
        cy, cz = cy_ref[i], cz_ref[i]
        d = cx_ref[i] + cx_ref[above] + (cy + roll(cy, -1, 0)) + (cz + roll(cz, -1, 1)) + ew[i]
        inv = 1.0 / d
        inv_ref[i] = inv
        dw[i] = d
        g = 4.0 * va[i] * inv
        rhs_ref[i] = g
        first = FIRST * g
        upd[i] = first
        va[i] = first

    loop(0, 32, 4, coefficients)
    for m in saves[:5]:
        m.start()
    level = Level(cx_ref, cy_ref, cz_ref, inv_ref, rhs_ref, 32)
    sweep(level, va, vb, upd, 0, 32, 4, *TERMS[0])
    sweep(level, vb, va, upd, 0, 32, 4, *TERMS[1])
    sweep(level, va, u_ref, upd, 0, 32, 4, *TERMS[2], store_update=False)
    saves[5].start()
    for p in range(16):
        i = 2 * p
        _, d0 = level.defect(u_ref, i)
        _, d1 = level.defect(u_ref, i + 1)
        at = slice(32 * p, 32 * p + 32)
        scr[0, at, :] = 0.03125 * (dw[i] * d0 + dw[i + 1] * d1)
        scr[1, at, :] = 0.25 * cx_ref[i]
        scr[2, at, :] = 0.25 * (cy_ref[i] + cy_ref[i + 1])
        scr[3, at, :] = 0.25 * (cz_ref[i] + cz_ref[i + 1])
        scr[4, at, :] = 0.25 * (ew[i] + ew[i + 1])
    both, even = pair_matrices(96)
    f, cx, cy, cz, e = [r.reshape(16, 16, 128) for r in restrict(scr, both, even, 256)]
    cx_next = jnp.concatenate([cx[1:], cx[:1]], axis=0)
    planes = []
    for p in range(16):
        d = cx[p] + cx_next[p] + (cy[p] + roll(cy[p], -1, 0)) + (cz[p] + roll(cz[p], -1, 1)) + e[p]
        planes.append((f[p], cx[p], cy[p], cz[p], d))
    lane8 = iota((16, 128), 1)
    row8 = iota((8, 128), 0)
    for a in range(5):
        for j in range(4):
            packed = planes[j][a]
            for k in range(1, 4):
                packed = jnp.where(lane8 >= 32 * k, roll(planes[4 * k + j][a], 32 * k, 1), packed)
            own_ref[a, j] = packed
            ym_ref[a, j] = jnp.where(row8 == 7, packed[8:16], packed[0:8])
            yp_ref[a, j] = jnp.where(row8 < 5, packed[0:8], packed[8:16])
    for m in saves:
        m.wait()


def pack2(own_ref, hi_ref, far_ref, lo_ref, up_ref, down_ref, w_ref):
    row = iota((8, 128), 0)
    for a in range(5):
        for j in range(4):
            hi, far, lo = hi_ref[a, j], far_ref[a, j], lo_ref[a, j]
            w_ref[a, j, 0:8, :] = jnp.where(row == 7, hi, own_ref[a, j, 0:8, :])
            w_ref[a, j, 8:16, :] = jnp.where(row == 7, far, hi)
            w_ref[a, j, 16:24, :] = jnp.where(row < 5, far, lo)
            w_ref[a, j, 24:32, :] = jnp.where(row < 5, lo, own_ref[a, j, 8:16, :])

        def get(p):
            return w_ref[a, p % 4], 32 * (p // 4)

        ups, downs = z_pack(get, 16, 32, (21, 0), 11, 11)
        for g in range(2):
            up_ref[a, g] = ups[g]
            down_ref[a, g] = downs[g]


def low_down(
    w_ref, zlo_ref, zhi_ref,
    u_far, cx_far, cy_far, cz_far, inv_far, rhs_far, own_ref,
    u_ref, cx_ref, cy_ref, cz_ref, inv_ref, rhs_ref,
    va, vb, upd, dw, scr, *sems,
):
    saves = copies_of(
        (cx_ref, cy_ref, cz_ref, inv_ref, rhs_ref, u_ref),
        (cx_far, cy_far, cz_far, inv_far, rhs_far, u_far),
        sems,
    )
    lane = iota((32, 128), 1)
    targets = (va, cx_ref, cy_ref, cz_ref, dw)
    for a in range(5):
        fill = 1.0 if a == 4 else 0.0
        for p in range(16):
            base = roll(w_ref[a, p % 4], -32 * (p // 4), 1)
            g, at = p // 11, (p % 11) * 11
            right = roll(zhi_ref[a, g], 32 - at, 1)
            left = roll(zlo_ref[a, g], 117 - at, 1)
            halo = jnp.where(lane < 43, right, jnp.where(lane >= 117, left, fill))
            targets[a][p] = jnp.where(lane < 32, base, halo)

    def coefficients(i):
        inv = 1.0 / dw[i]
        inv_ref[i] = inv
        g = 16.0 * va[i] * inv
        rhs_ref[i] = g
        first = FIRST * g
        upd[i] = first
        va[i] = first

    loop(0, 16, 4, coefficients)
    for m in saves[:5]:
        m.start()
    level = Level(cx_ref, cy_ref, cz_ref, inv_ref, rhs_ref, 16)
    sweep(level, va, vb, upd, 0, 16, 4, *TERMS[0])
    sweep(level, vb, va, upd, 0, 16, 4, *TERMS[1])
    sweep(level, va, u_ref, upd, 0, 16, 4, *TERMS[2], store_update=False)
    saves[5].start()

    def edge(i):
        above = (i + 1) & 15
        cy, cz = cy_ref[i], cz_ref[i]
        inner = cx_ref[i] + cx_ref[above] + (cy + roll(cy, -1, 0)) + (cz + roll(cz, -1, 1))
        return dw[i] - inner

    for p in range(8):
        i = 2 * p
        _, d0 = level.defect(u_ref, i)
        _, d1 = level.defect(u_ref, i + 1)
        at = slice(32 * p, 32 * p + 32)
        scr[0, at, :] = 0.0078125 * (dw[i] * d0 + dw[i + 1] * d1)
        scr[1, at, :] = 0.25 * cx_ref[i]
        scr[2, at, :] = 0.25 * (cy_ref[i] + cy_ref[i + 1])
        scr[3, at, :] = 0.25 * (cz_ref[i] + cz_ref[i + 1])
        scr[4, at, :] = 0.25 * (edge(i) + edge(i + 1))
    both, even = pair_matrices(96)
    f, cx, cy, cz, e = [r.reshape(8, 16, 128) for r in restrict(scr, both, even, 128)]
    planes = []
    for p in range(8):
        inner = cx[p] + cx[(p + 1) % 8] + (cy[p] + roll(cy[p], -1, 0))
        d = inner + (cz[p] + roll(cz[p], -1, 1)) + e[p]
        planes.append((f[p], cx[p], cy[p], cz[p], d))
    lane16 = iota((16, 128), 1)
    for a in range(5):
        packed = planes[0][a]
        for p in range(1, 8):
            packed = jnp.where(lane16 >= 16 * p, roll(planes[p][a], 16 * p, 1), packed)
        own_ref[a] = packed
    for m in saves:
        m.wait()


def spread(dup, w, rows, matrix):
    count = w.shape[0]
    dup[pl.ds(0, count, stride=2), :] = w
    dup[pl.ds(1, count, stride=2), :] = w
    return exact_dot(dup[0 : 2 * count, :], matrix)


def spread_matrix(cut, size):
    coarse = iota((128, size), 0)
    at = signed(iota((128, size), 1), size, cut)
    return jnp.where(((at >> 1) & 127) == coarse, 1.0, 0.0)


def post(level, va, vb, upd, ranges, unroll):
    lo, hi = ranges[0]
    sweep(level, va, vb, upd, lo, hi, unroll, None, FIRST)
    src, dst = vb, va
    for n in range(3):
        lo, hi = ranges[n + 1]
        sweep(level, src, dst, upd, lo, hi, unroll, *TERMS[n], store_update=n < 2)
        src, dst = dst, src


def up(
    g_ref, *refs,
):
    fars, refs = refs[:19], refs[19:]
    (sol_ref, res_ref), refs = refs[:2], refs[2:]
    (l3, inv3, rhs3, u3, va3, vb3, upd3, scr3), refs = refs[:8], refs[8:]
    (va2, vb2, upd2, dup2, va1, vb1, upd1, dup1, va0, vb0, upd0, dup0), refs = refs[:12], refs[12:]
    nears, sems = refs[:19], refs[19:]
    u2, cx2, cy2, cz2, inv2, rhs2 = nears[:6]
    u1, cx1, cy1, cz1, inv1, rhs1 = nears[6:12]
    u0, cx0, cy0, cz0, inv0, rhs0, diag0 = nears[12:]
    loads = copies_of(fars, nears, sems)
    for m in loads:
        m.start()
    me = lax.axis_index("gz")
    lane = iota((16, 128), 1)
    for a in range(5):
        tiles = [g_ref[(me + k) & 7, a] for k in range(8)]
        for p in range(8):
            plane = roll(tiles[0], -16 * p, 1)
            for k in range(1, 8):
                plane = jnp.where(lane >= 16 * k, roll(tiles[k], 16 * (k - p), 1), plane)
            l3[a, p] = plane
    f3, cx3, cy3, cz3, d3 = [l3.at[a] for a in range(5)]
    level = Level(cx3, cy3, cz3, inv3, rhs3, 8)

    def start3(i):
        inv = 1.0 / d3[i]
        inv3[i] = inv
        g = 64.0 * f3[i] * inv
        rhs3[i] = g
        first = FIRST * g
        upd3[i] = first
        va3[i] = first

    loop(0, 8, 8, start3)
    sweep(level, va3, vb3, upd3, 0, 8, 8, *TERMS[0])
    sweep(level, vb3, va3, upd3, 0, 8, 8, *TERMS[1])
    sweep(level, va3, u3, upd3, 0, 8, 8, *TERMS[2], store_update=False)
    for p in range(4):
        i = 2 * p
        _, r0 = level.defect(u3, i)
        _, r1 = level.defect(u3, i + 1)
        at = slice(16 * p, 16 * p + 16)
        scr3[0, at, :] = (0.125 / 64.0) * (d3[i] * r0 + d3[i + 1] * r1)
        scr3[1, at, :] = 0.25 * cx3[i]
        scr3[2, at, :] = 0.25 * (cy3[i] + cy3[i + 1])
        scr3[3, at, :] = 0.25 * (cz3[i] + cz3[i + 1])
        total = None
        for k in (i, i + 1):
            cy, cz = cy3[k], cz3[k]
            inner = cx3[k] + cx3[(k + 1) % 8] + (cy + roll(cy, -1, 0))
            inner = inner + (cz + roll(cz, -1, 1))
            total = d3[k] - inner if total is None else total + (d3[k] - inner)
        scr3[4, at, :] = 0.25 * total
    fine = iota((128, 128), 0)
    coarse = iota((128, 128), 1) & 63
    both = jnp.where((fine >> 1) == coarse, 1.0, 0.0)
    even = jnp.where(fine == 2 * coarse, 1.0, 0.0)
    f, cx, cy, cz, e = restrict(scr3, both, even, 32)

    def cut(a, p):
        return a[8 * p : 8 * p + 8]

    fs, cxs, cys, czs = [[cut(a, p) for p in range(4)] for a in (f, cx, cy, cz)]
    invs, gs, vs, es = [], [], [], []
    for p in range(4):
        d = cxs[p] + cxs[(p + 1) % 4] + (cys[p] + roll(cys[p], -1, 0))
        d = d + (czs[p] + roll(czs[p], -1, 1)) + cut(e, p)
        invs.append(1.0 / d)
        gs.append(256.0 * fs[p] * invs[p])
        es.append(CFIRST * gs[p])
        vs.append(es[p])
    xlo = [invs[p] * cxs[p] for p in range(4)]
    xhi = [invs[p] * cxs[(p + 1) % 4] for p in range(4)]
    ylo = [invs[p] * cys[p] for p in range(4)]
    yhi = [invs[p] * roll(cys[p], -1, 0) for p in range(4)]
    zlo = [invs[p] * czs[p] for p in range(4)]
    zhi = [invs[p] * roll(czs[p], -1, 1) for p in range(4)]
    for momentum, push in CTERMS:
        momentum, push = float(np.float32(momentum)), float(np.float32(push))
        new_v, new_e = [], []
        for p in range(4):
            v = vs[p]
            total = xlo[p] * vs[(p + 3) % 4] + xhi[p] * vs[(p + 1) % 4]
            total = total + (ylo[p] * roll(v, 1, 0) + yhi[p] * roll(v, -1, 0))
            total = total + (zlo[p] * roll(v, 1, 1) + zhi[p] * roll(v, -1, 1))
            ne = momentum * es[p] + push * ((gs[p] - v) + total)
            new_e.append(ne)
            new_v.append(v + ne)
        vs, es = new_v, new_e
    w4 = jnp.concatenate(vs, axis=0)
    fine = iota((128, 128), 1)
    coarse = iota((128, 128), 0)
    m = jnp.where((fine >> 1) == coarse, 1.0, 0.0)
    wide = spread(dup2, w4, 8, m)
    for i in range(8):
        p = i // 2
        va3[i] = u3[i] + wide[16 * p : 16 * p + 16]
    post(level, va3, vb3, upd3, [(0, 8)] * 4, 8)
    for m in loads[:6]:
        m.wait()
    w3 = va3[...].reshape(128, 128)
    wide = spread(dup2, w3, 16, spread_matrix(96, 128))
    for i in range(16):
        p = i // 2
        va2[i] = u2[i] + wide[32 * p : 32 * p + 32]
    level = Level(cx2, cy2, cz2, inv2, rhs2, 16)
    post(level, va2, vb2, upd2, [(0, 16)] * 4, 4)
    for m in loads[6:12]:
        m.wait()
    w2 = jnp.concatenate([va2[:, 0:8, :], va2[:, 24:32, :]], axis=1).reshape(256, 128)
    wide = spread(dup1, w2, 16, spread_matrix(96, 128))
    for i in range(32):
        p = i // 2
        va1[i] = u1[i] + wide[32 * p : 32 * p + 32]
    level = Level(cx1, cy1, cz1, inv1, rhs1, 32)
    post(level, va1, vb1, upd1, [(0, 32)] * 4, 4)
    for m in loads[12:]:
        m.wait()
    rows = [
        jnp.concatenate([va1[i % 32, 0:8, :], mix_rows(va1, i % 32)], axis=0) for i in range(-4, 12)
    ]
    w1 = jnp.concatenate(rows, axis=0)
    wide = spread(dup0, w1, 16, spread_matrix(192, 256))
    for i in range(3, 29):
        p = i // 2
        va0[i] = u0[i] + wide[32 * p : 32 * p + 32]
    level = Level(cx0, cy0, cz0, inv0, rhs0, 0)
    post(level, va0, vb0, upd0, [(4, 28), (5, 27), (6, 26), (7, 25)], 2)

    def finish(i):
        here, d = level.defect(va0, i)
        sol_ref[i - 8] = here[0:16, 0:128]
        res_ref[i - 8] = diag0[i - 8] * d[0:16, 0:128]

    loop(8, 24, 2, finish)


def mix_rows(ref, i):
    low = iota((8, 128), 0) < 4
    return jnp.where(low, ref[i, 8:16, :], ref[i, 24:32, :])


def call(body, args, outs, scratch=(), limit=16, far_in=(), far_out=(), copies=0):
    near, far = pl.BlockSpec(memory_space=pltpu.VMEM), pl.BlockSpec(memory_space=pltpu.HBM)
    return pl.pallas_call(
        body,
        out_shape=[jax.ShapeDtypeStruct(s, F32) for s in outs],
        in_specs=[far if i in far_in else near for i in range(len(args))],
        out_specs=[far if i in far_out else near for i in range(len(outs))],
        scratch_shapes=[pltpu.VMEM(s, F32) for s in scratch]
        + [pltpu.SemaphoreType.DMA] * copies,
        compiler_params=pltpu.CompilerParams(vmem_limit_bytes=limit * MIB),
        name=body.__name__,
    )(*args)


def move(values, axis, shift):
    size = lax.axis_size(axis)
    return lax.ppermute(values, axis, [((i + shift) % size, i) for i in range(size)])


def local(source, conductivity):
    f, b = source, conductivity
    to_hi, to_lo = call(
        packx0, (f, b), [(17, 16, 128)] * 2, far_in=(0, 1), copies=4
    )
    from_lo, from_hi = move(to_hi, "gx", -1), move(to_lo, "gx", 1)
    fx = jnp.concatenate([from_lo[:8], f, from_hi[:8]])
    bx = jnp.concatenate([from_lo[8:], b, from_hi[8:]])

    def y_slab(at, edge):
        return jnp.concatenate(
            [fx[:, at : at + 8], bx[1:33, at : at + 8], bx[9:25, edge].reshape(2, 8, 128)]
        )

    from_lo = move(y_slab(8, 7), "gy", -1)
    from_hi = move(y_slab(0, 8), "gy", 1)
    fw = jnp.concatenate([fx, from_hi[:32], from_lo[:32]], axis=1)
    inner = jnp.concatenate([bx[1:33], from_hi[32:64], from_lo[32:64]], axis=1)
    first = jnp.concatenate([bx[:1], bx[:1]], axis=1)
    last = jnp.concatenate([bx[33:], bx[33:]], axis=1)
    bw = jnp.concatenate([first, inner, last])
    ylo, yhi = from_lo[64:].reshape(16, 128), from_hi[64:].reshape(16, 128)
    up0, down0 = call(pack0, (fw, bw), [(5, 32, 128)] * 2)
    zlo, zhi = move(up0, "gz", -1), move(down0, "gz", 1)
    big = (32, 32, 256)
    u0, cx0, cy0, cz0, inv0, rhs0, diag0, xp = call(
        fine_down,
        (fw, bw, ylo, yhi, zlo, zhi),
        [big] * 6 + [(16, 16, 128), (5, 4, 16, 128)],
        [big] * 6 + [(34, 32, 256), big, big, big, big, (33, 32, 256), big, (5, 2, 256, 128)],
        28,
        far_out=range(6),
        copies=6,
    )
    xs = [xp] + [move(xp, "gx", k) for k in (1, 2, 3)]
    to_hi, to_lo = call(packy1, xs, [(5, 24, 8, 128)] * 2)
    from_lo, from_hi = move(to_hi, "gy", -1), move(to_lo, "gy", 1)
    up1, down1, w1 = call(
        pack1, xs + [from_lo, from_hi], [(5, 3, 32, 128)] * 2 + [(5, 16, 32, 128)]
    )
    zlo, zhi = move(up1, "gz", -1), move(down1, "gz", 1)
    mid = (32, 32, 128)
    u1, cx1, cy1, cz1, inv1, rhs1, own2, ym, yp = call(
        mid_down,
        (w1, zlo, zhi),
        [mid] * 6 + [(5, 4, 16, 128), (5, 4, 8, 128), (5, 4, 8, 128)],
        [mid] * 11 + [(5, 512, 128)],
        far_out=range(6),
        copies=6,
    )
    from_hi, from_lo, far = move(ym, "gy", 2), move(yp, "gy", -2), move(ym, "gy", 4)
    up2, down2, w2 = call(
        pack2, (own2, from_hi, far, from_lo), [(5, 2, 32, 128)] * 2 + [(5, 4, 32, 128)]
    )
    zlo, zhi = move(up2, "gz", -1), move(down2, "gz", 1)
    low = (16, 32, 128)
    u2, cx2, cy2, cz2, inv2, rhs2, own3 = call(
        low_down,
        (w2, zlo, zhi),
        [low] * 6 + [(5, 16, 128)],
        [low] * 10 + [(5, 256, 128)],
        far_out=range(6),
        copies=6,
    )
    everyone = jnp.broadcast_to(own3[None], (8, 5, 16, 128))
    gathered = lax.all_to_all(everyone, "gz", 0, 0)
    tiny = (8, 16, 128)
    return tuple(
        call(
            up,
            (
                gathered,
                u2, cx2, cy2, cz2, inv2, rhs2,
                u1, cx1, cy1, cz1, inv1, rhs1,
                u0, cx0, cy0, cz0, inv0, rhs0, diag0,
            ),
            [(16, 16, 128)] * 2,
            [(5,) + tiny] + [tiny] * 6 + [(5, 64, 128)]
            + [low] * 3 + [(256, 128)] + [mid] * 3 + [(512, 128)] + [big] * 3 + [(512, 128)]
            + [low] * 6 + [mid] * 6 + [big] * 6 + [(16, 16, 128)],
            28,
            far_in=range(1, 20),
            copies=19,
        )
    )


def solution(mesh):
    spec = P("gx", "gy", "gz")
    return jax.shard_map(
        local, mesh=mesh, in_specs=(spec, spec), out_specs=(spec, spec), check_vma=False
    )
```

```python
import functools

import jax
import jax.numpy as jnp
import numpy as np
from jax import lax
from jax.experimental import pallas as pl
from jax.experimental.pallas import tpu as pltpu
from jax.sharding import PartitionSpec as P

F32 = jnp.float32
CSWEEPS = 32
MIB = 1024 * 1024
NEAR, FULL = 8, 16


def chebyshev_terms(sweep_count, lower_bound, upper_bound):
    center = (upper_bound + lower_bound) / 2.0
    half_width = (upper_bound - lower_bound) / 2.0
    sigma_ratio = center / half_width
    rho_now = 1.0 / sigma_ratio
    terms = []
    for _ in range(sweep_count - 1):
        rho_next = 1.0 / (2.0 * sigma_ratio - rho_now)
        terms.append((rho_next * rho_now, 2.0 * rho_next / half_width))
        rho_now = rho_next
    return 1.0 / center, terms


FIRST, TERMS = chebyshev_terms(4, 0.6, 2.0)
CFIRST, CTERMS = chebyshev_terms(CSWEEPS, 0.05, 2.0)


def harmonic(a, b):
    return 2.0 * a * b / (a + b)


def roll(a, shift, axis):
    return pltpu.roll(a, shift % a.shape[axis], axis)


def iota(shape, dim):
    return lax.broadcasted_iota(jnp.int32, shape, dim)


def exact_dot(a, m):
    m = m.astype(jnp.bfloat16)
    high = a.astype(jnp.bfloat16)
    rest = a - high.astype(F32)
    mid = rest.astype(jnp.bfloat16)
    low = (rest - mid.astype(F32)).astype(jnp.bfloat16)
    parts = [jnp.dot(p, m, preferred_element_type=F32) for p in (high, mid, low)]
    return parts[0] + (parts[1] + parts[2])


def signed(index, size, cut):
    return jnp.where(index < cut, index, index - size)


def loop(lo, hi, unroll, body):
    rounds = (hi - lo) // unroll

    def step(t, carry):
        for u in range(unroll):
            body(lo + t * unroll + u)
        return carry

    if rounds:
        lax.fori_loop(0, rounds, step, 0)
    for i in range(lo + rounds * unroll, hi):
        body(i)


def copies_of(sources, targets, sems):
    return [pltpu.make_async_copy(a, b, s) for a, b, s in zip(sources, targets, sems)]


class Level:
    def __init__(self, cx, cy, cz, inv, rhs, wrap):
        self.cx, self.cy, self.cz, self.inv, self.rhs, self.wrap = cx, cy, cz, inv, rhs, wrap

    def around(self, i):
        if self.wrap:
            return (i + self.wrap - 1) & (self.wrap - 1), (i + 1) & (self.wrap - 1)
        return i - 1, i + 1

    def defect(self, v, i):
        below, above = self.around(i)
        here = v[i]
        cy, cz = self.cy[i], self.cz[i]
        total = self.cx[i] * v[below] + self.cx[above] * v[above]
        total = total + (cy * roll(here, 1, 0) + roll(cy * here, -1, 0))
        total = total + (cz * roll(here, 1, 1) + roll(cz * here, -1, 1))
        return here, self.rhs[i] - here + self.inv[i] * total


def sweep(level, src, dst, upd, lo, hi, unroll, momentum, push, store_update=True):
    def body(i):
        here, d = level.defect(src, i)
        e = push * d
        if momentum is not None:
            e = momentum * upd[i] + e
        if store_update:
            upd[i] = e
        dst[i] = here + e

    loop(lo, hi, unroll, body)


def z_pack(get, planes, rows, starts, width, per):
    lane = iota((rows, 128), 1)
    out = []
    for start in starts:
        tiles = []
        for g in range(0, planes, per):
            acc = jnp.zeros((rows, 128), F32)
            for p in range(g, min(g + per, planes)):
                plane, base = get(p)
                at = (p - g) * width
                moved = roll(plane, at - start - base, 1)
                acc = jnp.where((lane >= at) & (lane < at + width), moved, acc)
            tiles.append(acc)
        out.append(tiles)
    return out


def x_plane(own_ref, lo_ref, hi_ref, first, width, p):
    if p < width:
        return lo_ref, first + p
    if p < width + 16:
        return own_ref, p - width
    return hi_ref, first + p - width - 16


def f_plane(f_ref, lo_ref, hi_ref, p):
    return x_plane(f_ref, lo_ref, hi_ref, 0, 8, p)


def b_plane(b_ref, lo_ref, hi_ref, p):
    return x_plane(b_ref, lo_ref, hi_ref, 8, 9, p)


def packy0(f_ref, b_ref, lo_ref, hi_ref, up_ref, down_ref):
    for p in range(32):
        for at, (ref, q) in (
            (p, f_plane(f_ref, lo_ref, hi_ref, p)),
            (32 + p, b_plane(b_ref, lo_ref, hi_ref, p + 1)),
        ):
            up_ref[at] = ref[q, 8:16, :]
            down_ref[at] = ref[q, 0:8, :]
    row = iota((8, 128), 0)
    for ref, edge in ((up_ref, 7), (down_ref, 8)):
        for t in range(2):
            acc = jnp.zeros((8, 128), F32)
            for r in range(8):
                line = jnp.broadcast_to(b_ref[8 * t + r, edge : edge + 1, :], (8, 128))
                acc = jnp.where(row == r, line, acc)
            ref[64 + t] = acc


def pack0(
    f_ref, b_ref, xlo_ref, xhi_ref, ylo_ref, yhi_ref, up_ref, down_ref, fw_ref, bw_ref
):
    for p in range(32):
        ref, q = f_plane(f_ref, xlo_ref, xhi_ref, p)
        fw_ref[p, 0:16, :] = ref[q]
        fw_ref[p, 16:24, :] = yhi_ref[p]
        fw_ref[p, 24:32, :] = ylo_ref[p]
    for p in range(34):
        ref, q = b_plane(b_ref, xlo_ref, xhi_ref, p)
        bw_ref[p, 0:16, :] = ref[q]
        if 0 < p < 33:
            bw_ref[p, 16:24, :] = yhi_ref[31 + p]
            bw_ref[p, 24:32, :] = ylo_ref[31 + p]
        else:
            bw_ref[p, 16:32, :] = ref[q]
    ups, downs = z_pack(lambda p: (fw_ref[p], 0), 32, 32, (104, 0), 24, 5)
    more = z_pack(lambda p: (bw_ref[p + 1], 0), 32, 32, (103, 0), 25, 5)
    for g in range(7):
        up_ref[g] = ups[g]
        down_ref[g] = downs[g]
        up_ref[7 + g] = more[0][g]
        down_ref[7 + g] = more[1][g]


def fold_lanes(scr, count, slots, xp_ref):
    fine_lane = iota((256, 128), 0)
    coarse_lane = iota((256, 128), 1)
    both = jnp.where((fine_lane >> 1) == coarse_lane, 1.0, 0.0)
    even = jnp.where(fine_lane == 2 * coarse_lane, 1.0, 0.0)
    lane = iota((8, 128), 1)
    half = lane < 64
    for a, kind in enumerate(slots):
        def rows_of(offset):
            return jnp.concatenate(
                [scr[a, t, pl.ds(offset, 128, stride=2), :] for t in range(2)], axis=1
            )

        folded = rows_of(0)
        if kind != "y":
            folded = folded + rows_of(1)
        res = exact_dot(folded, even if kind == "z" else both)
        for j in range(4):
            for t in range(2):
                lo = res[j * 16 + t * 8 : j * 16 + t * 8 + 8]
                hi = res[(j + 4) * 16 + t * 8 : (j + 4) * 16 + t * 8 + 8]
                xp_ref[a, j, t * 8 : t * 8 + 8, :] = jnp.where(half, lo, roll(hi, 64, 1))
        for g in range(2):
            for t in range(2):
                acc = None
                for q in range(4):
                    at = (4 * g + q) * 16 + t * 8
                    plane = res[at : at + 8]
                    part = jnp.where(lane < 80, plane, roll(plane, -32, 1))
                    part = roll(part, 32 * q - 64, 1)
                    acc = part if acc is None else jnp.where(lane >= 32 * q, part, acc)
                xp_ref[a, 4 + g, t * 8 : t * 8 + 8, :] = acc


def put_lanes(scr, a, p, value):
    scr[a, 0, p * 32 : p * 32 + 32, :] = value[:, 0:128]
    scr[a, 1, p * 32 : p * 32 + 32, :] = value[:, 128:256]


def fine_coef(
    b_ref, ylo_ref, yhi_ref, zlo_ref, zhi_ref,
    cx_ref, cy_ref, cz_ref, inv_ref, dw, xp_ref,
    bw, ew, cxw, scr,
):
    px, py, pz = lax.axis_index("gx"), lax.axis_index("gy"), lax.axis_index("gz")
    lane1 = iota((32, 128), 1)
    lane = iota((32, 256), 1)
    row = iota((32, 256), 0)
    for i in range(34):
        q = min(max(i - 1, 0), 31)
        g, at = 7 + q // 5, (q % 5) * 25
        right = roll(zhi_ref[g], -at, 1)
        left = roll(zlo_ref[g], 103 - at, 1)
        bw[i, :, 0:128] = b_ref[i]
        bw[i, :, 128:256] = jnp.where(lane1 < 25, right, jnp.where(lane1 >= 103, left, 1.0))
    y_at = (16 * py + signed(row, 32, 24)) & 127
    z_at = (128 * pz + signed(lane, 256, 192)) & 1023
    y_open = jnp.where(y_at == 0, 0.0, 1.0)
    z_open = jnp.where(z_at == 0, 0.0, 1.0)
    y_edge = jnp.where((y_at == 0) | (y_at == 127), 1.0, 0.0)
    z_edge = jnp.where((z_at == 0) | (z_at == 1023), 1.0, 0.0)

    def x_at(i):
        return (16 * px + (i + 56)) & 63

    def face_x(i):
        open_x = jnp.where(x_at(i) == 0, 0.0, 1.0).astype(F32)
        cxw[i] = open_x * harmonic(bw[i + 1], bw[i])

    loop(0, 33, 3, face_x)

    def coefficients(i):
        b = bw[i + 1]
        e_at = jnp.clip(i - 8, 0, 15)
        below = ylo_ref[pl.ds(e_at, 1), :]
        above = yhi_ref[pl.ds(e_at, 1), :]
        below = jnp.concatenate([below, below], axis=1)
        above = jnp.concatenate([above, above], axis=1)
        before = jnp.where(row == 24, jnp.broadcast_to(below, (32, 256)), roll(b, 1, 0))
        cy = y_open * harmonic(b, before)
        outer = harmonic(b[16:24], jnp.broadcast_to(above, (8, 256))) * y_open_next
        after = roll(cy, -1, 0)
        after = jnp.concatenate(
            [after[0:16], jnp.where(row[16:24] == 23, outer, after[16:24]), after[24:32]], axis=0
        )
        cz = z_open * harmonic(b, roll(b, 1, 1))
        own = harmonic(b, b)
        x_edge = jnp.where((x_at(i) == 0) | (x_at(i) == 63), 1.0, 0.0).astype(F32)
        e = own * (y_edge + z_edge + x_edge)
        d = cxw[i] + cxw[i + 1] + (cy + after) + (cz + roll(cz, -1, 1)) + e
        inv = 1.0 / d
        cx_ref[i] = cxw[i]
        cy_ref[i] = cy
        cz_ref[i] = cz
        inv_ref[i] = inv
        ew[i] = e
        dw[i] = d

    y_next = (16 * py + 24) & 127
    y_open_next = jnp.where(y_next == 0, 0.0, 1.0).astype(F32)
    loop(0, 32, 4, coefficients)
    for p in range(8):
        i = 8 + 2 * p
        put_lanes(scr, 0, p, 0.25 * cx_ref[i])
        put_lanes(scr, 1, p, 0.25 * (cy_ref[i] + cy_ref[i + 1]))
        put_lanes(scr, 2, p, 0.25 * (cz_ref[i] + cz_ref[i + 1]))
        put_lanes(scr, 3, p, 0.25 * (ew[i] + ew[i + 1]))
    fold_lanes(scr, 4, ("x", "y", "z", "e"), xp_ref)


def fine_down(
    f_ref, zlo_ref, zhi_ref, cx_ref, cy_ref, cz_ref, inv_ref, dw,
    u_far, cx_far, cy_far, cz_far, inv_far, rhs_far, diag_ref, xp_ref,
    u_ref, rhs_ref, va, vb, upd, scr, *sems,
):
    saves = copies_of(
        (cx_ref, cy_ref, cz_ref, inv_ref, rhs_ref, u_ref),
        (cx_far, cy_far, cz_far, inv_far, rhs_far, u_far),
        sems,
    )
    for m in saves[:4]:
        m.start()
    lane1 = iota((32, 128), 1)
    for i in range(32):
        g, at = i // 5, (i % 5) * 24
        right = roll(zhi_ref[g], -at, 1)
        left = roll(zlo_ref[g], 104 - at, 1)
        halo = jnp.where(lane1 < 24, right, jnp.where(lane1 >= 104, left, 0.0))
        for t, part in enumerate((f_ref[i], halo)):
            at = slice(128 * t, 128 * t + 128)
            scaled = part * inv_ref[i, :, at]
            rhs_ref[i, :, at] = scaled
            scaled = FIRST * scaled
            upd[i, :, at] = scaled
            va[i, :, at] = scaled
    saves[4].start()
    level = Level(cx_ref, cy_ref, cz_ref, inv_ref, rhs_ref, 0)
    sweep(level, va, vb, upd, 1, 31, NEAR, *TERMS[0])
    sweep(level, vb, va, upd, 2, 30, NEAR, *TERMS[1])
    sweep(level, va, u_ref, upd, 3, 29, NEAR, *TERMS[2], store_update=False)
    saves[5].start()

    def save_diag(i):
        diag_ref[i] = dw[i + 8, 0:16, 0:128]

    loop(0, 16, 4, save_diag)
    for p in range(8):
        i = 8 + 2 * p
        total = None
        for k in (i, i + 1):
            _, d = level.defect(u_ref, k)
            r = dw[k] * d
            total = r if total is None else total + r
        put_lanes(scr, 0, p, 0.125 * total)
    fold_lanes(scr, 1, ("f",), xp_ref)
    for m in saves:
        m.wait()


TILES = 6


def packy1(x0, x1, x2, x3, up_ref, down_ref):
    low = iota((8, 128), 0) < 4
    xs = (x0, x1, x2, x3)
    half = 2 * TILES
    for a in range(x0.shape[0]):
        for q in range(2 * half):
            own = xs[q // TILES][a, q % TILES, 0:8, :]
            up_ref[a, q] = own
            down_ref[a, q] = own
        for q in range(half):
            one = xs[q // TILES][a, q % TILES, 8:16, :]
            two = xs[2 + q // TILES][a, q % TILES, 8:16, :]
            up_ref[a, 2 * half + q] = jnp.where(low, roll(one, 4, 0), two)
            down_ref[a, 2 * half + q] = jnp.where(low, one, roll(two, 4, 0))


def unpack1(xs, lo_ref, hi_ref, a, q):
    low = iota((8, 128), 0) < 4
    half = 2 * TILES
    right, left = hi_ref[a, 2 * half + q % half], lo_ref[a, 2 * half + q % half]
    if q < half:
        edge = jnp.where(low, right, roll(left, 4, 0))
    else:
        edge = jnp.where(low, roll(right, 4, 0), left)
    own = xs[q // TILES][a, q % TILES, 0:8, :]
    return jnp.concatenate([own, hi_ref[a, q], edge, lo_ref[a, q]], axis=0)


def pair_matrices(cut, size_in=128):
    fine = iota((size_in, 128), 0)
    coarse = iota((size_in, 128), 1)
    at = signed(fine, size_in, cut)
    both = jnp.where(((at >> 1) & 127) == coarse, 1.0, 0.0)
    even = jnp.where((((at >> 1) & 127) == coarse) & ((at & 1) == 0), 1.0, 0.0)
    return both, even


def restrict(scr, both, even, count):
    out = []
    for a in range(5):
        folded = scr[a, pl.ds(0, count, stride=2), :]
        if a != 2:
            folded = folded + scr[a, pl.ds(1, count, stride=2), :]
        out.append(exact_dot(folded, even if a == 3 else both))
    return out


def mid_down(
    c0, c1, c2, c3, clo_ref, chi_ref, f0, f1, f2, f3, flo_ref, fhi_ref,
    u_far, cx_far, cy_far, cz_far, inv_far, rhs_far, own_ref, ym_ref, yp_ref,
    u_ref, cx_ref, cy_ref, cz_ref, inv_ref, rhs_ref,
    va, vb, upd, ew, dw, scr, *sems,
):
    saves = copies_of(
        (cx_ref, cy_ref, cz_ref, inv_ref, rhs_ref, u_ref),
        (cx_far, cy_far, cz_far, inv_far, rhs_far, u_far),
        sems,
    )
    lane = iota((32, 128), 1)
    coarse = ((c0, c1, c2, c3), clo_ref, chi_ref)
    pieces = [(cx_ref, 0.0) + coarse + (0,), (cy_ref, 0.0) + coarse + (1,)]
    pieces += [(cz_ref, 0.0) + coarse + (2,), (ew, 1.0) + coarse + (3,)]
    pieces += [(va, 0.0, (f0, f1, f2, f3), flo_ref, fhi_ref, 0)]
    for target, fill, xs, lo_ref, hi_ref, a in pieces:
        for k in range(4):
            sides = [unpack1(xs, lo_ref, hi_ref, a, TILES * k + 4 + g) for g in range(2)]
            for j in range(4):
                base = unpack1(xs, lo_ref, hi_ref, a, TILES * k + j)
                for g in range(2):
                    own = roll(base, 64, 1) if g else base
                    right = roll(sides[g], 64 - 32 * j, 1)
                    left = roll(sides[g], 96 - 32 * j, 1)
                    halo = jnp.where(lane < 80, right, jnp.where(lane >= 112, left, fill))
                    target[8 * k + 4 * g + j] = jnp.where(lane < 64, own, halo)

    def coefficients(i):
        above = (i + 1) & 31
        cy, cz = cy_ref[i], cz_ref[i]
        d = cx_ref[i] + cx_ref[above] + (cy + roll(cy, -1, 0)) + (cz + roll(cz, -1, 1)) + ew[i]
        inv = 1.0 / d
        inv_ref[i] = inv
        dw[i] = d
        g = 4.0 * va[i] * inv
        rhs_ref[i] = g
        first = FIRST * g
        upd[i] = first
        va[i] = first

    loop(0, 32, 8, coefficients)
    for m in saves[:5]:
        m.start()
    level = Level(cx_ref, cy_ref, cz_ref, inv_ref, rhs_ref, 32)
    sweep(level, va, vb, upd, 0, 32, FULL, *TERMS[0])
    sweep(level, vb, va, upd, 0, 32, FULL, *TERMS[1])
    sweep(level, va, u_ref, upd, 0, 32, FULL, *TERMS[2], store_update=False)
    saves[5].start()
    for p in range(16):
        i = 2 * p
        _, d0 = level.defect(u_ref, i)
        _, d1 = level.defect(u_ref, i + 1)
        at = slice(32 * p, 32 * p + 32)
        scr[0, at, :] = 0.03125 * (dw[i] * d0 + dw[i + 1] * d1)
        scr[1, at, :] = 0.25 * cx_ref[i]
        scr[2, at, :] = 0.25 * (cy_ref[i] + cy_ref[i + 1])
        scr[3, at, :] = 0.25 * (cz_ref[i] + cz_ref[i + 1])
        scr[4, at, :] = 0.25 * (ew[i] + ew[i + 1])
    both, even = pair_matrices(96)
    f, cx, cy, cz, e = [r.reshape(16, 16, 128) for r in restrict(scr, both, even, 256)]
    cx_next = jnp.concatenate([cx[1:], cx[:1]], axis=0)
    planes = []
    for p in range(16):
        d = cx[p] + cx_next[p] + (cy[p] + roll(cy[p], -1, 0)) + (cz[p] + roll(cz[p], -1, 1)) + e[p]
        planes.append((f[p], cx[p], cy[p], cz[p], d))
    lane8 = iota((16, 128), 1)
    row8 = iota((8, 128), 0)
    for a in range(5):
        for j in range(4):
            packed = planes[j][a]
            for k in range(1, 4):
                packed = jnp.where(lane8 >= 32 * k, roll(planes[4 * k + j][a], 32 * k, 1), packed)
            own_ref[a, j] = packed
            ym_ref[a, j] = jnp.where(row8 == 7, packed[8:16], packed[0:8])
            yp_ref[a, j] = jnp.where(row8 < 5, packed[0:8], packed[8:16])
    for m in saves:
        m.wait()


def pack2(own_ref, hi_ref, far_ref, lo_ref, up_ref, down_ref, w_ref):
    row = iota((8, 128), 0)
    for a in range(5):
        for j in range(4):
            hi, far, lo = hi_ref[a, j], far_ref[a, j], lo_ref[a, j]
            w_ref[a, j, 0:8, :] = jnp.where(row == 7, hi, own_ref[a, j, 0:8, :])
            w_ref[a, j, 8:16, :] = jnp.where(row == 7, far, hi)
            w_ref[a, j, 16:24, :] = jnp.where(row < 5, far, lo)
            w_ref[a, j, 24:32, :] = jnp.where(row < 5, lo, own_ref[a, j, 8:16, :])

        def get(p):
            return w_ref[a, p % 4], 32 * (p // 4)

        ups, downs = z_pack(get, 16, 32, (21, 0), 11, 11)
        for g in range(2):
            up_ref[a, g] = ups[g]
            down_ref[a, g] = downs[g]


def low_down(
    w_ref, zlo_ref, zhi_ref,
    u_far, cx_far, cy_far, cz_far, inv_far, rhs_far, own_ref,
    u_ref, cx_ref, cy_ref, cz_ref, inv_ref, rhs_ref,
    va, vb, upd, dw, scr, *sems,
):
    saves = copies_of(
        (cx_ref, cy_ref, cz_ref, inv_ref, rhs_ref, u_ref),
        (cx_far, cy_far, cz_far, inv_far, rhs_far, u_far),
        sems,
    )
    lane = iota((32, 128), 1)
    targets = (va, cx_ref, cy_ref, cz_ref, dw)
    for a in range(5):
        fill = 1.0 if a == 4 else 0.0
        for p in range(16):
            base = roll(w_ref[a, p % 4], -32 * (p // 4), 1)
            g, at = p // 11, (p % 11) * 11
            right = roll(zhi_ref[a, g], 32 - at, 1)
            left = roll(zlo_ref[a, g], 117 - at, 1)
            halo = jnp.where(lane < 43, right, jnp.where(lane >= 117, left, fill))
            targets[a][p] = jnp.where(lane < 32, base, halo)

    def coefficients(i):
        inv = 1.0 / dw[i]
        inv_ref[i] = inv
        g = 16.0 * va[i] * inv
        rhs_ref[i] = g
        first = FIRST * g
        upd[i] = first
        va[i] = first

    loop(0, 16, 8, coefficients)
    for m in saves[:5]:
        m.start()
    level = Level(cx_ref, cy_ref, cz_ref, inv_ref, rhs_ref, 16)
    sweep(level, va, vb, upd, 0, 16, FULL, *TERMS[0])
    sweep(level, vb, va, upd, 0, 16, FULL, *TERMS[1])
    sweep(level, va, u_ref, upd, 0, 16, FULL, *TERMS[2], store_update=False)
    saves[5].start()

    def edge(i):
        above = (i + 1) & 15
        cy, cz = cy_ref[i], cz_ref[i]
        inner = cx_ref[i] + cx_ref[above] + (cy + roll(cy, -1, 0)) + (cz + roll(cz, -1, 1))
        return dw[i] - inner

    for p in range(8):
        i = 2 * p
        _, d0 = level.defect(u_ref, i)
        _, d1 = level.defect(u_ref, i + 1)
        at = slice(32 * p, 32 * p + 32)
        scr[0, at, :] = 0.0078125 * (dw[i] * d0 + dw[i + 1] * d1)
        scr[1, at, :] = 0.25 * cx_ref[i]
        scr[2, at, :] = 0.25 * (cy_ref[i] + cy_ref[i + 1])
        scr[3, at, :] = 0.25 * (cz_ref[i] + cz_ref[i + 1])
        scr[4, at, :] = 0.25 * (edge(i) + edge(i + 1))
    both, even = pair_matrices(96)
    f, cx, cy, cz, e = [r.reshape(8, 16, 128) for r in restrict(scr, both, even, 128)]
    planes = []
    for p in range(8):
        inner = cx[p] + cx[(p + 1) % 8] + (cy[p] + roll(cy[p], -1, 0))
        d = inner + (cz[p] + roll(cz[p], -1, 1)) + e[p]
        planes.append((f[p], cx[p], cy[p], cz[p], d))
    lane16 = iota((16, 128), 1)
    for a in range(5):
        packed = planes[0][a]
        for p in range(1, 8):
            packed = jnp.where(lane16 >= 16 * p, roll(planes[p][a], 16 * p, 1), packed)
        own_ref[a] = packed
    for m in saves:
        m.wait()


def spread(dup, w, rows, matrix):
    count = w.shape[0]
    dup[pl.ds(0, count, stride=2), :] = w
    dup[pl.ds(1, count, stride=2), :] = w
    return exact_dot(dup[0 : 2 * count, :], matrix)


def spread_matrix(cut, size):
    coarse = iota((128, size), 0)
    at = signed(iota((128, size), 1), size, cut)
    return jnp.where(((at >> 1) & 127) == coarse, 1.0, 0.0)


def post(level, va, vb, upd, ranges, unroll):
    lo, hi = ranges[0]
    sweep(level, va, vb, upd, lo, hi, unroll, None, FIRST)
    src, dst = vb, va
    for n in range(3):
        lo, hi = ranges[n + 1]
        sweep(level, src, dst, upd, lo, hi, unroll, *TERMS[n], store_update=n < 2)
        src, dst = dst, src


def up(
    g_ref, *refs,
):
    fars, refs = refs[:19], refs[19:]
    (sol_ref, res_ref), refs = refs[:2], refs[2:]
    (l3, inv3, rhs3, u3, va3, vb3, upd3, scr3), refs = refs[:8], refs[8:]
    (va2, vb2, upd2, dup2, va1, vb1, upd1, dup1, va0, vb0, upd0, dup0), refs = refs[:12], refs[12:]
    nears, sems = refs[:19], refs[19:]
    u2, cx2, cy2, cz2, inv2, rhs2 = nears[:6]
    u1, cx1, cy1, cz1, inv1, rhs1 = nears[6:12]
    u0, cx0, cy0, cz0, inv0, rhs0, diag0 = nears[12:]
    loads = copies_of(fars, nears, sems)
    for m in loads:
        m.start()
    me = lax.axis_index("gz")
    lane = iota((16, 128), 1)
    for a in range(5):
        tiles = [g_ref[(me + k) & 7, a] for k in range(8)]
        for p in range(8):
            plane = roll(tiles[0], -16 * p, 1)
            for k in range(1, 8):
                plane = jnp.where(lane >= 16 * k, roll(tiles[k], 16 * (k - p), 1), plane)
            l3[a, p] = plane
    f3, cx3, cy3, cz3, d3 = [l3.at[a] for a in range(5)]
    level = Level(cx3, cy3, cz3, inv3, rhs3, 8)

    def start3(i):
        inv = 1.0 / d3[i]
        inv3[i] = inv
        g = 64.0 * f3[i] * inv
        rhs3[i] = g
        first = FIRST * g
        upd3[i] = first
        va3[i] = first

    loop(0, 8, 8, start3)
    sweep(level, va3, vb3, upd3, 0, 8, 8, *TERMS[0])
    sweep(level, vb3, va3, upd3, 0, 8, 8, *TERMS[1])
    sweep(level, va3, u3, upd3, 0, 8, 8, *TERMS[2], store_update=False)
    for p in range(4):
        i = 2 * p
        _, r0 = level.defect(u3, i)
        _, r1 = level.defect(u3, i + 1)
        at = slice(16 * p, 16 * p + 16)
        scr3[0, at, :] = (0.125 / 64.0) * (d3[i] * r0 + d3[i + 1] * r1)
        scr3[1, at, :] = 0.25 * cx3[i]
        scr3[2, at, :] = 0.25 * (cy3[i] + cy3[i + 1])
        scr3[3, at, :] = 0.25 * (cz3[i] + cz3[i + 1])
        total = None
        for k in (i, i + 1):
            cy, cz = cy3[k], cz3[k]
            inner = cx3[k] + cx3[(k + 1) % 8] + (cy + roll(cy, -1, 0))
            inner = inner + (cz + roll(cz, -1, 1))
            total = d3[k] - inner if total is None else total + (d3[k] - inner)
        scr3[4, at, :] = 0.25 * total
    fine = iota((128, 128), 0)
    coarse = iota((128, 128), 1) & 63
    both = jnp.where((fine >> 1) == coarse, 1.0, 0.0)
    even = jnp.where(fine == 2 * coarse, 1.0, 0.0)
    f, cx, cy, cz, e = restrict(scr3, both, even, 32)

    def cut(a, p):
        return a[8 * p : 8 * p + 8]

    fs, cxs, cys, czs = [[cut(a, p) for p in range(4)] for a in (f, cx, cy, cz)]
    invs, gs, vs, es = [], [], [], []
    for p in range(4):
        d = cxs[p] + cxs[(p + 1) % 4] + (cys[p] + roll(cys[p], -1, 0))
        d = d + (czs[p] + roll(czs[p], -1, 1)) + cut(e, p)
        invs.append(1.0 / d)
        gs.append(256.0 * fs[p] * invs[p])
        es.append(CFIRST * gs[p])
        vs.append(es[p])
    xlo = [invs[p] * cxs[p] for p in range(4)]
    xhi = [invs[p] * cxs[(p + 1) % 4] for p in range(4)]
    ylo = [invs[p] * cys[p] for p in range(4)]
    yhi = [invs[p] * roll(cys[p], -1, 0) for p in range(4)]
    zlo = [invs[p] * czs[p] for p in range(4)]
    zhi = [invs[p] * roll(czs[p], -1, 1) for p in range(4)]
    for momentum, push in CTERMS:
        momentum, push = float(np.float32(momentum)), float(np.float32(push))
        new_v, new_e = [], []
        for p in range(4):
            v = vs[p]
            total = xlo[p] * vs[(p + 3) % 4] + xhi[p] * vs[(p + 1) % 4]
            total = total + (ylo[p] * roll(v, 1, 0) + yhi[p] * roll(v, -1, 0))
            total = total + (zlo[p] * roll(v, 1, 1) + zhi[p] * roll(v, -1, 1))
            ne = momentum * es[p] + push * ((gs[p] - v) + total)
            new_e.append(ne)
            new_v.append(v + ne)
        vs, es = new_v, new_e
    w4 = jnp.concatenate(vs, axis=0)
    fine = iota((128, 128), 1)
    coarse = iota((128, 128), 0)
    m = jnp.where((fine >> 1) == coarse, 1.0, 0.0)
    wide = spread(dup2, w4, 8, m)
    for i in range(8):
        p = i // 2
        va3[i] = u3[i] + wide[16 * p : 16 * p + 16]
    post(level, va3, vb3, upd3, [(0, 8)] * 4, 8)
    for m in loads[:6]:
        m.wait()
    w3 = va3[...].reshape(128, 128)
    wide = spread(dup2, w3, 16, spread_matrix(96, 128))
    for i in range(16):
        p = i // 2
        va2[i] = u2[i] + wide[32 * p : 32 * p + 32]
    level = Level(cx2, cy2, cz2, inv2, rhs2, 16)
    post(level, va2, vb2, upd2, [(0, 16)] * 4, FULL)
    for m in loads[6:12]:
        m.wait()
    w2 = jnp.concatenate([va2[:, 0:8, :], va2[:, 24:32, :]], axis=1).reshape(256, 128)
    wide = spread(dup1, w2, 16, spread_matrix(96, 128))
    for i in range(32):
        p = i // 2
        va1[i] = u1[i] + wide[32 * p : 32 * p + 32]
    level = Level(cx1, cy1, cz1, inv1, rhs1, 32)
    post(level, va1, vb1, upd1, [(0, 32)] * 4, FULL)
    for m in loads[12:]:
        m.wait()
    rows = [
        jnp.concatenate([va1[i % 32, 0:8, :], mix_rows(va1, i % 32)], axis=0) for i in range(-4, 12)
    ]
    w1 = jnp.concatenate(rows, axis=0)
    wide = spread(dup0, w1, 16, spread_matrix(192, 256))
    for i in range(3, 29):
        p = i // 2
        va0[i] = u0[i] + wide[32 * p : 32 * p + 32]
    level = Level(cx0, cy0, cz0, inv0, rhs0, 0)
    post(level, va0, vb0, upd0, [(4, 28), (5, 27), (6, 26), (7, 25)], NEAR)

    def finish(i):
        here, d = level.defect(va0, i)
        sol_ref[i - 8] = here[0:16, 0:128]
        res_ref[i - 8] = diag0[i - 8] * d[0:16, 0:128]

    loop(8, 24, NEAR, finish)


def mix_rows(ref, i):
    low = iota((8, 128), 0) < 4
    return jnp.where(low, ref[i, 8:16, :], ref[i, 24:32, :])


def call(body, args, outs, scratch=(), limit=16, far_in=(), far_out=(), copies=0, us=1):
    near, far = pl.BlockSpec(memory_space=pltpu.VMEM), pl.BlockSpec(memory_space=pltpu.HBM)
    return pl.pallas_call(
        body,
        out_shape=[jax.ShapeDtypeStruct(s, F32) for s in outs],
        in_specs=[far if i in far_in else near for i in range(len(args))],
        out_specs=[far if i in far_out else near for i in range(len(outs))],
        scratch_shapes=[pltpu.VMEM(s, F32) for s in scratch]
        + [pltpu.SemaphoreType.DMA] * copies,
        compiler_params=pltpu.CompilerParams(vmem_limit_bytes=limit * MIB),
        name=body.__name__,
        cost_estimate=pl.CostEstimate(
            flops=0, bytes_accessed=us * 3_000_000, transcendentals=0
        ),
    )(*args)


def move(values, axis, shift):
    size = lax.axis_size(axis)
    return lax.ppermute(values, axis, [((i + shift) % size, i) for i in range(size)])


def local(source, conductivity):
    f, b = source, conductivity
    ends = lax.optimization_barrier(jnp.concatenate([f[8:16], b[7:16], f[0:8], b[0:9]]))
    to_hi, to_lo = ends[:17], ends[17:]
    xs = [move(to_hi, "gx", -1), move(to_lo, "gx", 1)]
    to_hi, to_lo = call(packy0, [f, b] + xs, [(66, 8, 128)] * 2)
    ys = [move(to_hi, "gy", -1), move(to_lo, "gy", 1)]
    to_hi, to_lo, fw, bw = call(
        pack0, [f, b] + xs + ys, [(14, 32, 128)] * 2 + [(32, 32, 128), (34, 32, 128)]
    )
    zs = [move(to_hi, "gz", -1), move(to_lo, "gz", 1)]
    big = (32, 32, 256)
    cx0, cy0, cz0, inv0, d0, xpc = call(
        fine_coef,
        [bw] + [e[64:].reshape(16, 128) for e in ys] + zs,
        [big] * 5 + [(4, TILES, 16, 128)],
        [(34, 32, 256), big, (33, 32, 256), (4, 2, 256, 128)],
        24,
    )
    u0, cx0, cy0, cz0, inv0, rhs0, diag0, xpf = call(
        fine_down,
        [fw] + zs + [cx0, cy0, cz0, inv0, d0],
        [big] * 6 + [(16, 16, 128), (1, TILES, 16, 128)],
        [big] * 5 + [(1, 2, 256, 128)],
        24,
        far_out=range(6),
        copies=6,
        us=20,
    )

    def along_x(xp):
        return [xp] + [move(xp, "gx", k) for k in (1, 2, 3)]

    def along_y(xs):
        to_hi, to_lo = call(packy1, xs, [(xs[0].shape[0], 6 * TILES, 8, 128)] * 2)
        return xs + [move(to_hi, "gy", -1), move(to_lo, "gy", 1)]

    coarse, xpf = lax.optimization_barrier((along_x(xpc), xpf))
    coarse, right_side = along_y(coarse), along_y(along_x(xpf))
    mid = (32, 32, 128)
    u1, cx1, cy1, cz1, inv1, rhs1, own2, ym, yp = call(
        mid_down,
        coarse + right_side,
        [mid] * 6 + [(5, 4, 16, 128), (5, 4, 8, 128), (5, 4, 8, 128)],
        [mid] * 11 + [(5, 512, 128)],
        far_out=range(6),
        copies=6,
    )
    from_hi, from_lo, far = move(ym, "gy", 2), move(yp, "gy", -2), move(ym, "gy", 4)
    up2, down2, w2 = call(
        pack2, (own2, from_hi, far, from_lo), [(5, 2, 32, 128)] * 2 + [(5, 4, 32, 128)]
    )
    zlo, zhi = move(up2, "gz", -1), move(down2, "gz", 1)
    low = (16, 32, 128)
    u2, cx2, cy2, cz2, inv2, rhs2, own3 = call(
        low_down,
        (w2, zlo, zhi),
        [low] * 6 + [(5, 16, 128)],
        [low] * 10 + [(5, 256, 128)],
        far_out=range(6),
        copies=6,
    )
    everyone = jnp.broadcast_to(own3[None], (8, 5, 16, 128))
    gathered = lax.all_to_all(everyone, "gz", 0, 0)
    tiny = (8, 16, 128)
    return tuple(
        call(
            up,
            (
                gathered,
                u2, cx2, cy2, cz2, inv2, rhs2,
                u1, cx1, cy1, cz1, inv1, rhs1,
                u0, cx0, cy0, cz0, inv0, rhs0, diag0,
            ),
            [(16, 16, 128)] * 2,
            [(5,) + tiny] + [tiny] * 6 + [(5, 64, 128)]
            + [low] * 3 + [(256, 128)] + [mid] * 3 + [(512, 128)] + [big] * 3 + [(512, 128)]
            + [low] * 6 + [mid] * 6 + [big] * 6 + [(16, 16, 128)],
            28,
            far_in=range(1, 20),
            copies=19,
        )
    )


def solution(mesh):
    spec = P("gx", "gy", "gz")
    return jax.shard_map(
        local, mesh=mesh, in_specs=(spec, spec), out_specs=(spec, spec), check_vma=False
    )
```

```python
import functools

import jax
import jax.numpy as jnp
import numpy as np
from jax import lax
from jax.experimental import pallas as pl
from jax.experimental.pallas import tpu as pltpu
from jax.sharding import PartitionSpec as P

F32 = jnp.float32
CSWEEPS = 32
MIB = 1024 * 1024
NEAR, FULL = 12, 32


def chebyshev_terms(sweep_count, lower_bound, upper_bound):
    center = (upper_bound + lower_bound) / 2.0
    half_width = (upper_bound - lower_bound) / 2.0
    sigma_ratio = center / half_width
    rho_now = 1.0 / sigma_ratio
    terms = []
    for _ in range(sweep_count - 1):
        rho_next = 1.0 / (2.0 * sigma_ratio - rho_now)
        terms.append((rho_next * rho_now, 2.0 * rho_next / half_width))
        rho_now = rho_next
    return 1.0 / center, terms


FIRST, TERMS = chebyshev_terms(4, 0.6, 2.0)
CFIRST, CTERMS = chebyshev_terms(CSWEEPS, 0.05, 2.0)


def harmonic(a, b):
    return 2.0 * a * b / (a + b)


def roll(a, shift, axis):
    return pltpu.roll(a, shift % a.shape[axis], axis)


def iota(shape, dim):
    return lax.broadcasted_iota(jnp.int32, shape, dim)


def exact_dot(a, m):
    m = m.astype(jnp.bfloat16)
    high = a.astype(jnp.bfloat16)
    rest = a - high.astype(F32)
    mid = rest.astype(jnp.bfloat16)
    low = (rest - mid.astype(F32)).astype(jnp.bfloat16)
    parts = [jnp.dot(p, m, preferred_element_type=F32) for p in (high, mid, low)]
    return parts[0] + (parts[1] + parts[2])


def signed(index, size, cut):
    return jnp.where(index < cut, index, index - size)


def loop(lo, hi, unroll, body):
    rounds = (hi - lo) // unroll

    def step(t, carry):
        for u in range(unroll):
            body(lo + t * unroll + u)
        return carry

    if rounds:
        lax.fori_loop(0, rounds, step, 0)
    for i in range(lo + rounds * unroll, hi):
        body(i)


def copies_of(sources, targets, sems):
    return [pltpu.make_async_copy(a, b, s) for a, b, s in zip(sources, targets, sems)]


class Level:
    def __init__(self, cx, cy, cz, inv, rhs, wrap):
        self.cx, self.cy, self.cz, self.inv, self.rhs, self.wrap = cx, cy, cz, inv, rhs, wrap

    def around(self, i):
        if self.wrap:
            return (i + self.wrap - 1) & (self.wrap - 1), (i + 1) & (self.wrap - 1)
        return i - 1, i + 1

    def defect(self, v, i):
        below, above = self.around(i)
        here = v[i]
        cy, cz = self.cy[i], self.cz[i]
        total = self.cx[i] * v[below] + self.cx[above] * v[above]
        total = total + (cy * roll(here, 1, 0) + roll(cy * here, -1, 0))
        total = total + (cz * roll(here, 1, 1) + roll(cz * here, -1, 1))
        return here, self.rhs[i] - here + self.inv[i] * total


def sweep(level, src, dst, upd, lo, hi, unroll, momentum, push, store_update=True):
    def body(i):
        here, d = level.defect(src, i)
        e = push * d
        if momentum is not None:
            e = momentum * upd[i] + e
        if store_update:
            upd[i] = e
        dst[i] = here + e

    loop(lo, hi, unroll, body)


def z_pack(get, planes, rows, starts, width, per):
    lane = iota((rows, 128), 1)
    out = []
    for start in starts:
        tiles = []
        for g in range(0, planes, per):
            acc = jnp.zeros((rows, 128), F32)
            for p in range(g, min(g + per, planes)):
                plane, base = get(p)
                at = (p - g) * width
                moved = roll(plane, at - start - base, 1)
                acc = jnp.where((lane >= at) & (lane < at + width), moved, acc)
            tiles.append(acc)
        out.append(tiles)
    return out


def x_plane(own_ref, lo_ref, hi_ref, first, width, p):
    if p < width:
        return lo_ref, first + p
    if p < width + 16:
        return own_ref, p - width
    return hi_ref, first + p - width - 16


def f_plane(f_ref, lo_ref, hi_ref, p):
    return x_plane(f_ref, lo_ref, hi_ref, 0, 8, p)


def b_plane(b_ref, lo_ref, hi_ref, p):
    return x_plane(b_ref, lo_ref, hi_ref, 8, 9, p)


def packy0(f_ref, b_ref, lo_ref, hi_ref, up_ref, down_ref):
    for p in range(32):
        for at, (ref, q) in (
            (p, f_plane(f_ref, lo_ref, hi_ref, p)),
            (32 + p, b_plane(b_ref, lo_ref, hi_ref, p + 1)),
        ):
            up_ref[at] = ref[q, 8:16, :]
            down_ref[at] = ref[q, 0:8, :]
    row = iota((8, 128), 0)
    for ref, edge in ((up_ref, 7), (down_ref, 8)):
        for t in range(2):
            acc = jnp.zeros((8, 128), F32)
            for r in range(8):
                line = jnp.broadcast_to(b_ref[8 * t + r, edge : edge + 1, :], (8, 128))
                acc = jnp.where(row == r, line, acc)
            ref[64 + t] = acc


def pack0(
    f_ref, b_ref, xlo_ref, xhi_ref, ylo_ref, yhi_ref, up_ref, down_ref, fw_ref, bw_ref
):
    for p in range(32):
        ref, q = f_plane(f_ref, xlo_ref, xhi_ref, p)
        fw_ref[p, 0:16, :] = ref[q]
        fw_ref[p, 16:24, :] = yhi_ref[p]
        fw_ref[p, 24:32, :] = ylo_ref[p]
    for p in range(34):
        ref, q = b_plane(b_ref, xlo_ref, xhi_ref, p)
        bw_ref[p, 0:16, :] = ref[q]
        if 0 < p < 33:
            bw_ref[p, 16:24, :] = yhi_ref[31 + p]
            bw_ref[p, 24:32, :] = ylo_ref[31 + p]
        else:
            bw_ref[p, 16:32, :] = ref[q]
    ups, downs = z_pack(lambda p: (fw_ref[p], 0), 32, 32, (104, 0), 24, 5)
    more = z_pack(lambda p: (bw_ref[p + 1], 0), 32, 32, (103, 0), 25, 5)
    for g in range(7):
        up_ref[g] = ups[g]
        down_ref[g] = downs[g]
        up_ref[7 + g] = more[0][g]
        down_ref[7 + g] = more[1][g]


def fine_matrices():
    fine_lane = iota((256, 128), 0)
    coarse_lane = iota((256, 128), 1)
    both = jnp.where((fine_lane >> 1) == coarse_lane, 1.0, 0.0)
    even = jnp.where(fine_lane == 2 * coarse_lane, 1.0, 0.0)
    return both, even


def folded_rows(scr, a, count, pairs):
    def rows_of(offset):
        return jnp.concatenate(
            [scr[a, t, pl.ds(offset, count, stride=2), :] for t in range(2)], axis=1
        )

    return rows_of(0) + rows_of(1) if pairs else rows_of(0)


def fold_lanes(scr, slots, xp_ref):
    both, even = fine_matrices()
    lane = iota((8, 128), 1)
    half = lane < 64
    for a, kind in enumerate(slots):
        res = exact_dot(folded_rows(scr, a, 128, kind != "y"), even if kind == "z" else both)
        for t in range(2):
            rows = slice(t * 8, t * 8 + 8)
            for j in range(4):
                lo = res[j * 16 + t * 8 : j * 16 + t * 8 + 8]
                hi = res[(j + 4) * 16 + t * 8 : (j + 4) * 16 + t * 8 + 8]
                xp_ref[a * TILES + j, rows, :] = jnp.where(half, lo, roll(hi, 64, 1))
            for g in range(2):
                acc = None
                for q in range(4):
                    at = (4 * g + q) * 16 + t * 8
                    plane = res[at : at + 8]
                    part = jnp.where(lane < 80, plane, roll(plane, -32, 1))
                    part = roll(part, 32 * q - 64, 1)
                    acc = part if acc is None else jnp.where(lane >= 32 * q, part, acc)
                xp_ref[a * TILES + 4 + g, rows, :] = acc


def put_lanes(scr, a, p, value):
    scr[a, 0, p * 32 : p * 32 + 32, :] = value[:, 0:128]
    scr[a, 1, p * 32 : p * 32 + 32, :] = value[:, 128:256]


def fine_coef(
    b_ref, ylo_ref, yhi_ref, zlo_ref, zhi_ref,
    cx_ref, cy_ref, cz_ref, inv_ref, dw, xp_ref,
    bw, cyw, czw, cxw, scr,
):
    px, py, pz = lax.axis_index("gx"), lax.axis_index("gy"), lax.axis_index("gz")
    lane1 = iota((32, 128), 1)
    lane = iota((32, 256), 1)
    row = iota((32, 256), 0)
    for i in range(34):
        q = min(max(i - 1, 0), 31)
        g, at = 7 + q // 5, (q % 5) * 25
        right = roll(zhi_ref[g], -at, 1)
        left = roll(zlo_ref[g], 103 - at, 1)
        bw[i, :, 0:128] = b_ref[i]
        bw[i, :, 128:256] = jnp.where(lane1 < 25, right, jnp.where(lane1 >= 103, left, 1.0))
    y_at = (16 * py + signed(row, 32, 24)) & 127
    z_at = (128 * pz + signed(lane, 256, 192)) & 1023
    y_open = jnp.where(y_at == 0, 0.0, 1.0)
    z_open = jnp.where(z_at == 0, 0.0, 1.0)
    y_low, y_high = (row == 0) & (py == 0), (row == 16) & (py == 7)
    z_low, z_high = (lane == 0) & (pz == 0), (lane == 128) & (pz == 7)

    def face_x(i):
        here, below = bw[i + 1], bw[i]
        inner = jnp.where((px == 0) & (i == 8), here, below)
        outer = jnp.where((px == 3) & (i == 24), below, here)
        cxw[i] = harmonic(outer, inner)

    loop(0, 33, 3, face_x)

    def coefficients(i):
        b = bw[i + 1]
        e_at = jnp.clip(i - 8, 0, 15)
        below = ylo_ref[pl.ds(e_at, 1), :]
        above = yhi_ref[pl.ds(e_at, 1), :]
        below = jnp.concatenate([below, below], axis=1)
        above = jnp.concatenate([above, above], axis=1)
        before = jnp.where(row == 24, jnp.broadcast_to(below, (32, 256)), roll(b, 1, 0))
        cy = harmonic(jnp.where(y_high, before, b), jnp.where(y_low, b, before))
        outer = harmonic(b[16:24], jnp.broadcast_to(above, (8, 256)))
        after = roll(cy, -1, 0)
        after = jnp.concatenate(
            [after[0:16], jnp.where(row[16:24] == 23, outer, after[16:24]), after[24:32]], axis=0
        )
        before = roll(b, 1, 1)
        cz = harmonic(jnp.where(z_high, before, b), jnp.where(z_low, b, before))
        d = cxw[i] + cxw[i + 1] + (cy + after) + (cz + roll(cz, -1, 1))
        x_open = jnp.where(((16 * px + i + 56) & 63) == 0, 0.0, 1.0).astype(F32)
        cx_ref[i] = x_open * cxw[i]
        cy_ref[i] = y_open * cy
        cz_ref[i] = z_open * cz
        cyw[i] = cy
        czw[i] = cz
        inv_ref[i] = 1.0 / d
        dw[i] = d

    loop(0, 32, 4, coefficients)
    for p in range(8):
        i = 8 + 2 * p
        put_lanes(scr, 0, p, 0.25 * cxw[i])
        put_lanes(scr, 1, p, 0.25 * (cyw[i] + cyw[i + 1]))
        put_lanes(scr, 2, p, 0.25 * (czw[i] + czw[i + 1]))
    put_lanes(scr, 3, 0, 0.25 * cxw[24])

    def beyond(i):
        b = bw[i + 1]
        far = jnp.where(py == 0, roll(b, 1, 0)[0:8], b[16:24])
        return harmonic(far, far)

    for p in range(8):
        i = 8 + 2 * p
        far = 0.25 * (beyond(i) + beyond(i + 1))
        scr[3, 0, 32 + 8 * p : 40 + 8 * p, :] = far[:, 0:128]
        scr[3, 1, 32 + 8 * p : 40 + 8 * p, :] = far[:, 128:256]
    fold_lanes(scr, ("x", "y", "z"), xp_ref)
    both, _ = fine_matrices()
    xp_ref[3 * TILES] = exact_dot(folded_rows(scr, 3, 16, True), both)
    far = jnp.concatenate([scr[3, t, pl.ds(32, 8, stride=8), :] for t in range(2)], axis=1)
    xp_ref[3 * TILES + 1, 0:8, :] = exact_dot(far, both)
    xp_ref[3 * TILES + 1, 8:16, :] = jnp.zeros((8, 128), F32)


def fine_down(
    f_ref, zlo_ref, zhi_ref, cx_ref, cy_ref, cz_ref, inv_ref, dw,
    u_far, cx_far, cy_far, cz_far, inv_far, rhs_far, diag_ref, xp_ref,
    u_ref, rhs_ref, va, vb, upd, scr, *sems,
):
    saves = copies_of(
        (cx_ref, cy_ref, cz_ref, inv_ref, rhs_ref, u_ref),
        (cx_far, cy_far, cz_far, inv_far, rhs_far, u_far),
        sems,
    )
    for m in saves[:4]:
        m.start()
    lane1 = iota((32, 128), 1)
    for i in range(32):
        g, at = i // 5, (i % 5) * 24
        right = roll(zhi_ref[g], -at, 1)
        left = roll(zlo_ref[g], 104 - at, 1)
        halo = jnp.where(lane1 < 24, right, jnp.where(lane1 >= 104, left, 0.0))
        for t, part in enumerate((f_ref[i], halo)):
            at = slice(128 * t, 128 * t + 128)
            scaled = part * inv_ref[i, :, at]
            rhs_ref[i, :, at] = scaled
            scaled = FIRST * scaled
            upd[i, :, at] = scaled
            va[i, :, at] = scaled
    saves[4].start()
    level = Level(cx_ref, cy_ref, cz_ref, inv_ref, rhs_ref, 0)
    sweep(level, va, vb, upd, 1, 31, NEAR, *TERMS[0])
    sweep(level, vb, va, upd, 2, 30, NEAR, *TERMS[1])
    sweep(level, va, u_ref, upd, 3, 29, NEAR, *TERMS[2], store_update=False)
    saves[5].start()

    def save_diag(i):
        diag_ref[i] = dw[i + 8, 0:16, 0:128]

    loop(0, 16, 4, save_diag)
    for p in range(8):
        i = 8 + 2 * p
        total = None
        for k in (i, i + 1):
            _, d = level.defect(u_ref, k)
            r = dw[k] * d
            total = r if total is None else total + r
        put_lanes(scr, 0, p, 0.125 * total)
    fold_lanes(scr, ("f",), xp_ref)
    for m in saves:
        m.wait()


TILES = 6


def packy1(x0, x1, x2, x3, up_ref, down_ref):
    low = iota((8, 128), 0) < 4
    xs = (x0, x1, x2, x3)
    tiles = up_ref.shape[0] // 6
    half = 2 * tiles
    for q in range(2 * half):
        own = xs[q // tiles][q % tiles, 0:8, :]
        up_ref[q] = own
        down_ref[q] = own
    for q in range(half):
        one = xs[q // tiles][q % tiles, 8:16, :]
        two = xs[2 + q // tiles][q % tiles, 8:16, :]
        up_ref[2 * half + q] = jnp.where(low, roll(one, 4, 0), two)
        down_ref[2 * half + q] = jnp.where(low, one, roll(two, 4, 0))


def unpack1(xs, lo_ref, hi_ref, k, t, own_face=False):
    row = iota((8, 128), 0)
    tiles = hi_ref.shape[0] // 6
    q, half = k * tiles + t, 2 * tiles
    right, left = hi_ref[2 * half + q % half], lo_ref[2 * half + q % half]
    if q < half:
        edge = jnp.where(row < 4, right, roll(left, 4, 0))
    else:
        edge = jnp.where(row < 4, roll(right, 4, 0), left)
    after = hi_ref[q]
    if own_face:
        after = jnp.where(row == 0, xs[k][t, 8:16, :], after)
    return jnp.concatenate([xs[k][t, 0:8, :], after, edge, lo_ref[q]], axis=0)


def pair_matrices(cut, size_in=128):
    fine = iota((size_in, 128), 0)
    coarse = iota((size_in, 128), 1)
    at = signed(fine, size_in, cut)
    both = jnp.where(((at >> 1) & 127) == coarse, 1.0, 0.0)
    even = jnp.where((((at >> 1) & 127) == coarse) & ((at & 1) == 0), 1.0, 0.0)
    return both, even


def restrict(scr, both, even, count, arrays=5):
    out = []
    for a in range(arrays):
        folded = scr[a, pl.ds(0, count, stride=2), :]
        if a != 2:
            folded = folded + scr[a, pl.ds(1, count, stride=2), :]
        out.append(exact_dot(folded, even if a == 3 else both))
    return out


def mid_down(
    c0, c1, c2, c3, clo_ref, chi_ref, f0, f1, f2, f3, flo_ref, fhi_ref,
    u_far, cx_far, cy_far, cz_far, inv_far, rhs_far, own_ref, ym_ref, yp_ref,
    u_ref, cx_ref, cy_ref, cz_ref, inv_ref, rhs_ref,
    va, vb, upd, dw, ux, uy, uz, hx, oth, scr, *sems,
):
    saves = copies_of(
        (cx_ref, cy_ref, cz_ref, inv_ref, rhs_ref, u_ref),
        (cx_far, cy_far, cz_far, inv_far, rhs_far, u_far),
        sems,
    )
    lane = iota((32, 128), 1)
    px, py, pz = lax.axis_index("gx"), lax.axis_index("gy"), lax.axis_index("gz")
    row = iota((32, 128), 0)
    coarse = ((c0, c1, c2, c3), clo_ref, chi_ref)
    pieces = [(ux, 0.0) + coarse + (0,), (uy, 0.0) + coarse + (1,), (uz, 1.0) + coarse + (2,)]
    pieces += [(va, 0.0, (f0, f1, f2, f3), flo_ref, fhi_ref, 0)]
    for target, fill, xs, lo_ref, hi_ref, a in pieces:
        face = target is uy
        for k in range(4):
            sides = [
                unpack1(xs, lo_ref, hi_ref, k, TILES * a + 4 + g, face) for g in range(2)
            ]
            for j in range(4):
                base = unpack1(xs, lo_ref, hi_ref, k, TILES * a + j, face)
                for g in range(2):
                    own = roll(base, 64, 1) if g else base
                    right = roll(sides[g], 64 - 32 * j, 1)
                    left = roll(sides[g], 96 - 32 * j, 1)
                    halo = jnp.where(lane < 80, right, jnp.where(lane >= 112, left, fill))
                    target[8 * k + 4 * g + j] = jnp.where(lane < 64, own, halo)
    high_x = None
    for k in range(4):
        part = unpack1(coarse[0], clo_ref, chi_ref, k, 3 * TILES)
        high_x = part if high_x is None else jnp.where(px == 3 - k, part, high_x)
    hx[...] = high_x
    for k in range(4):
        oth[8 * k : 8 * k + 8, :] = coarse[0][k][3 * TILES + 1, 0:8, :]
    y_open = jnp.where(((8 * py + signed(row, 32, 20)) & 63) == 0, 0.0, 1.0)
    z_open = jnp.where(((64 * pz + signed(lane, 128, 96)) & 511) == 0, 0.0, 1.0)

    def coefficients(i):
        x_at = (8 * px + i) & 31
        cx, cy, cz = ux[i], uy[i], uz[i]
        above = jnp.where(x_at == 31, hx[...], ux[(i + 1) & 31])
        other = jnp.broadcast_to(oth[pl.ds(i, 1), :], (32, 128))
        here = jnp.where((row == 8) & (py == 7), other, cy)
        after = jnp.where((row == 31) & (py == 0), other, roll(cy, -1, 0))
        d = cx + above + (here + after) + (cz + roll(cz, -1, 1))
        cx_ref[i] = jnp.where(x_at == 0, 0.0, 1.0).astype(F32) * cx
        cy_ref[i] = y_open * cy
        cz_ref[i] = z_open * cz
        inv = 1.0 / d
        inv_ref[i] = inv
        dw[i] = d
        g = 4.0 * va[i] * inv
        rhs_ref[i] = g
        first = FIRST * g
        upd[i] = first
        va[i] = first

    loop(0, 32, 8, coefficients)
    for m in saves[:5]:
        m.start()
    level = Level(cx_ref, cy_ref, cz_ref, inv_ref, rhs_ref, 32)
    sweep(level, va, vb, upd, 0, 32, FULL, *TERMS[0])
    sweep(level, vb, va, upd, 0, 32, FULL, *TERMS[1])
    sweep(level, va, u_ref, upd, 0, 32, FULL, *TERMS[2], store_update=False)
    saves[5].start()
    for p in range(16):
        i = 2 * p
        _, d0 = level.defect(u_ref, i)
        _, d1 = level.defect(u_ref, i + 1)
        at = slice(32 * p, 32 * p + 32)
        scr[0, at, :] = 0.03125 * (dw[i] * d0 + dw[i + 1] * d1)
        scr[1, at, :] = 0.25 * ux[i]
        scr[2, at, :] = 0.25 * (uy[i] + uy[i + 1])
        scr[3, at, :] = 0.25 * (uz[i] + uz[i + 1])
    scr[4, 0:32, :] = 0.25 * hx[...]
    both, even = pair_matrices(96)
    f, cx, cy, cz = [r.reshape(16, 16, 128) for r in restrict(scr, both, even, 256, 4)]
    high_x = exact_dot(scr[4, pl.ds(0, 16, stride=2), :] + scr[4, pl.ds(1, 16, stride=2), :], both)
    y_open = jnp.where(((4 * py + signed(row[:16], 16, 10)) & 31) == 0, 0.0, 1.0)
    z_open = jnp.where(((32 * pz + signed(lane[:16], 128, 96)) & 255) == 0, 0.0, 1.0)
    others = exact_dot(oth[pl.ds(0, 16, stride=2), :] + oth[pl.ds(1, 16, stride=2), :], both)
    planes = []
    for p in range(16):
        x_at = (4 * px + p) & 15
        other = jnp.broadcast_to(0.25 * others[p : p + 1], (16, 128))
        here = jnp.where((row[:16] == 4) & (py == 7), other, cy[p])
        after = jnp.where((row[:16] == 15) & (py == 0), other, roll(cy[p], -1, 0))
        above = jnp.where(x_at == 15, high_x, cx[(p + 1) % 16])
        d = cx[p] + above + (here + after) + (cz[p] + roll(cz[p], -1, 1))
        x_open = jnp.where(x_at == 0, 0.0, 1.0).astype(F32)
        planes.append((f[p], x_open * cx[p], y_open * cy[p], z_open * cz[p], d))
    lane8 = iota((16, 128), 1)
    row8 = iota((8, 128), 0)
    for a in range(5):
        for j in range(4):
            packed = planes[j][a]
            for k in range(1, 4):
                packed = jnp.where(lane8 >= 32 * k, roll(planes[4 * k + j][a], 32 * k, 1), packed)
            own_ref[a, j] = packed
            ym_ref[a, j] = jnp.where(row8 == 7, packed[8:16], packed[0:8])
            yp_ref[a, j] = jnp.where(row8 < 5, packed[0:8], packed[8:16])
    for m in saves:
        m.wait()


def pack2(own_ref, hi_ref, far_ref, lo_ref, up_ref, down_ref, w_ref):
    row = iota((8, 128), 0)
    for a in range(5):
        for j in range(4):
            hi, far, lo = hi_ref[a, j], far_ref[a, j], lo_ref[a, j]
            w_ref[a, j, 0:8, :] = jnp.where(row == 7, hi, own_ref[a, j, 0:8, :])
            w_ref[a, j, 8:16, :] = jnp.where(row == 7, far, hi)
            w_ref[a, j, 16:24, :] = jnp.where(row < 5, far, lo)
            w_ref[a, j, 24:32, :] = jnp.where(row < 5, lo, own_ref[a, j, 8:16, :])

    def get(p):
        return w_ref[p // 16, p % 4], 32 * (p % 16 // 4)

    ups, downs = z_pack(get, 80, 32, (21, 0), 11, 11)
    for g in range(8):
        up_ref[g] = ups[g]
        down_ref[g] = downs[g]


def low_down(
    w_ref, zlo_ref, zhi_ref,
    u_far, cx_far, cy_far, cz_far, inv_far, rhs_far, own_ref,
    u_ref, cx_ref, cy_ref, cz_ref, inv_ref, rhs_ref,
    va, vb, upd, dw, scr, *sems,
):
    saves = copies_of(
        (cx_ref, cy_ref, cz_ref, inv_ref, rhs_ref, u_ref),
        (cx_far, cy_far, cz_far, inv_far, rhs_far, u_far),
        sems,
    )
    lane = iota((32, 128), 1)
    targets = (va, cx_ref, cy_ref, cz_ref, dw)
    for a in range(5):
        fill = 1.0 if a == 4 else 0.0
        for p in range(16):
            base = roll(w_ref[a, p % 4], -32 * (p // 4), 1)
            g, at = (16 * a + p) // 11, (16 * a + p) % 11 * 11
            right = roll(zhi_ref[g], 32 - at, 1)
            left = roll(zlo_ref[g], 117 - at, 1)
            halo = jnp.where(lane < 43, right, jnp.where(lane >= 117, left, fill))
            targets[a][p] = jnp.where(lane < 32, base, halo)

    def coefficients(i):
        inv = 1.0 / dw[i]
        inv_ref[i] = inv
        g = 16.0 * va[i] * inv
        rhs_ref[i] = g
        first = FIRST * g
        upd[i] = first
        va[i] = first

    loop(0, 16, 8, coefficients)
    for m in saves[:5]:
        m.start()
    level = Level(cx_ref, cy_ref, cz_ref, inv_ref, rhs_ref, 16)
    sweep(level, va, vb, upd, 0, 16, FULL, *TERMS[0])
    sweep(level, vb, va, upd, 0, 16, FULL, *TERMS[1])
    sweep(level, va, u_ref, upd, 0, 16, FULL, *TERMS[2], store_update=False)
    saves[5].start()

    def edge(i):
        above = (i + 1) & 15
        cy, cz = cy_ref[i], cz_ref[i]
        inner = cx_ref[i] + cx_ref[above] + (cy + roll(cy, -1, 0)) + (cz + roll(cz, -1, 1))
        return dw[i] - inner

    for p in range(8):
        i = 2 * p
        _, d0 = level.defect(u_ref, i)
        _, d1 = level.defect(u_ref, i + 1)
        at = slice(32 * p, 32 * p + 32)
        scr[0, at, :] = 0.0078125 * (dw[i] * d0 + dw[i + 1] * d1)
        scr[1, at, :] = 0.25 * cx_ref[i]
        scr[2, at, :] = 0.25 * (cy_ref[i] + cy_ref[i + 1])
        scr[3, at, :] = 0.25 * (cz_ref[i] + cz_ref[i + 1])
        scr[4, at, :] = 0.25 * (edge(i) + edge(i + 1))
    both, even = pair_matrices(96)
    f, cx, cy, cz, e = [r.reshape(8, 16, 128) for r in restrict(scr, both, even, 128)]
    planes = []
    for p in range(8):
        inner = cx[p] + cx[(p + 1) % 8] + (cy[p] + roll(cy[p], -1, 0))
        d = inner + (cz[p] + roll(cz[p], -1, 1)) + e[p]
        planes.append((f[p], cx[p], cy[p], cz[p], d))
    lane16 = iota((16, 128), 1)
    for a in range(5):
        packed = planes[0][a]
        for p in range(1, 8):
            packed = jnp.where(lane16 >= 16 * p, roll(planes[p][a], 16 * p, 1), packed)
        own_ref[a] = packed
    for m in saves:
        m.wait()


def spread(dup, w, rows, matrix):
    count = w.shape[0]
    dup[pl.ds(0, count, stride=2), :] = w
    dup[pl.ds(1, count, stride=2), :] = w
    return exact_dot(dup[0 : 2 * count, :], matrix)


def spread_matrix(cut, size):
    coarse = iota((128, size), 0)
    at = signed(iota((128, size), 1), size, cut)
    return jnp.where(((at >> 1) & 127) == coarse, 1.0, 0.0)


def post(level, va, vb, upd, ranges, unroll):
    lo, hi = ranges[0]
    sweep(level, va, vb, upd, lo, hi, unroll, None, FIRST)
    src, dst = vb, va
    for n in range(3):
        lo, hi = ranges[n + 1]
        sweep(level, src, dst, upd, lo, hi, unroll, *TERMS[n], store_update=n < 2)
        src, dst = dst, src


def up(
    g_ref, *refs,
):
    fars, refs = refs[:19], refs[19:]
    (sol_ref, res_ref), refs = refs[:2], refs[2:]
    (l3, inv3, rhs3, u3, va3, vb3, upd3, scr3), refs = refs[:8], refs[8:]
    (va2, vb2, upd2, dup2, va1, vb1, upd1, dup1, va0, vb0, upd0, dup0), refs = refs[:12], refs[12:]
    nears, sems = refs[:19], refs[19:]
    u2, cx2, cy2, cz2, inv2, rhs2 = nears[:6]
    u1, cx1, cy1, cz1, inv1, rhs1 = nears[6:12]
    u0, cx0, cy0, cz0, inv0, rhs0, diag0 = nears[12:]
    loads = copies_of(fars, nears, sems)
    for m in loads:
        m.start()
    me = lax.axis_index("gz")
    lane = iota((16, 128), 1)
    for a in range(5):
        tiles = [g_ref[(me + k) & 7, a] for k in range(8)]
        for p in range(8):
            plane = roll(tiles[0], -16 * p, 1)
            for k in range(1, 8):
                plane = jnp.where(lane >= 16 * k, roll(tiles[k], 16 * (k - p), 1), plane)
            l3[a, p] = plane
    f3, cx3, cy3, cz3, d3 = [l3.at[a] for a in range(5)]
    level = Level(cx3, cy3, cz3, inv3, rhs3, 8)

    def start3(i):
        inv = 1.0 / d3[i]
        inv3[i] = inv
        g = 64.0 * f3[i] * inv
        rhs3[i] = g
        first = FIRST * g
        upd3[i] = first
        va3[i] = first

    loop(0, 8, 8, start3)
    sweep(level, va3, vb3, upd3, 0, 8, 8, *TERMS[0])
    sweep(level, vb3, va3, upd3, 0, 8, 8, *TERMS[1])
    sweep(level, va3, u3, upd3, 0, 8, 8, *TERMS[2], store_update=False)
    for p in range(4):
        i = 2 * p
        _, r0 = level.defect(u3, i)
        _, r1 = level.defect(u3, i + 1)
        at = slice(16 * p, 16 * p + 16)
        scr3[0, at, :] = (0.125 / 64.0) * (d3[i] * r0 + d3[i + 1] * r1)
        scr3[1, at, :] = 0.25 * cx3[i]
        scr3[2, at, :] = 0.25 * (cy3[i] + cy3[i + 1])
        scr3[3, at, :] = 0.25 * (cz3[i] + cz3[i + 1])
        total = None
        for k in (i, i + 1):
            cy, cz = cy3[k], cz3[k]
            inner = cx3[k] + cx3[(k + 1) % 8] + (cy + roll(cy, -1, 0))
            inner = inner + (cz + roll(cz, -1, 1))
            total = d3[k] - inner if total is None else total + (d3[k] - inner)
        scr3[4, at, :] = 0.25 * total
    fine = iota((128, 128), 0)
    coarse = iota((128, 128), 1) & 63
    both = jnp.where((fine >> 1) == coarse, 1.0, 0.0)
    even = jnp.where(fine == 2 * coarse, 1.0, 0.0)
    f, cx, cy, cz, e = restrict(scr3, both, even, 32)

    def cut(a, p):
        return a[8 * p : 8 * p + 8]

    fs, cxs, cys, czs = [[cut(a, p) for p in range(4)] for a in (f, cx, cy, cz)]
    invs, gs, vs, es = [], [], [], []
    for p in range(4):
        d = cxs[p] + cxs[(p + 1) % 4] + (cys[p] + roll(cys[p], -1, 0))
        d = d + (czs[p] + roll(czs[p], -1, 1)) + cut(e, p)
        invs.append(1.0 / d)
        gs.append(256.0 * fs[p] * invs[p])
        es.append(CFIRST * gs[p])
        vs.append(es[p])
    xlo = [invs[p] * cxs[p] for p in range(4)]
    xhi = [invs[p] * cxs[(p + 1) % 4] for p in range(4)]
    ylo = [invs[p] * cys[p] for p in range(4)]
    yhi = [invs[p] * roll(cys[p], -1, 0) for p in range(4)]
    zlo = [invs[p] * czs[p] for p in range(4)]
    zhi = [invs[p] * roll(czs[p], -1, 1) for p in range(4)]
    for momentum, push in CTERMS:
        momentum, push = float(np.float32(momentum)), float(np.float32(push))
        new_v, new_e = [], []
        for p in range(4):
            v = vs[p]
            total = xlo[p] * vs[(p + 3) % 4] + xhi[p] * vs[(p + 1) % 4]
            total = total + (ylo[p] * roll(v, 1, 0) + yhi[p] * roll(v, -1, 0))
            total = total + (zlo[p] * roll(v, 1, 1) + zhi[p] * roll(v, -1, 1))
            ne = momentum * es[p] + push * ((gs[p] - v) + total)
            new_e.append(ne)
            new_v.append(v + ne)
        vs, es = new_v, new_e
    w4 = jnp.concatenate(vs, axis=0)
    fine = iota((128, 128), 1)
    coarse = iota((128, 128), 0)
    m = jnp.where((fine >> 1) == coarse, 1.0, 0.0)
    wide = spread(dup2, w4, 8, m)
    for i in range(8):
        p = i // 2
        va3[i] = u3[i] + wide[16 * p : 16 * p + 16]
    post(level, va3, vb3, upd3, [(0, 8)] * 4, 8)
    for m in loads[:6]:
        m.wait()
    w3 = va3[...].reshape(128, 128)
    wide = spread(dup2, w3, 16, spread_matrix(96, 128))
    for i in range(16):
        p = i // 2
        va2[i] = u2[i] + wide[32 * p : 32 * p + 32]
    level = Level(cx2, cy2, cz2, inv2, rhs2, 16)
    post(level, va2, vb2, upd2, [(0, 16)] * 4, FULL)
    for m in loads[6:12]:
        m.wait()
    w2 = jnp.concatenate([va2[:, 0:8, :], va2[:, 24:32, :]], axis=1).reshape(256, 128)
    wide = spread(dup1, w2, 16, spread_matrix(96, 128))
    for i in range(32):
        p = i // 2
        va1[i] = u1[i] + wide[32 * p : 32 * p + 32]
    level = Level(cx1, cy1, cz1, inv1, rhs1, 32)
    post(level, va1, vb1, upd1, [(0, 32)] * 4, FULL)
    for m in loads[12:]:
        m.wait()
    rows = [
        jnp.concatenate([va1[i % 32, 0:8, :], mix_rows(va1, i % 32)], axis=0) for i in range(-4, 12)
    ]
    w1 = jnp.concatenate(rows, axis=0)
    wide = spread(dup0, w1, 16, spread_matrix(192, 256))
    for i in range(3, 29):
        p = i // 2
        va0[i] = u0[i] + wide[32 * p : 32 * p + 32]
    level = Level(cx0, cy0, cz0, inv0, rhs0, 0)
    post(level, va0, vb0, upd0, [(4, 28), (5, 27), (6, 26), (7, 25)], NEAR)

    def finish(i):
        here, d = level.defect(va0, i)
        sol_ref[i - 8] = here[0:16, 0:128]
        res_ref[i - 8] = diag0[i - 8] * d[0:16, 0:128]

    loop(8, 24, NEAR, finish)


def mix_rows(ref, i):
    low = iota((8, 128), 0) < 4
    return jnp.where(low, ref[i, 8:16, :], ref[i, 24:32, :])


def call(body, args, outs, scratch=(), limit=16, far_in=(), far_out=(), copies=0, us=1):
    near, far = pl.BlockSpec(memory_space=pltpu.VMEM), pl.BlockSpec(memory_space=pltpu.HBM)
    return pl.pallas_call(
        body,
        out_shape=[jax.ShapeDtypeStruct(s, F32) for s in outs],
        in_specs=[far if i in far_in else near for i in range(len(args))],
        out_specs=[far if i in far_out else near for i in range(len(outs))],
        scratch_shapes=[pltpu.VMEM(s, F32) for s in scratch]
        + [pltpu.SemaphoreType.DMA] * copies,
        compiler_params=pltpu.CompilerParams(vmem_limit_bytes=limit * MIB),
        name=body.__name__,
        cost_estimate=pl.CostEstimate(
            flops=0, bytes_accessed=us * 3_000_000, transcendentals=0
        ),
    )(*args)


def move(values, axis, shift):
    size = lax.axis_size(axis)
    return lax.ppermute(values, axis, [((i + shift) % size, i) for i in range(size)])


def local(source, conductivity):
    f, b = source, conductivity
    ends = lax.optimization_barrier(jnp.concatenate([f[8:16], b[7:16], f[0:8], b[0:9]]))
    to_hi, to_lo = ends[:17], ends[17:]
    xs = [move(to_hi, "gx", -1), move(to_lo, "gx", 1)]
    to_hi, to_lo = call(packy0, [f, b] + xs, [(66, 8, 128)] * 2)
    ys = [move(to_hi, "gy", -1), move(to_lo, "gy", 1)]
    to_hi, to_lo, fw, bw = call(
        pack0, [f, b] + xs + ys, [(14, 32, 128)] * 2 + [(32, 32, 128), (34, 32, 128)]
    )
    zs = [move(to_hi, "gz", -1), move(to_lo, "gz", 1)]
    big = (32, 32, 256)
    cx0, cy0, cz0, inv0, d0, xpc = call(
        fine_coef,
        [bw] + [e[64:].reshape(16, 128) for e in ys] + zs,
        [big] * 5 + [(3 * TILES + 2, 16, 128)],
        [(34, 32, 256), big, big, (33, 32, 256), (4, 2, 256, 128)],
        24,
    )
    u0, cx0, cy0, cz0, inv0, rhs0, diag0, xpf = call(
        fine_down,
        [fw] + zs + [cx0, cy0, cz0, inv0, d0],
        [big] * 6 + [(16, 16, 128), (TILES, 16, 128)],
        [big] * 5 + [(1, 2, 256, 128)],
        24,
        far_out=range(6),
        copies=6,
        us=20,
    )

    def along_x(xp):
        return [xp] + [move(xp, "gx", k) for k in (1, 2, 3)]

    def along_y(xs, tiles, us):
        to_hi, to_lo = call(packy1, xs, [(6 * tiles, 8, 128)] * 2, us=us)
        return xs + [move(to_hi, "gy", -1), move(to_lo, "gy", 1)]

    coarse, xpf = lax.optimization_barrier((along_x(xpc), xpf))
    coarse, right_side = along_y(coarse, 3 * TILES + 1, 20), along_y(along_x(xpf), TILES, 1)
    mid = (32, 32, 128)
    u1, cx1, cy1, cz1, inv1, rhs1, own2, ym, yp = call(
        mid_down,
        coarse + right_side,
        [mid] * 6 + [(5, 4, 16, 128), (5, 4, 8, 128), (5, 4, 8, 128)],
        [mid] * 13 + [(32, 128), (32, 128), (5, 512, 128)],
        far_out=range(6),
        copies=6,
    )
    from_hi, from_lo, far = move(ym, "gy", 2), move(yp, "gy", -2), move(ym, "gy", 4)
    up2, down2, w2 = call(
        pack2, (own2, from_hi, far, from_lo), [(8, 32, 128)] * 2 + [(5, 4, 32, 128)]
    )
    zlo, zhi = move(up2, "gz", -1), move(down2, "gz", 1)
    low = (16, 32, 128)
    u2, cx2, cy2, cz2, inv2, rhs2, own3 = call(
        low_down,
        (w2, zlo, zhi),
        [low] * 6 + [(5, 16, 128)],
        [low] * 10 + [(5, 256, 128)],
        far_out=range(6),
        copies=6,
    )
    everyone = jnp.broadcast_to(own3[None], (8, 5, 16, 128))
    gathered = lax.all_to_all(everyone, "gz", 0, 0)
    tiny = (8, 16, 128)
    return tuple(
        call(
            up,
            (
                gathered,
                u2, cx2, cy2, cz2, inv2, rhs2,
                u1, cx1, cy1, cz1, inv1, rhs1,
                u0, cx0, cy0, cz0, inv0, rhs0, diag0,
            ),
            [(16, 16, 128)] * 2,
            [(5,) + tiny] + [tiny] * 6 + [(5, 64, 128)]
            + [low] * 3 + [(256, 128)] + [mid] * 3 + [(512, 128)] + [big] * 3 + [(512, 128)]
            + [low] * 6 + [mid] * 6 + [big] * 6 + [(16, 16, 128)],
            28,
            far_in=range(1, 20),
            copies=19,
        )
    )


def solution(mesh):
    spec = P("gx", "gy", "gz")
    return jax.shard_map(
        local, mesh=mesh, in_specs=(spec, spec), out_specs=(spec, spec), check_vma=False
    )
```

```python
import functools

import jax
import jax.numpy as jnp
import numpy as np
from jax import lax
from jax.experimental import pallas as pl
from jax.experimental.pallas import tpu as pltpu
from jax.sharding import PartitionSpec as P

F32 = jnp.float32
CSWEEPS = 32
MIB = 1024 * 1024
NEAR, FULL = 12, 32


def chebyshev_terms(sweep_count, lower_bound, upper_bound):
    center = (upper_bound + lower_bound) / 2.0
    half_width = (upper_bound - lower_bound) / 2.0
    sigma_ratio = center / half_width
    rho_now = 1.0 / sigma_ratio
    terms = []
    for _ in range(sweep_count - 1):
        rho_next = 1.0 / (2.0 * sigma_ratio - rho_now)
        terms.append((rho_next * rho_now, 2.0 * rho_next / half_width))
        rho_now = rho_next
    return 1.0 / center, terms


FIRST, TERMS = chebyshev_terms(4, 0.6, 2.0)
CFIRST, CTERMS = chebyshev_terms(CSWEEPS, 0.05, 2.0)


def harmonic(a, b):
    return 2.0 * a * b / (a + b)


def roll(a, shift, axis):
    return pltpu.roll(a, shift % a.shape[axis], axis)


def iota(shape, dim):
    return lax.broadcasted_iota(jnp.int32, shape, dim)


def exact_dot(a, m):
    m = m.astype(jnp.bfloat16)
    high = a.astype(jnp.bfloat16)
    rest = a - high.astype(F32)
    mid = rest.astype(jnp.bfloat16)
    low = (rest - mid.astype(F32)).astype(jnp.bfloat16)
    parts = [jnp.dot(p, m, preferred_element_type=F32) for p in (high, mid, low)]
    return parts[0] + (parts[1] + parts[2])


def signed(index, size, cut):
    return jnp.where(index < cut, index, index - size)


def loop(lo, hi, unroll, body):
    rounds = (hi - lo) // unroll

    def step(t, carry):
        for u in range(unroll):
            body(lo + t * unroll + u)
        return carry

    if rounds:
        lax.fori_loop(0, rounds, step, 0)
    for i in range(lo + rounds * unroll, hi):
        body(i)


def copies_of(sources, targets, sems):
    return [pltpu.make_async_copy(a, b, s) for a, b, s in zip(sources, targets, sems)]


class Level:
    def __init__(self, cx, cy, cz, inv, rhs, wrap):
        self.cx, self.cy, self.cz, self.inv, self.rhs, self.wrap = cx, cy, cz, inv, rhs, wrap

    def around(self, i):
        if self.wrap:
            return (i + self.wrap - 1) & (self.wrap - 1), (i + 1) & (self.wrap - 1)
        return i - 1, i + 1

    def defect(self, v, i):
        below, above = self.around(i)
        here = v[i]
        cy, cz = self.cy[i], self.cz[i]
        total = self.cx[i] * v[below] + self.cx[above] * v[above]
        total = total + (cy * roll(here, 1, 0) + roll(cy * here, -1, 0))
        total = total + (cz * roll(here, 1, 1) + roll(cz * here, -1, 1))
        return here, self.rhs[i] - here + self.inv[i] * total


def sweep(level, src, dst, upd, lo, hi, unroll, momentum, push, store_update=True):
    def body(i):
        here, d = level.defect(src, i)
        e = push * d
        if momentum is not None:
            e = momentum * upd[i] + e
        if store_update:
            upd[i] = e
        dst[i] = here + e

    loop(lo, hi, unroll, body)


def z_pack(get, planes, rows, starts, width, per):
    lane = iota((rows, 128), 1)
    out = []
    for start in starts:
        tiles = []
        for g in range(0, planes, per):
            acc = jnp.zeros((rows, 128), F32)
            for p in range(g, min(g + per, planes)):
                plane, base = get(p)
                at = (p - g) * width
                moved = roll(plane, at - start - base, 1)
                acc = jnp.where((lane >= at) & (lane < at + width), moved, acc)
            tiles.append(acc)
        out.append(tiles)
    return out


def x_plane(own_ref, lo_ref, hi_ref, first, width, p):
    if p < width:
        return lo_ref, first + p
    if p < width + 16:
        return own_ref, p - width
    return hi_ref, first + p - width - 16


def f_plane(f_ref, lo_ref, hi_ref, p):
    return x_plane(f_ref, lo_ref, hi_ref, 0, 8, p)


def b_plane(b_ref, lo_ref, hi_ref, p):
    return x_plane(b_ref, lo_ref, hi_ref, 8, 9, p)


def packy0(f_ref, b_ref, lo_ref, hi_ref, up_ref, down_ref):
    for p in range(32):
        for at, (ref, q) in (
            (p, f_plane(f_ref, lo_ref, hi_ref, p)),
            (32 + p, b_plane(b_ref, lo_ref, hi_ref, p + 1)),
        ):
            up_ref[at] = ref[q, 8:16, :]
            down_ref[at] = ref[q, 0:8, :]
    row = iota((8, 128), 0)
    for ref, edge in ((up_ref, 7), (down_ref, 8)):
        for t in range(2):
            acc = jnp.zeros((8, 128), F32)
            for r in range(8):
                line = jnp.broadcast_to(b_ref[8 * t + r, edge : edge + 1, :], (8, 128))
                acc = jnp.where(row == r, line, acc)
            ref[64 + t] = acc


def pack0b(b_ref, xlo_ref, xhi_ref, ylo_ref, yhi_ref, up_ref, down_ref, w_ref):
    for p in range(34):
        ref, q = b_plane(b_ref, xlo_ref, xhi_ref, p)
        w_ref[p, 0:16, :] = ref[q]
        if 0 < p < 33:
            w_ref[p, 16:24, :] = yhi_ref[31 + p]
            w_ref[p, 24:32, :] = ylo_ref[31 + p]
        else:
            w_ref[p, 16:32, :] = ref[q]
    ups, downs = z_pack(lambda p: (w_ref[p + 1], 0), 32, 32, (103, 0), 25, 5)
    for g in range(7):
        up_ref[g] = ups[g]
        down_ref[g] = downs[g]


def pack0f(f_ref, xlo_ref, xhi_ref, ylo_ref, yhi_ref, up_ref, down_ref, w_ref):
    for p in range(32):
        ref, q = f_plane(f_ref, xlo_ref, xhi_ref, p)
        w_ref[p, 0:16, :] = ref[q]
        w_ref[p, 16:24, :] = yhi_ref[p]
        w_ref[p, 24:32, :] = ylo_ref[p]
    ups, downs = z_pack(lambda p: (w_ref[p], 0), 32, 32, (104, 0), 24, 5)
    for g in range(7):
        up_ref[g] = ups[g]
        down_ref[g] = downs[g]


def fine_matrices():
    fine_lane = iota((256, 128), 0)
    coarse_lane = iota((256, 128), 1)
    both = jnp.where((fine_lane >> 1) == coarse_lane, 1.0, 0.0)
    even = jnp.where(fine_lane == 2 * coarse_lane, 1.0, 0.0)
    return both, even


def folded_rows(scr, a, count, pairs):
    def rows_of(offset):
        return jnp.concatenate(
            [scr[a, t, pl.ds(offset, count, stride=2), :] for t in range(2)], axis=1
        )

    return rows_of(0) + rows_of(1) if pairs else rows_of(0)


def fold_lanes(scr, slots, xp_ref):
    both, even = fine_matrices()
    lane = iota((8, 128), 1)
    half = lane < 64
    for a, kind in enumerate(slots):
        res = exact_dot(folded_rows(scr, a, 128, kind != "y"), even if kind == "z" else both)
        for t in range(2):
            rows = slice(t * 8, t * 8 + 8)
            for j in range(4):
                lo = res[j * 16 + t * 8 : j * 16 + t * 8 + 8]
                hi = res[(j + 4) * 16 + t * 8 : (j + 4) * 16 + t * 8 + 8]
                xp_ref[a * TILES + j, rows, :] = jnp.where(half, lo, roll(hi, 64, 1))
            for g in range(2):
                acc = None
                for q in range(4):
                    at = (4 * g + q) * 16 + t * 8
                    plane = res[at : at + 8]
                    part = jnp.where(lane < 80, plane, roll(plane, -32, 1))
                    part = roll(part, 32 * q - 64, 1)
                    acc = part if acc is None else jnp.where(lane >= 32 * q, part, acc)
                xp_ref[a * TILES + 4 + g, rows, :] = acc


def put_lanes(scr, a, p, value):
    scr[a, 0, p * 32 : p * 32 + 32, :] = value[:, 0:128]
    scr[a, 1, p * 32 : p * 32 + 32, :] = value[:, 128:256]


def fine_coef(
    b_ref, ylo_ref, yhi_ref, zlo_ref, zhi_ref,
    cx_ref, cy_ref, cz_ref, inv_ref, dw, xp_ref,
    bw, cyw, czw, cxw, scr,
):
    px, py, pz = lax.axis_index("gx"), lax.axis_index("gy"), lax.axis_index("gz")
    lane1 = iota((32, 128), 1)
    lane = iota((32, 256), 1)
    row = iota((32, 256), 0)
    for i in range(34):
        q = min(max(i - 1, 0), 31)
        g, at = q // 5, (q % 5) * 25
        right = roll(zhi_ref[g], -at, 1)
        left = roll(zlo_ref[g], 103 - at, 1)
        bw[i, :, 0:128] = b_ref[i]
        bw[i, :, 128:256] = jnp.where(lane1 < 25, right, jnp.where(lane1 >= 103, left, 1.0))
    y_at = (16 * py + signed(row, 32, 24)) & 127
    z_at = (128 * pz + signed(lane, 256, 192)) & 1023
    y_open = jnp.where(y_at == 0, 0.0, 1.0)
    z_open = jnp.where(z_at == 0, 0.0, 1.0)
    y_low, y_high = (row == 0) & (py == 0), (row == 16) & (py == 7)
    z_low, z_high = (lane == 0) & (pz == 0), (lane == 128) & (pz == 7)

    def face_x(i):
        here, below = bw[i + 1], bw[i]
        inner = jnp.where((px == 0) & (i == 8), here, below)
        outer = jnp.where((px == 3) & (i == 24), below, here)
        cxw[i] = harmonic(outer, inner)

    loop(0, 33, 3, face_x)

    def coefficients(i):
        b = bw[i + 1]
        e_at = jnp.clip(i - 8, 0, 15)
        below = ylo_ref[pl.ds(e_at, 1), :]
        above = yhi_ref[pl.ds(e_at, 1), :]
        below = jnp.concatenate([below, below], axis=1)
        above = jnp.concatenate([above, above], axis=1)
        before = jnp.where(row == 24, jnp.broadcast_to(below, (32, 256)), roll(b, 1, 0))
        cy = harmonic(jnp.where(y_high, before, b), jnp.where(y_low, b, before))
        outer = harmonic(b[16:24], jnp.broadcast_to(above, (8, 256)))
        after = roll(cy, -1, 0)
        after = jnp.concatenate(
            [after[0:16], jnp.where(row[16:24] == 23, outer, after[16:24]), after[24:32]], axis=0
        )
        before = roll(b, 1, 1)
        cz = harmonic(jnp.where(z_high, before, b), jnp.where(z_low, b, before))
        d = cxw[i] + cxw[i + 1] + (cy + after) + (cz + roll(cz, -1, 1))
        x_open = jnp.where(((16 * px + i + 56) & 63) == 0, 0.0, 1.0).astype(F32)
        cx_ref[i] = x_open * cxw[i]
        cy_ref[i] = y_open * cy
        cz_ref[i] = z_open * cz
        cyw[i] = cy
        czw[i] = cz
        inv_ref[i] = 1.0 / d
        dw[i] = d

    loop(0, 32, 4, coefficients)
    for p in range(8):
        i = 8 + 2 * p
        put_lanes(scr, 0, p, 0.25 * cxw[i])
        put_lanes(scr, 1, p, 0.25 * (cyw[i] + cyw[i + 1]))
        put_lanes(scr, 2, p, 0.25 * (czw[i] + czw[i + 1]))
    put_lanes(scr, 3, 0, 0.25 * cxw[24])

    def beyond(i):
        b = bw[i + 1]
        far = jnp.where(py == 0, roll(b, 1, 0)[0:8], b[16:24])
        return harmonic(far, far)

    for p in range(8):
        i = 8 + 2 * p
        far = 0.25 * (beyond(i) + beyond(i + 1))
        scr[3, 0, 32 + 8 * p : 40 + 8 * p, :] = far[:, 0:128]
        scr[3, 1, 32 + 8 * p : 40 + 8 * p, :] = far[:, 128:256]
    fold_lanes(scr, ("x", "y", "z"), xp_ref)
    both, _ = fine_matrices()
    xp_ref[3 * TILES] = exact_dot(folded_rows(scr, 3, 16, True), both)
    far = jnp.concatenate([scr[3, t, pl.ds(32, 8, stride=8), :] for t in range(2)], axis=1)
    xp_ref[3 * TILES + 1, 0:8, :] = exact_dot(far, both)
    xp_ref[3 * TILES + 1, 8:16, :] = jnp.zeros((8, 128), F32)


def fine_down(
    f_ref, zlo_ref, zhi_ref, cx_ref, cy_ref, cz_ref, inv_ref, dw,
    u_far, cx_far, cy_far, cz_far, inv_far, rhs_far, diag_ref, xp_ref,
    u_ref, rhs_ref, va, vb, upd, scr, *sems,
):
    saves = copies_of(
        (cx_ref, cy_ref, cz_ref, inv_ref, rhs_ref, u_ref),
        (cx_far, cy_far, cz_far, inv_far, rhs_far, u_far),
        sems,
    )
    for m in saves[:4]:
        m.start()
    lane1 = iota((32, 128), 1)
    for i in range(32):
        g, at = i // 5, (i % 5) * 24
        right = roll(zhi_ref[g], -at, 1)
        left = roll(zlo_ref[g], 104 - at, 1)
        halo = jnp.where(lane1 < 24, right, jnp.where(lane1 >= 104, left, 0.0))
        for t, part in enumerate((f_ref[i], halo)):
            at = slice(128 * t, 128 * t + 128)
            scaled = part * inv_ref[i, :, at]
            rhs_ref[i, :, at] = scaled
            scaled = FIRST * scaled
            upd[i, :, at] = scaled
            va[i, :, at] = scaled
    saves[4].start()
    level = Level(cx_ref, cy_ref, cz_ref, inv_ref, rhs_ref, 0)
    sweep(level, va, vb, upd, 1, 31, NEAR, *TERMS[0])
    sweep(level, vb, va, upd, 2, 30, NEAR, *TERMS[1])
    sweep(level, va, u_ref, upd, 3, 29, NEAR, *TERMS[2], store_update=False)
    saves[5].start()

    def save_diag(i):
        diag_ref[i] = dw[i + 8, 0:16, 0:128]

    loop(0, 16, 4, save_diag)
    for p in range(8):
        i = 8 + 2 * p
        total = None
        for k in (i, i + 1):
            _, d = level.defect(u_ref, k)
            r = dw[k] * d
            total = r if total is None else total + r
        put_lanes(scr, 0, p, 0.125 * total)
    fold_lanes(scr, ("f",), xp_ref)
    for m in saves:
        m.wait()


TILES = 6


def packy1(x0, x1, x2, x3, up_ref, down_ref):
    low = iota((8, 128), 0) < 4
    xs = (x0, x1, x2, x3)
    tiles = up_ref.shape[0] // 6
    half = 2 * tiles
    for q in range(2 * half):
        own = xs[q // tiles][q % tiles, 0:8, :]
        up_ref[q] = own
        down_ref[q] = own
    for q in range(half):
        one = xs[q // tiles][q % tiles, 8:16, :]
        two = xs[2 + q // tiles][q % tiles, 8:16, :]
        up_ref[2 * half + q] = jnp.where(low, roll(one, 4, 0), two)
        down_ref[2 * half + q] = jnp.where(low, one, roll(two, 4, 0))


def unpack1(xs, lo_ref, hi_ref, k, t, own_face=False):
    row = iota((8, 128), 0)
    tiles = hi_ref.shape[0] // 6
    q, half = k * tiles + t, 2 * tiles
    right, left = hi_ref[2 * half + q % half], lo_ref[2 * half + q % half]
    if q < half:
        edge = jnp.where(row < 4, right, roll(left, 4, 0))
    else:
        edge = jnp.where(row < 4, roll(right, 4, 0), left)
    after = hi_ref[q]
    if own_face:
        after = jnp.where(row == 0, xs[k][t, 8:16, :], after)
    return jnp.concatenate([xs[k][t, 0:8, :], after, edge, lo_ref[q]], axis=0)


def pair_matrices(cut, size_in=128):
    fine = iota((size_in, 128), 0)
    coarse = iota((size_in, 128), 1)
    at = signed(fine, size_in, cut)
    both = jnp.where(((at >> 1) & 127) == coarse, 1.0, 0.0)
    even = jnp.where((((at >> 1) & 127) == coarse) & ((at & 1) == 0), 1.0, 0.0)
    return both, even


def restrict(scr, both, even, count, arrays=5):
    out = []
    for a in range(arrays):
        folded = scr[a, pl.ds(0, count, stride=2), :]
        if a != 2:
            folded = folded + scr[a, pl.ds(1, count, stride=2), :]
        out.append(exact_dot(folded, even if a == 3 else both))
    return out


def mid_down(
    c0, c1, c2, c3, clo_ref, chi_ref, f0, f1, f2, f3, flo_ref, fhi_ref,
    u_far, cx_far, cy_far, cz_far, inv_far, rhs_far, own_ref, ym_ref, yp_ref,
    u_ref, cx_ref, cy_ref, cz_ref, inv_ref, rhs_ref,
    va, vb, upd, dw, ux, uy, uz, hx, oth, scr, *sems,
):
    saves = copies_of(
        (cx_ref, cy_ref, cz_ref, inv_ref, rhs_ref, u_ref),
        (cx_far, cy_far, cz_far, inv_far, rhs_far, u_far),
        sems,
    )
    lane = iota((32, 128), 1)
    px, py, pz = lax.axis_index("gx"), lax.axis_index("gy"), lax.axis_index("gz")
    row = iota((32, 128), 0)
    coarse = ((c0, c1, c2, c3), clo_ref, chi_ref)
    pieces = [(ux, 0.0) + coarse + (0,), (uy, 0.0) + coarse + (1,), (uz, 1.0) + coarse + (2,)]
    pieces += [(va, 0.0, (f0, f1, f2, f3), flo_ref, fhi_ref, 0)]
    for target, fill, xs, lo_ref, hi_ref, a in pieces:
        face = target is uy
        for k in range(4):
            sides = [
                unpack1(xs, lo_ref, hi_ref, k, TILES * a + 4 + g, face) for g in range(2)
            ]
            for j in range(4):
                base = unpack1(xs, lo_ref, hi_ref, k, TILES * a + j, face)
                for g in range(2):
                    own = roll(base, 64, 1) if g else base
                    right = roll(sides[g], 64 - 32 * j, 1)
                    left = roll(sides[g], 96 - 32 * j, 1)
                    halo = jnp.where(lane < 80, right, jnp.where(lane >= 112, left, fill))
                    target[8 * k + 4 * g + j] = jnp.where(lane < 64, own, halo)
    high_x = None
    for k in range(4):
        part = unpack1(coarse[0], clo_ref, chi_ref, k, 3 * TILES)
        high_x = part if high_x is None else jnp.where(px == 3 - k, part, high_x)
    hx[...] = high_x
    for k in range(4):
        oth[8 * k : 8 * k + 8, :] = coarse[0][k][3 * TILES + 1, 0:8, :]
    y_open = jnp.where(((8 * py + signed(row, 32, 20)) & 63) == 0, 0.0, 1.0)
    z_open = jnp.where(((64 * pz + signed(lane, 128, 96)) & 511) == 0, 0.0, 1.0)

    def coefficients(i):
        x_at = (8 * px + i) & 31
        cx, cy, cz = ux[i], uy[i], uz[i]
        above = jnp.where(x_at == 31, hx[...], ux[(i + 1) & 31])
        other = jnp.broadcast_to(oth[pl.ds(i, 1), :], (32, 128))
        here = jnp.where((row == 8) & (py == 7), other, cy)
        after = jnp.where((row == 31) & (py == 0), other, roll(cy, -1, 0))
        d = cx + above + (here + after) + (cz + roll(cz, -1, 1))
        cx_ref[i] = jnp.where(x_at == 0, 0.0, 1.0).astype(F32) * cx
        cy_ref[i] = y_open * cy
        cz_ref[i] = z_open * cz
        inv = 1.0 / d
        inv_ref[i] = inv
        dw[i] = d
        g = 4.0 * va[i] * inv
        rhs_ref[i] = g
        first = FIRST * g
        upd[i] = first
        va[i] = first

    loop(0, 32, 8, coefficients)
    for m in saves[:5]:
        m.start()
    level = Level(cx_ref, cy_ref, cz_ref, inv_ref, rhs_ref, 32)
    sweep(level, va, vb, upd, 0, 32, FULL, *TERMS[0])
    sweep(level, vb, va, upd, 0, 32, FULL, *TERMS[1])
    sweep(level, va, u_ref, upd, 0, 32, FULL, *TERMS[2], store_update=False)
    saves[5].start()
    for p in range(16):
        i = 2 * p
        _, d0 = level.defect(u_ref, i)
        _, d1 = level.defect(u_ref, i + 1)
        at = slice(32 * p, 32 * p + 32)
        scr[0, at, :] = 0.03125 * (dw[i] * d0 + dw[i + 1] * d1)
        scr[1, at, :] = 0.25 * ux[i]
        scr[2, at, :] = 0.25 * (uy[i] + uy[i + 1])
        scr[3, at, :] = 0.25 * (uz[i] + uz[i + 1])
    scr[4, 0:32, :] = 0.25 * hx[...]
    both, even = pair_matrices(96)
    f, cx, cy, cz = [r.reshape(16, 16, 128) for r in restrict(scr, both, even, 256, 4)]
    high_x = exact_dot(scr[4, pl.ds(0, 16, stride=2), :] + scr[4, pl.ds(1, 16, stride=2), :], both)
    y_open = jnp.where(((4 * py + signed(row[:16], 16, 10)) & 31) == 0, 0.0, 1.0)
    z_open = jnp.where(((32 * pz + signed(lane[:16], 128, 96)) & 255) == 0, 0.0, 1.0)
    others = exact_dot(oth[pl.ds(0, 16, stride=2), :] + oth[pl.ds(1, 16, stride=2), :], both)
    planes = []
    for p in range(16):
        x_at = (4 * px + p) & 15
        other = jnp.broadcast_to(0.25 * others[p : p + 1], (16, 128))
        here = jnp.where((row[:16] == 4) & (py == 7), other, cy[p])
        after = jnp.where((row[:16] == 15) & (py == 0), other, roll(cy[p], -1, 0))
        above = jnp.where(x_at == 15, high_x, cx[(p + 1) % 16])
        d = cx[p] + above + (here + after) + (cz[p] + roll(cz[p], -1, 1))
        x_open = jnp.where(x_at == 0, 0.0, 1.0).astype(F32)
        planes.append((f[p], x_open * cx[p], y_open * cy[p], z_open * cz[p], d))
    lane8 = iota((16, 128), 1)
    row8 = iota((8, 128), 0)
    for a in range(5):
        for j in range(4):
            packed = planes[j][a]
            for k in range(1, 4):
                packed = jnp.where(lane8 >= 32 * k, roll(planes[4 * k + j][a], 32 * k, 1), packed)
            own_ref[a, j] = packed
            ym_ref[a, j] = jnp.where(row8 == 7, packed[8:16], packed[0:8])
            yp_ref[a, j] = jnp.where(row8 < 5, packed[0:8], packed[8:16])
    for m in saves:
        m.wait()


def pack2(own_ref, hi_ref, far_ref, lo_ref, up_ref, down_ref, w_ref):
    row = iota((8, 128), 0)
    for a in range(5):
        for j in range(4):
            hi, far, lo = hi_ref[a, j], far_ref[a, j], lo_ref[a, j]
            w_ref[a, j, 0:8, :] = jnp.where(row == 7, hi, own_ref[a, j, 0:8, :])
            w_ref[a, j, 8:16, :] = jnp.where(row == 7, far, hi)
            w_ref[a, j, 16:24, :] = jnp.where(row < 5, far, lo)
            w_ref[a, j, 24:32, :] = jnp.where(row < 5, lo, own_ref[a, j, 8:16, :])

    def get(p):
        return w_ref[p // 16, p % 4], 32 * (p % 16 // 4)

    ups, downs = z_pack(get, 80, 32, (21, 0), 11, 11)
    for g in range(8):
        up_ref[g] = ups[g]
        down_ref[g] = downs[g]


def low_down(
    w_ref, zlo_ref, zhi_ref,
    u_far, cx_far, cy_far, cz_far, inv_far, rhs_far, own_ref,
    u_ref, cx_ref, cy_ref, cz_ref, inv_ref, rhs_ref,
    va, vb, upd, dw, scr, *sems,
):
    saves = copies_of(
        (cx_ref, cy_ref, cz_ref, inv_ref, rhs_ref, u_ref),
        (cx_far, cy_far, cz_far, inv_far, rhs_far, u_far),
        sems,
    )
    lane = iota((32, 128), 1)
    targets = (va, cx_ref, cy_ref, cz_ref, dw)
    for a in range(5):
        fill = 1.0 if a == 4 else 0.0
        for p in range(16):
            base = roll(w_ref[a, p % 4], -32 * (p // 4), 1)
            g, at = (16 * a + p) // 11, (16 * a + p) % 11 * 11
            right = roll(zhi_ref[g], 32 - at, 1)
            left = roll(zlo_ref[g], 117 - at, 1)
            halo = jnp.where(lane < 43, right, jnp.where(lane >= 117, left, fill))
            targets[a][p] = jnp.where(lane < 32, base, halo)

    def coefficients(i):
        inv = 1.0 / dw[i]
        inv_ref[i] = inv
        g = 16.0 * va[i] * inv
        rhs_ref[i] = g
        first = FIRST * g
        upd[i] = first
        va[i] = first

    loop(0, 16, 8, coefficients)
    for m in saves[:5]:
        m.start()
    level = Level(cx_ref, cy_ref, cz_ref, inv_ref, rhs_ref, 16)
    sweep(level, va, vb, upd, 0, 16, FULL, *TERMS[0])
    sweep(level, vb, va, upd, 0, 16, FULL, *TERMS[1])
    sweep(level, va, u_ref, upd, 0, 16, FULL, *TERMS[2], store_update=False)
    saves[5].start()

    def edge(i):
        above = (i + 1) & 15
        cy, cz = cy_ref[i], cz_ref[i]
        inner = cx_ref[i] + cx_ref[above] + (cy + roll(cy, -1, 0)) + (cz + roll(cz, -1, 1))
        return dw[i] - inner

    for p in range(8):
        i = 2 * p
        _, d0 = level.defect(u_ref, i)
        _, d1 = level.defect(u_ref, i + 1)
        at = slice(32 * p, 32 * p + 32)
        scr[0, at, :] = 0.0078125 * (dw[i] * d0 + dw[i + 1] * d1)
        scr[1, at, :] = 0.25 * cx_ref[i]
        scr[2, at, :] = 0.25 * (cy_ref[i] + cy_ref[i + 1])
        scr[3, at, :] = 0.25 * (cz_ref[i] + cz_ref[i + 1])
        scr[4, at, :] = 0.25 * (edge(i) + edge(i + 1))
    both, even = pair_matrices(96)
    f, cx, cy, cz, e = [r.reshape(8, 16, 128) for r in restrict(scr, both, even, 128)]
    planes = []
    for p in range(8):
        inner = cx[p] + cx[(p + 1) % 8] + (cy[p] + roll(cy[p], -1, 0))
        d = inner + (cz[p] + roll(cz[p], -1, 1)) + e[p]
        planes.append((f[p], cx[p], cy[p], cz[p], d))
    lane16 = iota((16, 128), 1)
    for a in range(5):
        packed = planes[0][a]
        for p in range(1, 8):
            packed = jnp.where(lane16 >= 16 * p, roll(planes[p][a], 16 * p, 1), packed)
        own_ref[a] = packed
    for m in saves:
        m.wait()


def spread(dup, w, rows, matrix):
    count = w.shape[0]
    dup[pl.ds(0, count, stride=2), :] = w
    dup[pl.ds(1, count, stride=2), :] = w
    return exact_dot(dup[0 : 2 * count, :], matrix)


def spread_matrix(cut, size):
    coarse = iota((128, size), 0)
    at = signed(iota((128, size), 1), size, cut)
    return jnp.where(((at >> 1) & 127) == coarse, 1.0, 0.0)


def post(level, va, vb, upd, ranges, unroll):
    lo, hi = ranges[0]
    sweep(level, va, vb, upd, lo, hi, unroll, None, FIRST)
    src, dst = vb, va
    for n in range(3):
        lo, hi = ranges[n + 1]
        sweep(level, src, dst, upd, lo, hi, unroll, *TERMS[n], store_update=n < 2)
        src, dst = dst, src


def up(
    g_ref, *refs,
):
    fars, refs = refs[:19], refs[19:]
    (sol_far, res_far), refs = refs[:2], refs[2:]
    (l3, inv3, rhs3, u3, va3, vb3, upd3, scr3), refs = refs[:8], refs[8:]
    (va2, vb2, upd2, dup2, va1, vb1, upd1, dup1, va0, vb0, upd0, dup0), refs = refs[:12], refs[12:]
    nears, (sol_ref, res_ref), sems = refs[:19], refs[19:21], refs[21:]
    u2, cx2, cy2, cz2, inv2, rhs2 = nears[:6]
    u1, cx1, cy1, cz1, inv1, rhs1 = nears[6:12]
    u0, cx0, cy0, cz0, inv0, rhs0, diag0 = nears[12:]
    loads = copies_of(fars, nears, sems)
    for m in loads:
        m.start()
    me = lax.axis_index("gz")
    lane = iota((16, 128), 1)
    for a in range(5):
        tiles = [g_ref[(me + k) & 7, a] for k in range(8)]
        for p in range(8):
            plane = roll(tiles[0], -16 * p, 1)
            for k in range(1, 8):
                plane = jnp.where(lane >= 16 * k, roll(tiles[k], 16 * (k - p), 1), plane)
            l3[a, p] = plane
    f3, cx3, cy3, cz3, d3 = [l3.at[a] for a in range(5)]
    level = Level(cx3, cy3, cz3, inv3, rhs3, 8)

    def start3(i):
        inv = 1.0 / d3[i]
        inv3[i] = inv
        g = 64.0 * f3[i] * inv
        rhs3[i] = g
        first = FIRST * g
        upd3[i] = first
        va3[i] = first

    loop(0, 8, 8, start3)
    sweep(level, va3, vb3, upd3, 0, 8, 8, *TERMS[0])
    sweep(level, vb3, va3, upd3, 0, 8, 8, *TERMS[1])
    sweep(level, va3, u3, upd3, 0, 8, 8, *TERMS[2], store_update=False)
    for p in range(4):
        i = 2 * p
        _, r0 = level.defect(u3, i)
        _, r1 = level.defect(u3, i + 1)
        at = slice(16 * p, 16 * p + 16)
        scr3[0, at, :] = (0.125 / 64.0) * (d3[i] * r0 + d3[i + 1] * r1)
        scr3[1, at, :] = 0.25 * cx3[i]
        scr3[2, at, :] = 0.25 * (cy3[i] + cy3[i + 1])
        scr3[3, at, :] = 0.25 * (cz3[i] + cz3[i + 1])
        total = None
        for k in (i, i + 1):
            cy, cz = cy3[k], cz3[k]
            inner = cx3[k] + cx3[(k + 1) % 8] + (cy + roll(cy, -1, 0))
            inner = inner + (cz + roll(cz, -1, 1))
            total = d3[k] - inner if total is None else total + (d3[k] - inner)
        scr3[4, at, :] = 0.25 * total
    fine = iota((128, 128), 0)
    coarse = iota((128, 128), 1) & 63
    both = jnp.where((fine >> 1) == coarse, 1.0, 0.0)
    even = jnp.where(fine == 2 * coarse, 1.0, 0.0)
    f, cx, cy, cz, e = restrict(scr3, both, even, 32)

    def cut(a, p):
        return a[8 * p : 8 * p + 8]

    fs, cxs, cys, czs = [[cut(a, p) for p in range(4)] for a in (f, cx, cy, cz)]
    invs, gs, vs, es = [], [], [], []
    for p in range(4):
        d = cxs[p] + cxs[(p + 1) % 4] + (cys[p] + roll(cys[p], -1, 0))
        d = d + (czs[p] + roll(czs[p], -1, 1)) + cut(e, p)
        invs.append(1.0 / d)
        gs.append(256.0 * fs[p] * invs[p])
        es.append(CFIRST * gs[p])
        vs.append(es[p])
    xlo = [invs[p] * cxs[p] for p in range(4)]
    xhi = [invs[p] * cxs[(p + 1) % 4] for p in range(4)]
    ylo = [invs[p] * cys[p] for p in range(4)]
    yhi = [invs[p] * roll(cys[p], -1, 0) for p in range(4)]
    zlo = [invs[p] * czs[p] for p in range(4)]
    zhi = [invs[p] * roll(czs[p], -1, 1) for p in range(4)]
    for momentum, push in CTERMS:
        momentum, push = float(np.float32(momentum)), float(np.float32(push))
        new_v, new_e = [], []
        for p in range(4):
            v = vs[p]
            total = xlo[p] * vs[(p + 3) % 4] + xhi[p] * vs[(p + 1) % 4]
            total = total + (ylo[p] * roll(v, 1, 0) + yhi[p] * roll(v, -1, 0))
            total = total + (zlo[p] * roll(v, 1, 1) + zhi[p] * roll(v, -1, 1))
            ne = momentum * es[p] + push * ((gs[p] - v) + total)
            new_e.append(ne)
            new_v.append(v + ne)
        vs, es = new_v, new_e
    w4 = jnp.concatenate(vs, axis=0)
    fine = iota((128, 128), 1)
    coarse = iota((128, 128), 0)
    m = jnp.where((fine >> 1) == coarse, 1.0, 0.0)
    wide = spread(dup2, w4, 8, m)
    for i in range(8):
        p = i // 2
        va3[i] = u3[i] + wide[16 * p : 16 * p + 16]
    post(level, va3, vb3, upd3, [(0, 8)] * 4, 8)
    for m in loads[:6]:
        m.wait()
    w3 = va3[...].reshape(128, 128)
    wide = spread(dup2, w3, 16, spread_matrix(96, 128))
    for i in range(16):
        p = i // 2
        va2[i] = u2[i] + wide[32 * p : 32 * p + 32]
    level = Level(cx2, cy2, cz2, inv2, rhs2, 16)
    post(level, va2, vb2, upd2, [(0, 16)] * 4, FULL)
    for m in loads[6:12]:
        m.wait()
    w2 = jnp.concatenate([va2[:, 0:8, :], va2[:, 24:32, :]], axis=1).reshape(256, 128)
    wide = spread(dup1, w2, 16, spread_matrix(96, 128))
    for i in range(32):
        p = i // 2
        va1[i] = u1[i] + wide[32 * p : 32 * p + 32]
    level = Level(cx1, cy1, cz1, inv1, rhs1, 32)
    post(level, va1, vb1, upd1, [(0, 32)] * 4, FULL)
    for m in loads[12:]:
        m.wait()
    rows = [
        jnp.concatenate([va1[i % 32, 0:8, :], mix_rows(va1, i % 32)], axis=0) for i in range(-4, 12)
    ]
    w1 = jnp.concatenate(rows, axis=0)
    wide = spread(dup0, w1, 16, spread_matrix(192, 256))
    for i in range(3, 29):
        p = i // 2
        va0[i] = u0[i] + wide[32 * p : 32 * p + 32]
    level = Level(cx0, cy0, cz0, inv0, rhs0, 0)
    post(level, va0, vb0, upd0, [(4, 28), (5, 27), (6, 26), (7, 25)], NEAR)

    for i in range(16):
        sol_ref[i] = va0[i + 8, 0:16, 0:128]
    ends = copies_of((sol_ref, res_ref), (sol_far, res_far), sems[19:])
    ends[0].start()

    def finish(i):
        _, d = level.defect(va0, i)
        res_ref[i - 8] = diag0[i - 8] * d[0:16, 0:128]

    loop(8, 24, 16, finish)
    ends[1].start()
    for m in ends:
        m.wait()


def mix_rows(ref, i):
    low = iota((8, 128), 0) < 4
    return jnp.where(low, ref[i, 8:16, :], ref[i, 24:32, :])


def call(body, args, outs, scratch=(), limit=16, far_in=(), far_out=(), copies=0, us=1):
    near, far = pl.BlockSpec(memory_space=pltpu.VMEM), pl.BlockSpec(memory_space=pltpu.HBM)
    return pl.pallas_call(
        body,
        out_shape=[jax.ShapeDtypeStruct(s, F32) for s in outs],
        in_specs=[far if i in far_in else near for i in range(len(args))],
        out_specs=[far if i in far_out else near for i in range(len(outs))],
        scratch_shapes=[pltpu.VMEM(s, F32) for s in scratch]
        + [pltpu.SemaphoreType.DMA] * copies,
        compiler_params=pltpu.CompilerParams(vmem_limit_bytes=limit * MIB),
        name=body.__name__,
        cost_estimate=pl.CostEstimate(
            flops=0, bytes_accessed=us * 3_000_000, transcendentals=0
        ),
    )(*args)


def move(values, axis, shift):
    size = lax.axis_size(axis)
    return lax.ppermute(values, axis, [((i + shift) % size, i) for i in range(size)])


def local(source, conductivity):
    f, b = source, conductivity
    ends = lax.optimization_barrier(jnp.concatenate([f[8:16], b[7:16], f[0:8], b[0:9]]))
    to_hi, to_lo = ends[:17], ends[17:]
    xs = [move(to_hi, "gx", -1), move(to_lo, "gx", 1)]
    to_hi, to_lo = call(packy0, [f, b] + xs, [(66, 8, 128)] * 2)
    ys = [move(to_hi, "gy", -1), move(to_lo, "gy", 1)]
    to_hi, to_lo, bw = call(
        pack0b, [b] + xs + ys, [(7, 32, 128)] * 2 + [(34, 32, 128)]
    )
    zb = [move(to_hi, "gz", -1), move(to_lo, "gz", 1)]
    to_hi, to_lo, fw = call(
        pack0f, [f] + xs + ys, [(7, 32, 128)] * 2 + [(32, 32, 128)]
    )
    zf = [move(to_hi, "gz", -1), move(to_lo, "gz", 1)]
    big = (32, 32, 256)
    cx0, cy0, cz0, inv0, d0, xpc = call(
        fine_coef,
        [bw] + [e[64:].reshape(16, 128) for e in ys] + zb,
        [big] * 5 + [(3 * TILES + 2, 16, 128)],
        [(34, 32, 256), big, big, (33, 32, 256), (4, 2, 256, 128)],
        24,
        us=20,
    )
    xpc, zf = lax.optimization_barrier((xpc, zf))
    u0, cx0, cy0, cz0, inv0, rhs0, diag0, xpf = call(
        fine_down,
        [fw] + zf + [cx0, cy0, cz0, inv0, d0],
        [big] * 6 + [(16, 16, 128), (TILES, 16, 128)],
        [big] * 5 + [(1, 2, 256, 128)],
        24,
        far_out=range(6),
        copies=6,
        us=20,
    )

    def along_x(xp):
        return [xp] + [move(xp, "gx", k) for k in (1, 2, 3)]

    def along_y(xs, tiles, us):
        to_hi, to_lo = call(packy1, xs, [(6 * tiles, 8, 128)] * 2, us=us)
        return xs + [move(to_hi, "gy", -1), move(to_lo, "gy", 1)]

    coarse, xpf = lax.optimization_barrier((along_x(xpc), xpf))
    coarse, right_side = along_y(coarse, 3 * TILES + 1, 20), along_y(along_x(xpf), TILES, 1)
    mid = (32, 32, 128)
    u1, cx1, cy1, cz1, inv1, rhs1, own2, ym, yp = call(
        mid_down,
        coarse + right_side,
        [mid] * 6 + [(5, 4, 16, 128), (5, 4, 8, 128), (5, 4, 8, 128)],
        [mid] * 13 + [(32, 128), (32, 128), (5, 512, 128)],
        far_out=range(6),
        copies=6,
    )
    from_hi, from_lo, far = move(ym, "gy", 2), move(yp, "gy", -2), move(ym, "gy", 4)
    up2, down2, w2 = call(
        pack2, (own2, from_hi, far, from_lo), [(8, 32, 128)] * 2 + [(5, 4, 32, 128)]
    )
    zlo, zhi = move(up2, "gz", -1), move(down2, "gz", 1)
    low = (16, 32, 128)
    u2, cx2, cy2, cz2, inv2, rhs2, own3 = call(
        low_down,
        (w2, zlo, zhi),
        [low] * 6 + [(5, 16, 128)],
        [low] * 10 + [(5, 256, 128)],
        far_out=range(6),
        copies=6,
    )
    everyone = jnp.broadcast_to(own3[None], (8, 5, 16, 128))
    gathered = lax.all_to_all(everyone, "gz", 0, 0)
    tiny = (8, 16, 128)
    return tuple(
        call(
            up,
            (
                gathered,
                u2, cx2, cy2, cz2, inv2, rhs2,
                u1, cx1, cy1, cz1, inv1, rhs1,
                u0, cx0, cy0, cz0, inv0, rhs0, diag0,
            ),
            [(16, 16, 128)] * 2,
            [(5,) + tiny] + [tiny] * 6 + [(5, 64, 128)]
            + [low] * 3 + [(256, 128)] + [mid] * 3 + [(512, 128)] + [big] * 3 + [(512, 128)]
            + [low] * 6 + [mid] * 6 + [big] * 6 + [(16, 16, 128)] * 3,
            28,
            far_in=range(1, 20),
            far_out=(0, 1),
            copies=21,
        )
    )


def solution(mesh):
    spec = P("gx", "gy", "gz")
    return jax.shard_map(
        local, mesh=mesh, in_specs=(spec, spec), out_specs=(spec, spec), check_vma=False
    )
```

```python
import functools

import jax
import jax.numpy as jnp
import numpy as np
from jax import lax
from jax.experimental import pallas as pl
from jax.experimental.pallas import tpu as pltpu
from jax.sharding import PartitionSpec as P

F32 = jnp.float32
CSWEEPS = 32
MIB = 1024 * 1024
NEAR, FULL = 16, 32


def chebyshev_terms(sweep_count, lower_bound, upper_bound):
    center = (upper_bound + lower_bound) / 2.0
    half_width = (upper_bound - lower_bound) / 2.0
    sigma_ratio = center / half_width
    rho_now = 1.0 / sigma_ratio
    terms = []
    for _ in range(sweep_count - 1):
        rho_next = 1.0 / (2.0 * sigma_ratio - rho_now)
        terms.append((rho_next * rho_now, 2.0 * rho_next / half_width))
        rho_now = rho_next
    return 1.0 / center, terms


FIRST, TERMS = chebyshev_terms(4, 0.6, 2.0)
CFIRST, CTERMS = chebyshev_terms(CSWEEPS, 0.05, 2.0)


def harmonic(a, b):
    return 2.0 * a * b / (a + b)


def roll(a, shift, axis):
    return pltpu.roll(a, shift % a.shape[axis], axis)


def iota(shape, dim):
    return lax.broadcasted_iota(jnp.int32, shape, dim)


def exact_dot(a, m):
    m = m.astype(jnp.bfloat16)
    high = a.astype(jnp.bfloat16)
    rest = a - high.astype(F32)
    mid = rest.astype(jnp.bfloat16)
    low = (rest - mid.astype(F32)).astype(jnp.bfloat16)
    parts = [jnp.dot(p, m, preferred_element_type=F32) for p in (high, mid, low)]
    return parts[0] + (parts[1] + parts[2])


def signed(index, size, cut):
    return jnp.where(index < cut, index, index - size)


def loop(lo, hi, unroll, body):
    rounds = (hi - lo) // unroll

    def step(t, carry):
        for u in range(unroll):
            body(lo + t * unroll + u)
        return carry

    if rounds:
        lax.fori_loop(0, rounds, step, 0)
    for i in range(lo + rounds * unroll, hi):
        body(i)


def copies_of(sources, targets, sems):
    return [pltpu.make_async_copy(a, b, s) for a, b, s in zip(sources, targets, sems)]


class Level:
    def __init__(self, cx, cy, cz, inv, rhs, wrap):
        self.cx, self.cy, self.cz, self.inv, self.rhs, self.wrap = cx, cy, cz, inv, rhs, wrap

    def around(self, i):
        if self.wrap:
            return (i + self.wrap - 1) & (self.wrap - 1), (i + 1) & (self.wrap - 1)
        return i - 1, i + 1

    def defect(self, v, i):
        below, above = self.around(i)
        here = v[i]
        cy, cz = self.cy[i], self.cz[i]
        total = self.cx[i] * v[below] + self.cx[above] * v[above]
        total = total + (cy * roll(here, 1, 0) + roll(cy * here, -1, 0))
        total = total + (cz * roll(here, 1, 1) + roll(cz * here, -1, 1))
        return here, self.rhs[i] - here + self.inv[i] * total


def sweep(level, src, dst, upd, lo, hi, unroll, momentum, push, store_update=True):
    def body(i):
        here, d = level.defect(src, i)
        e = push * d
        if momentum is not None:
            e = momentum * upd[i] + e
        if store_update:
            upd[i] = e
        dst[i] = here + e

    loop(lo, hi, unroll, body)


def z_pack(get, planes, rows, starts, width, per):
    lane = iota((rows, 128), 1)
    out = []
    for start in starts:
        tiles = []
        for g in range(0, planes, per):
            acc = jnp.zeros((rows, 128), F32)
            for p in range(g, min(g + per, planes)):
                plane, base = get(p)
                at = (p - g) * width
                moved = roll(plane, at - start - base, 1)
                acc = jnp.where((lane >= at) & (lane < at + width), moved, acc)
            tiles.append(acc)
        out.append(tiles)
    return out


def x_plane(own_ref, lo_ref, hi_ref, first, width, p):
    if p < width:
        return lo_ref, first + p
    if p < width + 16:
        return own_ref, p - width
    return hi_ref, first + p - width - 16


def f_plane(f_ref, lo_ref, hi_ref, p):
    return x_plane(f_ref, lo_ref, hi_ref, 0, 8, p)


def b_plane(b_ref, lo_ref, hi_ref, p):
    return x_plane(b_ref, lo_ref, hi_ref, 8, 9, p)


def packy0(f_ref, b_ref, lo_ref, hi_ref, up_ref, down_ref):
    for p in range(32):
        for at, (ref, q) in (
            (p, f_plane(f_ref, lo_ref, hi_ref, p)),
            (32 + p, b_plane(b_ref, lo_ref, hi_ref, p + 1)),
        ):
            up_ref[at] = ref[q, 8:16, :]
            down_ref[at] = ref[q, 0:8, :]
    row = iota((8, 128), 0)
    for ref, edge in ((up_ref, 7), (down_ref, 8)):
        for t in range(2):
            acc = jnp.zeros((8, 128), F32)
            for r in range(8):
                line = jnp.broadcast_to(b_ref[8 * t + r, edge : edge + 1, :], (8, 128))
                acc = jnp.where(row == r, line, acc)
            ref[64 + t] = acc


def pack0b(b_ref, xlo_ref, xhi_ref, ylo_ref, yhi_ref, up_ref, down_ref, w_ref):
    for p in range(34):
        ref, q = b_plane(b_ref, xlo_ref, xhi_ref, p)
        w_ref[p, 0:16, :] = ref[q]
        if 0 < p < 33:
            w_ref[p, 16:24, :] = yhi_ref[31 + p]
            w_ref[p, 24:32, :] = ylo_ref[31 + p]
        else:
            w_ref[p, 16:32, :] = ref[q]
    ups, downs = z_pack(lambda p: (w_ref[p + 1], 0), 32, 32, (103, 0), 25, 5)
    for g in range(7):
        up_ref[g] = ups[g]
        down_ref[g] = downs[g]


def pack0f(f_ref, xlo_ref, xhi_ref, ylo_ref, yhi_ref, up_ref, down_ref, w_ref):
    for p in range(32):
        ref, q = f_plane(f_ref, xlo_ref, xhi_ref, p)
        w_ref[p, 0:16, :] = ref[q]
        w_ref[p, 16:24, :] = yhi_ref[p]
        w_ref[p, 24:32, :] = ylo_ref[p]
    ups, downs = z_pack(lambda p: (w_ref[p], 0), 32, 32, (104, 0), 24, 5)
    for g in range(7):
        up_ref[g] = ups[g]
        down_ref[g] = downs[g]


def fine_matrices():
    fine_lane = iota((256, 128), 0)
    coarse_lane = iota((256, 128), 1)
    both = jnp.where((fine_lane >> 1) == coarse_lane, 1.0, 0.0)
    even = jnp.where(fine_lane == 2 * coarse_lane, 1.0, 0.0)
    return both, even


def folded_rows(scr, a, count, pairs):
    def rows_of(offset):
        return jnp.concatenate(
            [scr[a, t, pl.ds(offset, count, stride=2), :] for t in range(2)], axis=1
        )

    return rows_of(0) + rows_of(1) if pairs else rows_of(0)


def fold_lanes(scr, slots, xp_ref):
    both, even = fine_matrices()
    lane = iota((8, 128), 1)
    half = lane < 64
    for a, kind in enumerate(slots):
        res = exact_dot(folded_rows(scr, a, 128, kind != "y"), even if kind == "z" else both)
        for t in range(2):
            rows = slice(t * 8, t * 8 + 8)
            for j in range(4):
                lo = res[j * 16 + t * 8 : j * 16 + t * 8 + 8]
                hi = res[(j + 4) * 16 + t * 8 : (j + 4) * 16 + t * 8 + 8]
                xp_ref[a * TILES + j, rows, :] = jnp.where(half, lo, roll(hi, 64, 1))
            for g in range(2):
                acc = None
                for q in range(4):
                    at = (4 * g + q) * 16 + t * 8
                    plane = res[at : at + 8]
                    part = jnp.where(lane < 80, plane, roll(plane, -32, 1))
                    part = roll(part, 32 * q - 64, 1)
                    acc = part if acc is None else jnp.where(lane >= 32 * q, part, acc)
                xp_ref[a * TILES + 4 + g, rows, :] = acc


def put_lanes(scr, a, p, value):
    scr[a, 0, p * 32 : p * 32 + 32, :] = value[:, 0:128]
    scr[a, 1, p * 32 : p * 32 + 32, :] = value[:, 128:256]


def fine_coef(
    b_ref, ylo_ref, yhi_ref, zlo_ref, zhi_ref,
    cx_ref, cy_ref, cz_ref, inv_ref, dw, xp_ref,
    bw, cyw, czw, cxw, scr,
):
    px, py, pz = lax.axis_index("gx"), lax.axis_index("gy"), lax.axis_index("gz")
    lane1 = iota((32, 128), 1)
    lane = iota((32, 256), 1)
    row = iota((32, 256), 0)
    for i in range(34):
        q = min(max(i - 1, 0), 31)
        g, at = q // 5, (q % 5) * 25
        right = roll(zhi_ref[g], -at, 1)
        left = roll(zlo_ref[g], 103 - at, 1)
        bw[i, :, 0:128] = b_ref[i]
        bw[i, :, 128:256] = jnp.where(lane1 < 25, right, jnp.where(lane1 >= 103, left, 1.0))
    y_at = (16 * py + signed(row, 32, 24)) & 127
    z_at = (128 * pz + signed(lane, 256, 192)) & 1023
    y_open = jnp.where(y_at == 0, 0.0, 1.0)
    z_open = jnp.where(z_at == 0, 0.0, 1.0)
    y_low, y_high = (row == 0) & (py == 0), (row == 16) & (py == 7)
    z_low, z_high = (lane == 0) & (pz == 0), (lane == 128) & (pz == 7)

    def face_x(i):
        here, below = bw[i + 1], bw[i]
        inner = jnp.where((px == 0) & (i == 8), here, below)
        outer = jnp.where((px == 3) & (i == 24), below, here)
        cxw[i] = harmonic(outer, inner)

    loop(0, 33, 11, face_x)

    def coefficients(i):
        b = bw[i + 1]
        e_at = jnp.clip(i - 8, 0, 15)
        below = ylo_ref[pl.ds(e_at, 1), :]
        above = yhi_ref[pl.ds(e_at, 1), :]
        below = jnp.concatenate([below, below], axis=1)
        above = jnp.concatenate([above, above], axis=1)
        before = jnp.where(row == 24, jnp.broadcast_to(below, (32, 256)), roll(b, 1, 0))
        cy = harmonic(jnp.where(y_high, before, b), jnp.where(y_low, b, before))
        outer = harmonic(b[16:24], jnp.broadcast_to(above, (8, 256)))
        after = roll(cy, -1, 0)
        after = jnp.concatenate(
            [after[0:16], jnp.where(row[16:24] == 23, outer, after[16:24]), after[24:32]], axis=0
        )
        before = roll(b, 1, 1)
        cz = harmonic(jnp.where(z_high, before, b), jnp.where(z_low, b, before))
        d = cxw[i] + cxw[i + 1] + (cy + after) + (cz + roll(cz, -1, 1))
        x_open = jnp.where(((16 * px + i + 56) & 63) == 0, 0.0, 1.0).astype(F32)
        cx_ref[i] = x_open * cxw[i]
        cy_ref[i] = y_open * cy
        cz_ref[i] = z_open * cz
        cyw[i] = cy
        czw[i] = cz
        inv_ref[i] = 1.0 / d
        dw[i] = d

    loop(0, 32, 8, coefficients)
    for p in range(8):
        i = 8 + 2 * p
        put_lanes(scr, 0, p, 0.25 * cxw[i])
        put_lanes(scr, 1, p, 0.25 * (cyw[i] + cyw[i + 1]))
        put_lanes(scr, 2, p, 0.25 * (czw[i] + czw[i + 1]))
    put_lanes(scr, 3, 0, 0.25 * cxw[24])

    def beyond(i):
        b = bw[i + 1]
        far = jnp.where(py == 0, roll(b, 1, 0)[0:8], b[16:24])
        return harmonic(far, far)

    for p in range(8):
        i = 8 + 2 * p
        far = 0.25 * (beyond(i) + beyond(i + 1))
        scr[3, 0, 32 + 8 * p : 40 + 8 * p, :] = far[:, 0:128]
        scr[3, 1, 32 + 8 * p : 40 + 8 * p, :] = far[:, 128:256]
    fold_lanes(scr, ("x", "y", "z"), xp_ref)
    both, _ = fine_matrices()
    xp_ref[3 * TILES] = exact_dot(folded_rows(scr, 3, 16, True), both)
    far = jnp.concatenate([scr[3, t, pl.ds(32, 8, stride=8), :] for t in range(2)], axis=1)
    xp_ref[3 * TILES + 1, 0:8, :] = exact_dot(far, both)
    xp_ref[3 * TILES + 1, 8:16, :] = jnp.zeros((8, 128), F32)


def fine_down(
    f_ref, zlo_ref, zhi_ref, cx_ref, cy_ref, cz_ref, inv_ref, dw,
    u_far, cx_far, cy_far, cz_far, inv_far, rhs_far, diag_ref, xp_ref,
    u_ref, rhs_ref, va, vb, upd, scr, *sems,
):
    saves = copies_of(
        (cx_ref, cy_ref, cz_ref, inv_ref, rhs_ref, u_ref),
        (cx_far, cy_far, cz_far, inv_far, rhs_far, u_far),
        sems,
    )
    for m in saves[:4]:
        m.start()
    lane1 = iota((32, 128), 1)
    for i in range(32):
        g, at = i // 5, (i % 5) * 24
        right = roll(zhi_ref[g], -at, 1)
        left = roll(zlo_ref[g], 104 - at, 1)
        halo = jnp.where(lane1 < 24, right, jnp.where(lane1 >= 104, left, 0.0))
        for t, part in enumerate((f_ref[i], halo)):
            at = slice(128 * t, 128 * t + 128)
            scaled = part * inv_ref[i, :, at]
            rhs_ref[i, :, at] = scaled
            scaled = FIRST * scaled
            upd[i, :, at] = scaled
            va[i, :, at] = scaled
    saves[4].start()
    level = Level(cx_ref, cy_ref, cz_ref, inv_ref, rhs_ref, 0)
    sweep(level, va, vb, upd, 1, 31, NEAR, *TERMS[0])
    sweep(level, vb, va, upd, 2, 30, NEAR, *TERMS[1])
    sweep(level, va, u_ref, upd, 3, 29, NEAR, *TERMS[2], store_update=False)
    saves[5].start()

    def save_diag(i):
        diag_ref[i] = dw[i + 8, 0:16, 0:128]

    loop(0, 16, 4, save_diag)
    for p in range(8):
        i = 8 + 2 * p
        total = None
        for k in (i, i + 1):
            _, d = level.defect(u_ref, k)
            r = dw[k] * d
            total = r if total is None else total + r
        put_lanes(scr, 0, p, 0.125 * total)
    fold_lanes(scr, ("f",), xp_ref)
    for m in saves:
        m.wait()


TILES = 6


def packy1(x0, x1, x2, x3, up_ref, down_ref):
    low = iota((8, 128), 0) < 4
    xs = (x0, x1, x2, x3)
    tiles = up_ref.shape[0] // 6
    half = 2 * tiles
    for q in range(2 * half):
        own = xs[q // tiles][q % tiles, 0:8, :]
        up_ref[q] = own
        down_ref[q] = own
    for q in range(half):
        one = xs[q // tiles][q % tiles, 8:16, :]
        two = xs[2 + q // tiles][q % tiles, 8:16, :]
        up_ref[2 * half + q] = jnp.where(low, roll(one, 4, 0), two)
        down_ref[2 * half + q] = jnp.where(low, one, roll(two, 4, 0))


def unpack1(xs, lo_ref, hi_ref, k, t, own_face=False):
    row = iota((8, 128), 0)
    tiles = hi_ref.shape[0] // 6
    q, half = k * tiles + t, 2 * tiles
    right, left = hi_ref[2 * half + q % half], lo_ref[2 * half + q % half]
    if q < half:
        edge = jnp.where(row < 4, right, roll(left, 4, 0))
    else:
        edge = jnp.where(row < 4, roll(right, 4, 0), left)
    after = hi_ref[q]
    if own_face:
        after = jnp.where(row == 0, xs[k][t, 8:16, :], after)
    return jnp.concatenate([xs[k][t, 0:8, :], after, edge, lo_ref[q]], axis=0)


def pair_matrices(cut, size_in=128):
    fine = iota((size_in, 128), 0)
    coarse = iota((size_in, 128), 1)
    at = signed(fine, size_in, cut)
    both = jnp.where(((at >> 1) & 127) == coarse, 1.0, 0.0)
    even = jnp.where((((at >> 1) & 127) == coarse) & ((at & 1) == 0), 1.0, 0.0)
    return both, even


def restrict(scr, both, even, count, arrays=5):
    out = []
    for a in range(arrays):
        folded = scr[a, pl.ds(0, count, stride=2), :]
        if a != 2:
            folded = folded + scr[a, pl.ds(1, count, stride=2), :]
        out.append(exact_dot(folded, even if a == 3 else both))
    return out


def mid_down(
    c0, c1, c2, c3, clo_ref, chi_ref, f0, f1, f2, f3, flo_ref, fhi_ref,
    u_far, cx_far, cy_far, cz_far, inv_far, rhs_far, own_ref, ym_ref, yp_ref,
    u_ref, cx_ref, cy_ref, cz_ref, inv_ref, rhs_ref,
    va, vb, upd, dw, ux, uy, uz, hx, oth, scr, *sems,
):
    saves = copies_of(
        (cx_ref, cy_ref, cz_ref, inv_ref, rhs_ref, u_ref),
        (cx_far, cy_far, cz_far, inv_far, rhs_far, u_far),
        sems,
    )
    lane = iota((32, 128), 1)
    px, py, pz = lax.axis_index("gx"), lax.axis_index("gy"), lax.axis_index("gz")
    row = iota((32, 128), 0)
    coarse = ((c0, c1, c2, c3), clo_ref, chi_ref)
    pieces = [(ux, 0.0) + coarse + (0,), (uy, 0.0) + coarse + (1,), (uz, 1.0) + coarse + (2,)]
    pieces += [(va, 0.0, (f0, f1, f2, f3), flo_ref, fhi_ref, 0)]
    for target, fill, xs, lo_ref, hi_ref, a in pieces:
        face = target is uy
        for k in range(4):
            sides = [
                unpack1(xs, lo_ref, hi_ref, k, TILES * a + 4 + g, face) for g in range(2)
            ]
            for j in range(4):
                base = unpack1(xs, lo_ref, hi_ref, k, TILES * a + j, face)
                for g in range(2):
                    own = roll(base, 64, 1) if g else base
                    right = roll(sides[g], 64 - 32 * j, 1)
                    left = roll(sides[g], 96 - 32 * j, 1)
                    halo = jnp.where(lane < 80, right, jnp.where(lane >= 112, left, fill))
                    target[8 * k + 4 * g + j] = jnp.where(lane < 64, own, halo)
    high_x = None
    for k in range(4):
        part = unpack1(coarse[0], clo_ref, chi_ref, k, 3 * TILES)
        high_x = part if high_x is None else jnp.where(px == 3 - k, part, high_x)
    hx[...] = high_x
    for k in range(4):
        oth[8 * k : 8 * k + 8, :] = coarse[0][k][3 * TILES + 1, 0:8, :]
    y_open = jnp.where(((8 * py + signed(row, 32, 20)) & 63) == 0, 0.0, 1.0)
    z_open = jnp.where(((64 * pz + signed(lane, 128, 96)) & 511) == 0, 0.0, 1.0)

    def coefficients(i):
        x_at = (8 * px + i) & 31
        cx, cy, cz = ux[i], uy[i], uz[i]
        above = jnp.where(x_at == 31, hx[...], ux[(i + 1) & 31])
        other = jnp.broadcast_to(oth[pl.ds(i, 1), :], (32, 128))
        here = jnp.where((row == 8) & (py == 7), other, cy)
        after = jnp.where((row == 31) & (py == 0), other, roll(cy, -1, 0))
        d = cx + above + (here + after) + (cz + roll(cz, -1, 1))
        cx_ref[i] = jnp.where(x_at == 0, 0.0, 1.0).astype(F32) * cx
        cy_ref[i] = y_open * cy
        cz_ref[i] = z_open * cz
        inv = 1.0 / d
        inv_ref[i] = inv
        dw[i] = d
        g = 4.0 * va[i] * inv
        rhs_ref[i] = g
        first = FIRST * g
        upd[i] = first
        va[i] = first

    loop(0, 32, 8, coefficients)
    for m in saves[:5]:
        m.start()
    level = Level(cx_ref, cy_ref, cz_ref, inv_ref, rhs_ref, 32)
    sweep(level, va, vb, upd, 0, 32, FULL, *TERMS[0])
    sweep(level, vb, va, upd, 0, 32, FULL, *TERMS[1])
    sweep(level, va, u_ref, upd, 0, 32, FULL, *TERMS[2], store_update=False)
    saves[5].start()
    for p in range(16):
        i = 2 * p
        _, d0 = level.defect(u_ref, i)
        _, d1 = level.defect(u_ref, i + 1)
        at = slice(32 * p, 32 * p + 32)
        scr[0, at, :] = 0.03125 * (dw[i] * d0 + dw[i + 1] * d1)
        scr[1, at, :] = 0.25 * ux[i]
        scr[2, at, :] = 0.25 * (uy[i] + uy[i + 1])
        scr[3, at, :] = 0.25 * (uz[i] + uz[i + 1])
    scr[4, 0:32, :] = 0.25 * hx[...]
    both, even = pair_matrices(96)
    f, cx, cy, cz = [r.reshape(16, 16, 128) for r in restrict(scr, both, even, 256, 4)]
    high_x = exact_dot(scr[4, pl.ds(0, 16, stride=2), :] + scr[4, pl.ds(1, 16, stride=2), :], both)
    y_open = jnp.where(((4 * py + signed(row[:16], 16, 10)) & 31) == 0, 0.0, 1.0)
    z_open = jnp.where(((32 * pz + signed(lane[:16], 128, 96)) & 255) == 0, 0.0, 1.0)
    others = exact_dot(oth[pl.ds(0, 16, stride=2), :] + oth[pl.ds(1, 16, stride=2), :], both)
    planes = []
    for p in range(16):
        x_at = (4 * px + p) & 15
        other = jnp.broadcast_to(0.25 * others[p : p + 1], (16, 128))
        here = jnp.where((row[:16] == 4) & (py == 7), other, cy[p])
        after = jnp.where((row[:16] == 15) & (py == 0), other, roll(cy[p], -1, 0))
        above = jnp.where(x_at == 15, high_x, cx[(p + 1) % 16])
        d = cx[p] + above + (here + after) + (cz[p] + roll(cz[p], -1, 1))
        x_open = jnp.where(x_at == 0, 0.0, 1.0).astype(F32)
        planes.append((f[p], x_open * cx[p], y_open * cy[p], z_open * cz[p], d))
    lane8 = iota((16, 128), 1)
    row8 = iota((8, 128), 0)
    for a in range(5):
        for j in range(4):
            packed = planes[j][a]
            for k in range(1, 4):
                packed = jnp.where(lane8 >= 32 * k, roll(planes[4 * k + j][a], 32 * k, 1), packed)
            own_ref[a, j] = packed
            ym_ref[a, j] = jnp.where(row8 == 7, packed[8:16], packed[0:8])
            yp_ref[a, j] = jnp.where(row8 < 5, packed[0:8], packed[8:16])
    for m in saves:
        m.wait()


def pack2(own_ref, hi_ref, far_ref, lo_ref, up_ref, down_ref, w_ref):
    row = iota((8, 128), 0)
    for a in range(5):
        for j in range(4):
            hi, far, lo = hi_ref[a, j], far_ref[a, j], lo_ref[a, j]
            w_ref[a, j, 0:8, :] = jnp.where(row == 7, hi, own_ref[a, j, 0:8, :])
            w_ref[a, j, 8:16, :] = jnp.where(row == 7, far, hi)
            w_ref[a, j, 16:24, :] = jnp.where(row < 5, far, lo)
            w_ref[a, j, 24:32, :] = jnp.where(row < 5, lo, own_ref[a, j, 8:16, :])

    def get(p):
        return w_ref[p // 16, p % 4], 32 * (p % 16 // 4)

    ups, downs = z_pack(get, 80, 32, (21, 0), 11, 11)
    for g in range(8):
        up_ref[g] = ups[g]
        down_ref[g] = downs[g]


def low_down(
    w_ref, zlo_ref, zhi_ref,
    u_far, cx_far, cy_far, cz_far, inv_far, rhs_far, own_ref,
    u_ref, cx_ref, cy_ref, cz_ref, inv_ref, rhs_ref,
    va, vb, upd, dw, scr, *sems,
):
    saves = copies_of(
        (cx_ref, cy_ref, cz_ref, inv_ref, rhs_ref, u_ref),
        (cx_far, cy_far, cz_far, inv_far, rhs_far, u_far),
        sems,
    )
    lane = iota((32, 128), 1)
    targets = (va, cx_ref, cy_ref, cz_ref, dw)
    for a in range(5):
        fill = 1.0 if a == 4 else 0.0
        for p in range(16):
            base = roll(w_ref[a, p % 4], -32 * (p // 4), 1)
            g, at = (16 * a + p) // 11, (16 * a + p) % 11 * 11
            right = roll(zhi_ref[g], 32 - at, 1)
            left = roll(zlo_ref[g], 117 - at, 1)
            halo = jnp.where(lane < 43, right, jnp.where(lane >= 117, left, fill))
            targets[a][p] = jnp.where(lane < 32, base, halo)

    def coefficients(i):
        inv = 1.0 / dw[i]
        inv_ref[i] = inv
        g = 16.0 * va[i] * inv
        rhs_ref[i] = g
        first = FIRST * g
        upd[i] = first
        va[i] = first

    loop(0, 16, 8, coefficients)
    for m in saves[:5]:
        m.start()
    level = Level(cx_ref, cy_ref, cz_ref, inv_ref, rhs_ref, 16)
    sweep(level, va, vb, upd, 0, 16, FULL, *TERMS[0])
    sweep(level, vb, va, upd, 0, 16, FULL, *TERMS[1])
    sweep(level, va, u_ref, upd, 0, 16, FULL, *TERMS[2], store_update=False)
    saves[5].start()

    def edge(i):
        above = (i + 1) & 15
        cy, cz = cy_ref[i], cz_ref[i]
        inner = cx_ref[i] + cx_ref[above] + (cy + roll(cy, -1, 0)) + (cz + roll(cz, -1, 1))
        return dw[i] - inner

    for p in range(8):
        i = 2 * p
        _, d0 = level.defect(u_ref, i)
        _, d1 = level.defect(u_ref, i + 1)
        at = slice(32 * p, 32 * p + 32)
        scr[0, at, :] = 0.0078125 * (dw[i] * d0 + dw[i + 1] * d1)
        scr[1, at, :] = 0.25 * cx_ref[i]
        scr[2, at, :] = 0.25 * (cy_ref[i] + cy_ref[i + 1])
        scr[3, at, :] = 0.25 * (cz_ref[i] + cz_ref[i + 1])
        scr[4, at, :] = 0.25 * (edge(i) + edge(i + 1))
    both, even = pair_matrices(96)
    f, cx, cy, cz, e = [r.reshape(8, 16, 128) for r in restrict(scr, both, even, 128)]
    planes = []
    for p in range(8):
        inner = cx[p] + cx[(p + 1) % 8] + (cy[p] + roll(cy[p], -1, 0))
        d = inner + (cz[p] + roll(cz[p], -1, 1)) + e[p]
        planes.append((f[p], cx[p], cy[p], cz[p], d))
    lane16 = iota((16, 128), 1)
    for a in range(5):
        packed = planes[0][a]
        for p in range(1, 8):
            packed = jnp.where(lane16 >= 16 * p, roll(planes[p][a], 16 * p, 1), packed)
        own_ref[a] = packed
    for m in saves:
        m.wait()


def spread(dup, w, rows, matrix):
    count = w.shape[0]
    dup[pl.ds(0, count, stride=2), :] = w
    dup[pl.ds(1, count, stride=2), :] = w
    return exact_dot(dup[0 : 2 * count, :], matrix)


def spread_matrix(cut, size):
    coarse = iota((128, size), 0)
    at = signed(iota((128, size), 1), size, cut)
    return jnp.where(((at >> 1) & 127) == coarse, 1.0, 0.0)


def post(level, va, vb, upd, ranges, unroll):
    lo, hi = ranges[0]
    sweep(level, va, vb, upd, lo, hi, unroll, None, FIRST)
    src, dst = vb, va
    for n in range(3):
        lo, hi = ranges[n + 1]
        sweep(level, src, dst, upd, lo, hi, unroll, *TERMS[n], store_update=n < 2)
        src, dst = dst, src


def up(
    g_ref, *refs,
):
    fars, refs = refs[:19], refs[19:]
    (sol_far, res_far), refs = refs[:2], refs[2:]
    (l3, inv3, rhs3, u3, va3, vb3, upd3, scr3), refs = refs[:8], refs[8:]
    (va2, vb2, upd2, dup2, va1, vb1, upd1, dup1, va0, vb0, upd0, dup0), refs = refs[:12], refs[12:]
    nears, (sol_ref, res_ref), sems = refs[:19], refs[19:21], refs[21:]
    u2, cx2, cy2, cz2, inv2, rhs2 = nears[:6]
    u1, cx1, cy1, cz1, inv1, rhs1 = nears[6:12]
    u0, cx0, cy0, cz0, inv0, rhs0, diag0 = nears[12:]
    loads = copies_of(fars, nears, sems)
    for m in loads:
        m.start()
    me = lax.axis_index("gz")
    lane = iota((16, 128), 1)
    for a in range(5):
        tiles = [g_ref[(me + k) & 7, a] for k in range(8)]
        for p in range(8):
            plane = roll(tiles[0], -16 * p, 1)
            for k in range(1, 8):
                plane = jnp.where(lane >= 16 * k, roll(tiles[k], 16 * (k - p), 1), plane)
            l3[a, p] = plane
    f3, cx3, cy3, cz3, d3 = [l3.at[a] for a in range(5)]
    level = Level(cx3, cy3, cz3, inv3, rhs3, 8)

    def start3(i):
        inv = 1.0 / d3[i]
        inv3[i] = inv
        g = 64.0 * f3[i] * inv
        rhs3[i] = g
        first = FIRST * g
        upd3[i] = first
        va3[i] = first

    loop(0, 8, 8, start3)
    sweep(level, va3, vb3, upd3, 0, 8, 8, *TERMS[0])
    sweep(level, vb3, va3, upd3, 0, 8, 8, *TERMS[1])
    sweep(level, va3, u3, upd3, 0, 8, 8, *TERMS[2], store_update=False)
    for p in range(4):
        i = 2 * p
        _, r0 = level.defect(u3, i)
        _, r1 = level.defect(u3, i + 1)
        at = slice(16 * p, 16 * p + 16)
        scr3[0, at, :] = (0.125 / 64.0) * (d3[i] * r0 + d3[i + 1] * r1)
        scr3[1, at, :] = 0.25 * cx3[i]
        scr3[2, at, :] = 0.25 * (cy3[i] + cy3[i + 1])
        scr3[3, at, :] = 0.25 * (cz3[i] + cz3[i + 1])
        total = None
        for k in (i, i + 1):
            cy, cz = cy3[k], cz3[k]
            inner = cx3[k] + cx3[(k + 1) % 8] + (cy + roll(cy, -1, 0))
            inner = inner + (cz + roll(cz, -1, 1))
            total = d3[k] - inner if total is None else total + (d3[k] - inner)
        scr3[4, at, :] = 0.25 * total
    fine = iota((128, 128), 0)
    coarse = iota((128, 128), 1) & 63
    both = jnp.where((fine >> 1) == coarse, 1.0, 0.0)
    even = jnp.where(fine == 2 * coarse, 1.0, 0.0)
    f, cx, cy, cz, e = restrict(scr3, both, even, 32)

    def cut(a, p):
        return a[8 * p : 8 * p + 8]

    fs, cxs, cys, czs = [[cut(a, p) for p in range(4)] for a in (f, cx, cy, cz)]
    invs, gs, vs, es = [], [], [], []
    for p in range(4):
        d = cxs[p] + cxs[(p + 1) % 4] + (cys[p] + roll(cys[p], -1, 0))
        d = d + (czs[p] + roll(czs[p], -1, 1)) + cut(e, p)
        invs.append(1.0 / d)
        gs.append(256.0 * fs[p] * invs[p])
        es.append(CFIRST * gs[p])
        vs.append(es[p])
    xlo = [invs[p] * cxs[p] for p in range(4)]
    xhi = [invs[p] * cxs[(p + 1) % 4] for p in range(4)]
    ylo = [invs[p] * cys[p] for p in range(4)]
    yhi = [invs[p] * roll(cys[p], -1, 0) for p in range(4)]
    zlo = [invs[p] * czs[p] for p in range(4)]
    zhi = [invs[p] * roll(czs[p], -1, 1) for p in range(4)]
    for momentum, push in CTERMS:
        momentum, push = float(np.float32(momentum)), float(np.float32(push))
        new_v, new_e = [], []
        for p in range(4):
            v = vs[p]
            total = xlo[p] * vs[(p + 3) % 4] + xhi[p] * vs[(p + 1) % 4]
            total = total + (ylo[p] * roll(v, 1, 0) + yhi[p] * roll(v, -1, 0))
            total = total + (zlo[p] * roll(v, 1, 1) + zhi[p] * roll(v, -1, 1))
            ne = momentum * es[p] + push * ((gs[p] - v) + total)
            new_e.append(ne)
            new_v.append(v + ne)
        vs, es = new_v, new_e
    w4 = jnp.concatenate(vs, axis=0)
    fine = iota((128, 128), 1)
    coarse = iota((128, 128), 0)
    m = jnp.where((fine >> 1) == coarse, 1.0, 0.0)
    wide = spread(dup2, w4, 8, m)
    for i in range(8):
        p = i // 2
        va3[i] = u3[i] + wide[16 * p : 16 * p + 16]
    post(level, va3, vb3, upd3, [(0, 8)] * 4, 8)
    for m in loads[:6]:
        m.wait()
    w3 = va3[...].reshape(128, 128)
    wide = spread(dup2, w3, 16, spread_matrix(96, 128))
    for i in range(16):
        p = i // 2
        va2[i] = u2[i] + wide[32 * p : 32 * p + 32]
    level = Level(cx2, cy2, cz2, inv2, rhs2, 16)
    post(level, va2, vb2, upd2, [(0, 16)] * 4, FULL)
    for m in loads[6:12]:
        m.wait()
    w2 = jnp.concatenate([va2[:, 0:8, :], va2[:, 24:32, :]], axis=1).reshape(256, 128)
    wide = spread(dup1, w2, 16, spread_matrix(96, 128))
    for i in range(32):
        p = i // 2
        va1[i] = u1[i] + wide[32 * p : 32 * p + 32]
    level = Level(cx1, cy1, cz1, inv1, rhs1, 32)
    post(level, va1, vb1, upd1, [(0, 32)] * 4, FULL)
    for m in loads[12:]:
        m.wait()
    rows = [
        jnp.concatenate([va1[i % 32, 0:8, :], mix_rows(va1, i % 32)], axis=0) for i in range(-4, 12)
    ]
    w1 = jnp.concatenate(rows, axis=0)
    wide = spread(dup0, w1, 16, spread_matrix(192, 256))
    for i in range(3, 29):
        p = i // 2
        va0[i] = u0[i] + wide[32 * p : 32 * p + 32]
    level = Level(cx0, cy0, cz0, inv0, rhs0, 0)
    post(level, va0, vb0, upd0, [(4, 28), (5, 27), (6, 26), (7, 25)], NEAR)

    for i in range(16):
        sol_ref[i] = va0[i + 8, 0:16, 0:128]
    ends = copies_of((sol_ref, res_ref), (sol_far, res_far), sems[19:])
    ends[0].start()

    def finish(i):
        _, d = level.defect(va0, i)
        res_ref[i - 8] = diag0[i - 8] * d[0:16, 0:128]

    loop(8, 24, 16, finish)
    ends[1].start()
    for m in ends:
        m.wait()


def mix_rows(ref, i):
    low = iota((8, 128), 0) < 4
    return jnp.where(low, ref[i, 8:16, :], ref[i, 24:32, :])


def call(body, args, outs, scratch=(), limit=16, far_in=(), far_out=(), copies=0, us=1):
    near, far = pl.BlockSpec(memory_space=pltpu.VMEM), pl.BlockSpec(memory_space=pltpu.HBM)
    return pl.pallas_call(
        body,
        out_shape=[jax.ShapeDtypeStruct(s, F32) for s in outs],
        in_specs=[far if i in far_in else near for i in range(len(args))],
        out_specs=[far if i in far_out else near for i in range(len(outs))],
        scratch_shapes=[pltpu.VMEM(s, F32) for s in scratch]
        + [pltpu.SemaphoreType.DMA] * copies,
        compiler_params=pltpu.CompilerParams(vmem_limit_bytes=limit * MIB),
        name=body.__name__,
        cost_estimate=pl.CostEstimate(
            flops=0, bytes_accessed=us * 3_000_000, transcendentals=0
        ),
    )(*args)


def move(values, axis, shift):
    size = lax.axis_size(axis)
    return lax.ppermute(values, axis, [((i + shift) % size, i) for i in range(size)])


def local(source, conductivity):
    f, b = source, conductivity
    ends = lax.optimization_barrier(jnp.concatenate([f[8:16], b[7:16], f[0:8], b[0:9]]))
    to_hi, to_lo = ends[:17], ends[17:]
    xs = [move(to_hi, "gx", -1), move(to_lo, "gx", 1)]
    to_hi, to_lo = call(packy0, [f, b] + xs, [(66, 8, 128)] * 2)
    ys = [move(to_hi, "gy", -1), move(to_lo, "gy", 1)]
    to_hi, to_lo, bw = call(
        pack0b, [b] + xs + ys, [(7, 32, 128)] * 2 + [(34, 32, 128)]
    )
    zb = [move(to_hi, "gz", -1), move(to_lo, "gz", 1)]
    to_hi, to_lo, fw = call(
        pack0f, [f] + xs + ys, [(7, 32, 128)] * 2 + [(32, 32, 128)]
    )
    zf = [move(to_hi, "gz", -1), move(to_lo, "gz", 1)]
    big = (32, 32, 256)
    cx0, cy0, cz0, inv0, d0, xpc = call(
        fine_coef,
        [bw] + [e[64:].reshape(16, 128) for e in ys] + zb,
        [big] * 5 + [(3 * TILES + 2, 16, 128)],
        [(34, 32, 256), big, big, (33, 32, 256), (4, 2, 256, 128)],
        24,
        us=20,
    )
    xpc, zf = lax.optimization_barrier((xpc, zf))
    u0, cx0, cy0, cz0, inv0, rhs0, diag0, xpf = call(
        fine_down,
        [fw] + zf + [cx0, cy0, cz0, inv0, d0],
        [big] * 6 + [(16, 16, 128), (TILES, 16, 128)],
        [big] * 5 + [(1, 2, 256, 128)],
        24,
        far_out=range(6),
        copies=6,
        us=20,
    )

    def along_x(xp):
        got = {k: move(xp, "gx", k) for k in (1, 3, 2)}
        return [xp, got[1], got[2], got[3]]

    def along_y(xs, tiles, us):
        to_hi, to_lo = call(packy1, xs, [(6 * tiles, 8, 128)] * 2, us=us)
        return xs + [move(to_hi, "gy", -1), move(to_lo, "gy", 1)]

    coarse, xpf = lax.optimization_barrier((along_x(xpc), xpf))
    coarse, right_side = along_y(coarse, 3 * TILES + 1, 20), along_y(along_x(xpf), TILES, 1)
    mid = (32, 32, 128)
    u1, cx1, cy1, cz1, inv1, rhs1, own2, ym, yp = call(
        mid_down,
        coarse + right_side,
        [mid] * 6 + [(5, 4, 16, 128), (5, 4, 8, 128), (5, 4, 8, 128)],
        [mid] * 13 + [(32, 128), (32, 128), (5, 512, 128)],
        far_out=range(6),
        copies=6,
    )
    from_hi, from_lo, far = move(ym, "gy", 2), move(yp, "gy", -2), move(ym, "gy", 4)
    up2, down2, w2 = call(
        pack2, (own2, from_hi, far, from_lo), [(8, 32, 128)] * 2 + [(5, 4, 32, 128)]
    )
    zlo, zhi = move(up2, "gz", -1), move(down2, "gz", 1)
    low = (16, 32, 128)
    u2, cx2, cy2, cz2, inv2, rhs2, own3 = call(
        low_down,
        (w2, zlo, zhi),
        [low] * 6 + [(5, 16, 128)],
        [low] * 10 + [(5, 256, 128)],
        far_out=range(6),
        copies=6,
    )
    everyone = jnp.broadcast_to(own3[None], (8, 5, 16, 128))
    gathered = lax.all_to_all(everyone, "gz", 0, 0)
    tiny = (8, 16, 128)
    return tuple(
        call(
            up,
            (
                gathered,
                u2, cx2, cy2, cz2, inv2, rhs2,
                u1, cx1, cy1, cz1, inv1, rhs1,
                u0, cx0, cy0, cz0, inv0, rhs0, diag0,
            ),
            [(16, 16, 128)] * 2,
            [(5,) + tiny] + [tiny] * 6 + [(5, 64, 128)]
            + [low] * 3 + [(256, 128)] + [mid] * 3 + [(512, 128)] + [big] * 3 + [(512, 128)]
            + [low] * 6 + [mid] * 6 + [big] * 6 + [(16, 16, 128)] * 3,
            28,
            far_in=range(1, 20),
            far_out=(0, 1),
            copies=21,
        )
    )


def solution(mesh):
    spec = P("gx", "gy", "gz")
    return jax.shard_map(
        local, mesh=mesh, in_specs=(spec, spec), out_specs=(spec, spec), check_vma=False
    )
```

```python
import functools

import jax
import jax.numpy as jnp
import numpy as np
from jax import lax
from jax.experimental import pallas as pl
from jax.experimental.pallas import tpu as pltpu
from jax.sharding import PartitionSpec as P

F32 = jnp.float32
CSWEEPS = 32
MIB = 1024 * 1024
NEAR, FULL = 16, 32


def chebyshev_terms(sweep_count, lower_bound, upper_bound):
    center = (upper_bound + lower_bound) / 2.0
    half_width = (upper_bound - lower_bound) / 2.0
    sigma_ratio = center / half_width
    rho_now = 1.0 / sigma_ratio
    terms = []
    for _ in range(sweep_count - 1):
        rho_next = 1.0 / (2.0 * sigma_ratio - rho_now)
        terms.append((rho_next * rho_now, 2.0 * rho_next / half_width))
        rho_now = rho_next
    return 1.0 / center, terms


FIRST, TERMS = chebyshev_terms(4, 0.6, 2.0)
CFIRST, CTERMS = chebyshev_terms(CSWEEPS, 0.05, 2.0)


def harmonic(a, b):
    return 2.0 * a * b / (a + b)


def roll(a, shift, axis):
    return pltpu.roll(a, shift % a.shape[axis], axis)


def iota(shape, dim):
    return lax.broadcasted_iota(jnp.int32, shape, dim)


def exact_dot(a, m):
    m = m.astype(jnp.bfloat16)
    high = a.astype(jnp.bfloat16)
    rest = a - high.astype(F32)
    mid = rest.astype(jnp.bfloat16)
    low = (rest - mid.astype(F32)).astype(jnp.bfloat16)
    parts = [jnp.dot(p, m, preferred_element_type=F32) for p in (high, mid, low)]
    return parts[0] + (parts[1] + parts[2])


def signed(index, size, cut):
    return jnp.where(index < cut, index, index - size)


def loop(lo, hi, unroll, body):
    rounds = (hi - lo) // unroll

    def step(t, carry):
        for u in range(unroll):
            body(lo + t * unroll + u)
        return carry

    if rounds:
        lax.fori_loop(0, rounds, step, 0)
    for i in range(lo + rounds * unroll, hi):
        body(i)


def copies_of(sources, targets, sems):
    return [pltpu.make_async_copy(a, b, s) for a, b, s in zip(sources, targets, sems)]


class Level:
    def __init__(self, cx, cy, cz, inv, rhs, wrap):
        self.cx, self.cy, self.cz, self.inv, self.rhs, self.wrap = cx, cy, cz, inv, rhs, wrap

    def around(self, i):
        if self.wrap:
            return (i + self.wrap - 1) & (self.wrap - 1), (i + 1) & (self.wrap - 1)
        return i - 1, i + 1

    def defect(self, v, i):
        below, above = self.around(i)
        here = v[i]
        cy, cz = self.cy[i], self.cz[i]
        total = self.cx[i] * v[below] + self.cx[above] * v[above]
        total = total + (cy * roll(here, 1, 0) + roll(cy * here, -1, 0))
        total = total + (cz * roll(here, 1, 1) + roll(cz * here, -1, 1))
        return here, self.rhs[i] - here + self.inv[i] * total


def sweep(level, src, dst, upd, lo, hi, unroll, momentum, push, store_update=True):
    def body(i):
        here, d = level.defect(src, i)
        e = push * d
        if momentum is not None:
            e = momentum * upd[i] + e
        if store_update:
            upd[i] = e
        dst[i] = here + e

    loop(lo, hi, unroll, body)


def z_pack(get, planes, rows, starts, width, per):
    lane = iota((rows, 128), 1)
    out = []
    for start in starts:
        tiles = []
        for g in range(0, planes, per):
            acc = jnp.zeros((rows, 128), F32)
            for p in range(g, min(g + per, planes)):
                plane, base = get(p)
                at = (p - g) * width
                moved = roll(plane, at - start - base, 1)
                acc = jnp.where((lane >= at) & (lane < at + width), moved, acc)
            tiles.append(acc)
        out.append(tiles)
    return out


def x_plane(own_ref, lo_ref, hi_ref, first, width, p):
    if p < width:
        return lo_ref, first + p
    if p < width + 16:
        return own_ref, p - width
    return hi_ref, first + p - width - 16


def f_plane(f_ref, lo_ref, hi_ref, p):
    return x_plane(f_ref, lo_ref, hi_ref, 0, 8, p)


def b_plane(b_ref, lo_ref, hi_ref, p):
    return x_plane(b_ref, lo_ref, hi_ref, 8, 9, p)


def packy0(f_ref, b_ref, lo_ref, hi_ref, up_ref, down_ref):
    for p in range(32):
        for at, (ref, q) in (
            (p, f_plane(f_ref, lo_ref, hi_ref, p)),
            (32 + p, b_plane(b_ref, lo_ref, hi_ref, p + 1)),
        ):
            up_ref[at] = ref[q, 8:16, :]
            down_ref[at] = ref[q, 0:8, :]
    row = iota((8, 128), 0)
    for ref, edge in ((up_ref, 7), (down_ref, 8)):
        for t in range(2):
            acc = jnp.zeros((8, 128), F32)
            for r in range(8):
                line = jnp.broadcast_to(b_ref[8 * t + r, edge : edge + 1, :], (8, 128))
                acc = jnp.where(row == r, line, acc)
            ref[64 + t] = acc


def pack0b(b_ref, xlo_ref, xhi_ref, ylo_ref, yhi_ref, up_ref, down_ref, w_ref):
    for p in range(34):
        ref, q = b_plane(b_ref, xlo_ref, xhi_ref, p)
        w_ref[p, 0:16, :] = ref[q]
        if 0 < p < 33:
            w_ref[p, 16:24, :] = yhi_ref[31 + p]
            w_ref[p, 24:32, :] = ylo_ref[31 + p]
        else:
            w_ref[p, 16:32, :] = ref[q]
    ups, downs = z_pack(lambda p: (w_ref[p + 1], 0), 32, 32, (103, 0), 25, 5)
    for g in range(7):
        up_ref[g] = ups[g]
        down_ref[g] = downs[g]


def pack0f(f_ref, xlo_ref, xhi_ref, ylo_ref, yhi_ref, up_ref, down_ref, w_ref):
    for p in range(32):
        ref, q = f_plane(f_ref, xlo_ref, xhi_ref, p)
        w_ref[p, 0:16, :] = ref[q]
        w_ref[p, 16:24, :] = yhi_ref[p]
        w_ref[p, 24:32, :] = ylo_ref[p]
    ups, downs = z_pack(lambda p: (w_ref[p], 0), 32, 32, (104, 0), 24, 5)
    for g in range(7):
        up_ref[g] = ups[g]
        down_ref[g] = downs[g]


def fine_matrices():
    fine_lane = iota((256, 128), 0)
    coarse_lane = iota((256, 128), 1)
    both = jnp.where((fine_lane >> 1) == coarse_lane, 1.0, 0.0)
    even = jnp.where(fine_lane == 2 * coarse_lane, 1.0, 0.0)
    return both, even


def folded_rows(scr, a, count, pairs):
    def rows_of(offset):
        return jnp.concatenate(
            [scr[a, t, pl.ds(offset, count, stride=2), :] for t in range(2)], axis=1
        )

    return rows_of(0) + rows_of(1) if pairs else rows_of(0)


def fold_lanes(scr, slots, xp_ref):
    both, even = fine_matrices()
    lane = iota((8, 128), 1)
    half = lane < 64
    for a, kind in enumerate(slots):
        res = exact_dot(folded_rows(scr, a, 128, kind != "y"), even if kind == "z" else both)
        for t in range(2):
            rows = slice(t * 8, t * 8 + 8)
            for j in range(4):
                lo = res[j * 16 + t * 8 : j * 16 + t * 8 + 8]
                hi = res[(j + 4) * 16 + t * 8 : (j + 4) * 16 + t * 8 + 8]
                xp_ref[a * TILES + j, rows, :] = jnp.where(half, lo, roll(hi, 64, 1))
            for g in range(2):
                acc = None
                for q in range(4):
                    at = (4 * g + q) * 16 + t * 8
                    plane = res[at : at + 8]
                    part = jnp.where(lane < 80, plane, roll(plane, -32, 1))
                    part = roll(part, 32 * q - 64, 1)
                    acc = part if acc is None else jnp.where(lane >= 32 * q, part, acc)
                xp_ref[a * TILES + 4 + g, rows, :] = acc


def put_lanes(scr, a, p, value):
    scr[a, 0, p * 32 : p * 32 + 32, :] = value[:, 0:128]
    scr[a, 1, p * 32 : p * 32 + 32, :] = value[:, 128:256]


def fine_coef(
    b_ref, ylo_ref, yhi_ref, zlo_ref, zhi_ref,
    cx_ref, cy_ref, cz_ref, inv_ref, dw, xp_ref,
    bw, cyw, czw, cxw, scr,
):
    px, py, pz = lax.axis_index("gx"), lax.axis_index("gy"), lax.axis_index("gz")
    lane1 = iota((32, 128), 1)
    lane = iota((32, 256), 1)
    row = iota((32, 256), 0)
    for i in range(34):
        q = min(max(i - 1, 0), 31)
        g, at = q // 5, (q % 5) * 25
        right = roll(zhi_ref[g], -at, 1)
        left = roll(zlo_ref[g], 103 - at, 1)
        bw[i, :, 0:128] = b_ref[i]
        bw[i, :, 128:256] = jnp.where(lane1 < 25, right, jnp.where(lane1 >= 103, left, 1.0))
    y_at = (16 * py + signed(row, 32, 24)) & 127
    z_at = (128 * pz + signed(lane, 256, 192)) & 1023
    y_open = jnp.where(y_at == 0, 0.0, 1.0)
    z_open = jnp.where(z_at == 0, 0.0, 1.0)
    y_low, y_high = (row == 0) & (py == 0), (row == 16) & (py == 7)
    z_low, z_high = (lane == 0) & (pz == 0), (lane == 128) & (pz == 7)

    def face_x(i):
        here, below = bw[i + 1], bw[i]
        inner = jnp.where((px == 0) & (i == 8), here, below)
        outer = jnp.where((px == 3) & (i == 24), below, here)
        cxw[i] = harmonic(outer, inner)

    loop(0, 33, 11, face_x)

    def coefficients(i):
        b = bw[i + 1]
        e_at = jnp.clip(i - 8, 0, 15)
        below = ylo_ref[pl.ds(e_at, 1), :]
        above = yhi_ref[pl.ds(e_at, 1), :]
        below = jnp.concatenate([below, below], axis=1)
        above = jnp.concatenate([above, above], axis=1)
        before = jnp.where(row == 24, jnp.broadcast_to(below, (32, 256)), roll(b, 1, 0))
        cy = harmonic(jnp.where(y_high, before, b), jnp.where(y_low, b, before))
        outer = harmonic(b[16:24], jnp.broadcast_to(above, (8, 256)))
        after = roll(cy, -1, 0)
        after = jnp.concatenate(
            [after[0:16], jnp.where(row[16:24] == 23, outer, after[16:24]), after[24:32]], axis=0
        )
        before = roll(b, 1, 1)
        cz = harmonic(jnp.where(z_high, before, b), jnp.where(z_low, b, before))
        d = cxw[i] + cxw[i + 1] + (cy + after) + (cz + roll(cz, -1, 1))
        x_open = jnp.where(((16 * px + i + 56) & 63) == 0, 0.0, 1.0).astype(F32)
        cx_ref[i] = x_open * cxw[i]
        cy_ref[i] = y_open * cy
        cz_ref[i] = z_open * cz
        cyw[i] = cy
        czw[i] = cz
        inv_ref[i] = 1.0 / d
        dw[i] = d

    loop(0, 32, 8, coefficients)
    for p in range(8):
        i = 8 + 2 * p
        put_lanes(scr, 0, p, 0.25 * cxw[i])
        put_lanes(scr, 1, p, 0.25 * (cyw[i] + cyw[i + 1]))
        put_lanes(scr, 2, p, 0.25 * (czw[i] + czw[i + 1]))
    put_lanes(scr, 3, 0, 0.25 * cxw[24])

    def beyond(i):
        b = bw[i + 1]
        far = jnp.where(py == 0, roll(b, 1, 0)[0:8], b[16:24])
        return harmonic(far, far)

    for p in range(8):
        i = 8 + 2 * p
        far = 0.25 * (beyond(i) + beyond(i + 1))
        scr[3, 0, 32 + 8 * p : 40 + 8 * p, :] = far[:, 0:128]
        scr[3, 1, 32 + 8 * p : 40 + 8 * p, :] = far[:, 128:256]
    fold_lanes(scr, ("x", "y", "z"), xp_ref)
    both, _ = fine_matrices()
    xp_ref[3 * TILES] = exact_dot(folded_rows(scr, 3, 16, True), both)
    far = jnp.concatenate([scr[3, t, pl.ds(32, 8, stride=8), :] for t in range(2)], axis=1)
    xp_ref[3 * TILES + 1, 0:8, :] = exact_dot(far, both)
    xp_ref[3 * TILES + 1, 8:16, :] = jnp.zeros((8, 128), F32)


def fine_down(
    f_ref, zlo_ref, zhi_ref, cx_ref, cy_ref, cz_ref, inv_ref, dw,
    u_far, cx_far, cy_far, cz_far, inv_far, rhs_far, diag_ref, xp_ref,
    u_ref, rhs_ref, va, vb, upd, scr, *sems,
):
    saves = copies_of(
        (cx_ref, cy_ref, cz_ref, inv_ref, rhs_ref, u_ref),
        (cx_far, cy_far, cz_far, inv_far, rhs_far, u_far),
        sems,
    )
    for m in saves[:4]:
        m.start()
    lane1 = iota((32, 128), 1)
    for i in range(32):
        g, at = i // 5, (i % 5) * 24
        right = roll(zhi_ref[g], -at, 1)
        left = roll(zlo_ref[g], 104 - at, 1)
        halo = jnp.where(lane1 < 24, right, jnp.where(lane1 >= 104, left, 0.0))
        for t, part in enumerate((f_ref[i], halo)):
            at = slice(128 * t, 128 * t + 128)
            scaled = part * inv_ref[i, :, at]
            rhs_ref[i, :, at] = scaled
            scaled = FIRST * scaled
            upd[i, :, at] = scaled
            va[i, :, at] = scaled
    saves[4].start()
    level = Level(cx_ref, cy_ref, cz_ref, inv_ref, rhs_ref, 0)
    sweep(level, va, vb, upd, 1, 31, NEAR, *TERMS[0])
    sweep(level, vb, va, upd, 2, 30, NEAR, *TERMS[1])
    sweep(level, va, u_ref, upd, 3, 29, NEAR, *TERMS[2], store_update=False)
    saves[5].start()

    def save_diag(i):
        diag_ref[i] = dw[i + 8, 0:16, 0:128]

    loop(0, 16, 4, save_diag)
    for p in range(8):
        i = 8 + 2 * p
        total = None
        for k in (i, i + 1):
            _, d = level.defect(u_ref, k)
            r = dw[k] * d
            total = r if total is None else total + r
        put_lanes(scr, 0, p, 0.125 * total)
    fold_lanes(scr, ("f",), xp_ref)
    for m in saves:
        m.wait()


TILES = 6


def packy1(x0, x1, x2, x3, up_ref, down_ref):
    low = iota((8, 128), 0) < 4
    xs = (x0, x1, x2, x3)
    tiles = up_ref.shape[0] // 6
    half = 2 * tiles
    for q in range(2 * half):
        own = xs[q // tiles][q % tiles, 0:8, :]
        up_ref[q] = own
        down_ref[q] = own
    for q in range(half):
        one = xs[q // tiles][q % tiles, 8:16, :]
        two = xs[2 + q // tiles][q % tiles, 8:16, :]
        up_ref[2 * half + q] = jnp.where(low, roll(one, 4, 0), two)
        down_ref[2 * half + q] = jnp.where(low, one, roll(two, 4, 0))


def unpack1(xs, lo_ref, hi_ref, k, t, own_face=False):
    row = iota((8, 128), 0)
    tiles = hi_ref.shape[0] // 6
    q, half = k * tiles + t, 2 * tiles
    right, left = hi_ref[2 * half + q % half], lo_ref[2 * half + q % half]
    if q < half:
        edge = jnp.where(row < 4, right, roll(left, 4, 0))
    else:
        edge = jnp.where(row < 4, roll(right, 4, 0), left)
    after = hi_ref[q]
    if own_face:
        after = jnp.where(row == 0, xs[k][t, 8:16, :], after)
    return jnp.concatenate([xs[k][t, 0:8, :], after, edge, lo_ref[q]], axis=0)


def pair_matrices(cut, size_in=128):
    fine = iota((size_in, 128), 0)
    coarse = iota((size_in, 128), 1)
    at = signed(fine, size_in, cut)
    both = jnp.where(((at >> 1) & 127) == coarse, 1.0, 0.0)
    even = jnp.where((((at >> 1) & 127) == coarse) & ((at & 1) == 0), 1.0, 0.0)
    return both, even


def restrict(scr, both, even, count, arrays=5):
    out = []
    for a in range(arrays):
        folded = scr[a, pl.ds(0, count, stride=2), :]
        if a != 2:
            folded = folded + scr[a, pl.ds(1, count, stride=2), :]
        out.append(exact_dot(folded, even if a == 3 else both))
    return out


def mid_down(
    c0, c1, c2, c3, clo_ref, chi_ref, f0, f1, f2, f3, flo_ref, fhi_ref,
    u_far, cx_far, cy_far, cz_far, inv_far, rhs_far, own_ref, ym_ref, yp_ref,
    u_ref, cx_ref, cy_ref, cz_ref, inv_ref, rhs_ref,
    va, vb, upd, dw, ux, uy, uz, hx, oth, scr, *sems,
):
    saves = copies_of(
        (cx_ref, cy_ref, cz_ref, inv_ref, rhs_ref, u_ref),
        (cx_far, cy_far, cz_far, inv_far, rhs_far, u_far),
        sems,
    )
    lane = iota((32, 128), 1)
    px, py, pz = lax.axis_index("gx"), lax.axis_index("gy"), lax.axis_index("gz")
    row = iota((32, 128), 0)
    coarse = ((c0, c1, c2, c3), clo_ref, chi_ref)
    pieces = [(ux, 0.0) + coarse + (0,), (uy, 0.0) + coarse + (1,), (uz, 1.0) + coarse + (2,)]
    pieces += [(va, 0.0, (f0, f1, f2, f3), flo_ref, fhi_ref, 0)]
    for target, fill, xs, lo_ref, hi_ref, a in pieces:
        face = target is uy
        for k in range(4):
            sides = [
                unpack1(xs, lo_ref, hi_ref, k, TILES * a + 4 + g, face) for g in range(2)
            ]
            for j in range(4):
                base = unpack1(xs, lo_ref, hi_ref, k, TILES * a + j, face)
                for g in range(2):
                    own = roll(base, 64, 1) if g else base
                    right = roll(sides[g], 64 - 32 * j, 1)
                    left = roll(sides[g], 96 - 32 * j, 1)
                    halo = jnp.where(lane < 80, right, jnp.where(lane >= 112, left, fill))
                    target[8 * k + 4 * g + j] = jnp.where(lane < 64, own, halo)
    high_x = None
    for k in range(4):
        part = unpack1(coarse[0], clo_ref, chi_ref, k, 3 * TILES)
        high_x = part if high_x is None else jnp.where(px == 3 - k, part, high_x)
    hx[...] = high_x
    for k in range(4):
        oth[8 * k : 8 * k + 8, :] = coarse[0][k][3 * TILES + 1, 0:8, :]
    y_open = jnp.where(((8 * py + signed(row, 32, 20)) & 63) == 0, 0.0, 1.0)
    z_open = jnp.where(((64 * pz + signed(lane, 128, 96)) & 511) == 0, 0.0, 1.0)

    def coefficients(i):
        x_at = (8 * px + i) & 31
        cx, cy, cz = ux[i], uy[i], uz[i]
        above = jnp.where(x_at == 31, hx[...], ux[(i + 1) & 31])
        other = jnp.broadcast_to(oth[pl.ds(i, 1), :], (32, 128))
        here = jnp.where((row == 8) & (py == 7), other, cy)
        after = jnp.where((row == 31) & (py == 0), other, roll(cy, -1, 0))
        d = cx + above + (here + after) + (cz + roll(cz, -1, 1))
        cx_ref[i] = jnp.where(x_at == 0, 0.0, 1.0).astype(F32) * cx
        cy_ref[i] = y_open * cy
        cz_ref[i] = z_open * cz
        inv = 1.0 / d
        inv_ref[i] = inv
        dw[i] = d
        g = 4.0 * va[i] * inv
        rhs_ref[i] = g
        first = FIRST * g
        upd[i] = first
        va[i] = first

    loop(0, 32, 16, coefficients)
    for m in saves[:5]:
        m.start()
    level = Level(cx_ref, cy_ref, cz_ref, inv_ref, rhs_ref, 32)
    sweep(level, va, vb, upd, 0, 32, FULL, *TERMS[0])
    sweep(level, vb, va, upd, 0, 32, FULL, *TERMS[1])
    sweep(level, va, u_ref, upd, 0, 32, FULL, *TERMS[2], store_update=False)
    saves[5].start()
    for p in range(16):
        i = 2 * p
        _, d0 = level.defect(u_ref, i)
        _, d1 = level.defect(u_ref, i + 1)
        at = slice(32 * p, 32 * p + 32)
        scr[0, at, :] = 0.03125 * (dw[i] * d0 + dw[i + 1] * d1)
        scr[1, at, :] = 0.25 * ux[i]
        scr[2, at, :] = 0.25 * (uy[i] + uy[i + 1])
        scr[3, at, :] = 0.25 * (uz[i] + uz[i + 1])
    scr[4, 0:32, :] = 0.25 * hx[...]
    both, even = pair_matrices(96)
    f, cx, cy, cz = [r.reshape(16, 16, 128) for r in restrict(scr, both, even, 256, 4)]
    high_x = exact_dot(scr[4, pl.ds(0, 16, stride=2), :] + scr[4, pl.ds(1, 16, stride=2), :], both)
    y_open = jnp.where(((4 * py + signed(row[:16], 16, 10)) & 31) == 0, 0.0, 1.0)
    z_open = jnp.where(((32 * pz + signed(lane[:16], 128, 96)) & 255) == 0, 0.0, 1.0)
    others = exact_dot(oth[pl.ds(0, 16, stride=2), :] + oth[pl.ds(1, 16, stride=2), :], both)
    planes = []
    for p in range(16):
        x_at = (4 * px + p) & 15
        other = jnp.broadcast_to(0.25 * others[p : p + 1], (16, 128))
        here = jnp.where((row[:16] == 4) & (py == 7), other, cy[p])
        after = jnp.where((row[:16] == 15) & (py == 0), other, roll(cy[p], -1, 0))
        above = jnp.where(x_at == 15, high_x, cx[(p + 1) % 16])
        d = cx[p] + above + (here + after) + (cz[p] + roll(cz[p], -1, 1))
        x_open = jnp.where(x_at == 0, 0.0, 1.0).astype(F32)
        planes.append((f[p], x_open * cx[p], y_open * cy[p], z_open * cz[p], d))
    lane8 = iota((16, 128), 1)
    row8 = iota((8, 128), 0)
    for a in range(5):
        for j in range(4):
            packed = planes[j][a]
            for k in range(1, 4):
                packed = jnp.where(lane8 >= 32 * k, roll(planes[4 * k + j][a], 32 * k, 1), packed)
            own_ref[a, j] = packed
            ym_ref[a, j] = jnp.where(row8 == 7, packed[8:16], packed[0:8])
            yp_ref[a, j] = jnp.where(row8 < 5, packed[0:8], packed[8:16])
    for m in saves:
        m.wait()


def pack2(own_ref, hi_ref, far_ref, lo_ref, up_ref, down_ref, w_ref):
    row = iota((8, 128), 0)
    for a in range(5):
        for j in range(4):
            hi, far, lo = hi_ref[a, j], far_ref[a, j], lo_ref[a, j]
            w_ref[a, j, 0:8, :] = jnp.where(row == 7, hi, own_ref[a, j, 0:8, :])
            w_ref[a, j, 8:16, :] = jnp.where(row == 7, far, hi)
            w_ref[a, j, 16:24, :] = jnp.where(row < 5, far, lo)
            w_ref[a, j, 24:32, :] = jnp.where(row < 5, lo, own_ref[a, j, 8:16, :])

    def get(p):
        return w_ref[p // 16, p % 4], 32 * (p % 16 // 4)

    ups, downs = z_pack(get, 80, 32, (21, 0), 11, 11)
    for g in range(8):
        up_ref[g] = ups[g]
        down_ref[g] = downs[g]


def low_down(
    w_ref, zlo_ref, zhi_ref,
    u_far, cx_far, cy_far, cz_far, inv_far, rhs_far, own_ref,
    u_ref, cx_ref, cy_ref, cz_ref, inv_ref, rhs_ref,
    va, vb, upd, dw, scr, *sems,
):
    saves = copies_of(
        (cx_ref, cy_ref, cz_ref, inv_ref, rhs_ref, u_ref),
        (cx_far, cy_far, cz_far, inv_far, rhs_far, u_far),
        sems,
    )
    lane = iota((32, 128), 1)
    targets = (va, cx_ref, cy_ref, cz_ref, dw)
    for a in range(5):
        fill = 1.0 if a == 4 else 0.0
        for p in range(16):
            base = roll(w_ref[a, p % 4], -32 * (p // 4), 1)
            g, at = (16 * a + p) // 11, (16 * a + p) % 11 * 11
            right = roll(zhi_ref[g], 32 - at, 1)
            left = roll(zlo_ref[g], 117 - at, 1)
            halo = jnp.where(lane < 43, right, jnp.where(lane >= 117, left, fill))
            targets[a][p] = jnp.where(lane < 32, base, halo)

    def coefficients(i):
        inv = 1.0 / dw[i]
        inv_ref[i] = inv
        g = 16.0 * va[i] * inv
        rhs_ref[i] = g
        first = FIRST * g
        upd[i] = first
        va[i] = first

    loop(0, 16, 16, coefficients)
    for m in saves[:5]:
        m.start()
    level = Level(cx_ref, cy_ref, cz_ref, inv_ref, rhs_ref, 16)
    sweep(level, va, vb, upd, 0, 16, FULL, *TERMS[0])
    sweep(level, vb, va, upd, 0, 16, FULL, *TERMS[1])
    sweep(level, va, u_ref, upd, 0, 16, FULL, *TERMS[2], store_update=False)
    saves[5].start()

    def edge(i):
        above = (i + 1) & 15
        cy, cz = cy_ref[i], cz_ref[i]
        inner = cx_ref[i] + cx_ref[above] + (cy + roll(cy, -1, 0)) + (cz + roll(cz, -1, 1))
        return dw[i] - inner

    for p in range(8):
        i = 2 * p
        _, d0 = level.defect(u_ref, i)
        _, d1 = level.defect(u_ref, i + 1)
        at = slice(32 * p, 32 * p + 32)
        scr[0, at, :] = 0.0078125 * (dw[i] * d0 + dw[i + 1] * d1)
        scr[1, at, :] = 0.25 * cx_ref[i]
        scr[2, at, :] = 0.25 * (cy_ref[i] + cy_ref[i + 1])
        scr[3, at, :] = 0.25 * (cz_ref[i] + cz_ref[i + 1])
        scr[4, at, :] = 0.25 * (edge(i) + edge(i + 1))
    both, even = pair_matrices(96)
    f, cx, cy, cz, e = [r.reshape(8, 16, 128) for r in restrict(scr, both, even, 128)]
    planes = []
    for p in range(8):
        inner = cx[p] + cx[(p + 1) % 8] + (cy[p] + roll(cy[p], -1, 0))
        d = inner + (cz[p] + roll(cz[p], -1, 1)) + e[p]
        planes.append((f[p], cx[p], cy[p], cz[p], d))
    lane16 = iota((16, 128), 1)
    for a in range(5):
        packed = planes[0][a]
        for p in range(1, 8):
            packed = jnp.where(lane16 >= 16 * p, roll(planes[p][a], 16 * p, 1), packed)
        own_ref[a] = packed
    for m in saves:
        m.wait()


def spread(dup, w, rows, matrix):
    count = w.shape[0]
    dup[pl.ds(0, count, stride=2), :] = w
    dup[pl.ds(1, count, stride=2), :] = w
    return exact_dot(dup[0 : 2 * count, :], matrix)


def spread_matrix(cut, size):
    coarse = iota((128, size), 0)
    at = signed(iota((128, size), 1), size, cut)
    return jnp.where(((at >> 1) & 127) == coarse, 1.0, 0.0)


def post(level, va, vb, upd, ranges, unroll):
    lo, hi = ranges[0]
    sweep(level, va, vb, upd, lo, hi, unroll, None, FIRST)
    src, dst = vb, va
    for n in range(3):
        lo, hi = ranges[n + 1]
        sweep(level, src, dst, upd, lo, hi, unroll, *TERMS[n], store_update=n < 2)
        src, dst = dst, src


def up(
    g_ref, *refs,
):
    fars, refs = refs[:19], refs[19:]
    (sol_far, res_far), refs = refs[:2], refs[2:]
    (l3, inv3, rhs3, u3, va3, vb3, upd3, scr3), refs = refs[:8], refs[8:]
    (va2, vb2, upd2, dup2, va1, vb1, upd1, dup1, va0, vb0, upd0, dup0), refs = refs[:12], refs[12:]
    nears, (sol_ref, res_ref), sems = refs[:19], refs[19:21], refs[21:]
    u2, cx2, cy2, cz2, inv2, rhs2 = nears[:6]
    u1, cx1, cy1, cz1, inv1, rhs1 = nears[6:12]
    u0, cx0, cy0, cz0, inv0, rhs0, diag0 = nears[12:]
    loads = copies_of(fars, nears, sems)
    for m in loads:
        m.start()
    me = lax.axis_index("gz")
    lane = iota((16, 128), 1)
    for a in range(5):
        tiles = [g_ref[(me + k) & 7, a] for k in range(8)]
        for p in range(8):
            plane = roll(tiles[0], -16 * p, 1)
            for k in range(1, 8):
                plane = jnp.where(lane >= 16 * k, roll(tiles[k], 16 * (k - p), 1), plane)
            l3[a, p] = plane
    f3, cx3, cy3, cz3, d3 = [l3.at[a] for a in range(5)]
    level = Level(cx3, cy3, cz3, inv3, rhs3, 8)

    def start3(i):
        inv = 1.0 / d3[i]
        inv3[i] = inv
        g = 64.0 * f3[i] * inv
        rhs3[i] = g
        first = FIRST * g
        upd3[i] = first
        va3[i] = first

    loop(0, 8, 8, start3)
    sweep(level, va3, vb3, upd3, 0, 8, 8, *TERMS[0])
    sweep(level, vb3, va3, upd3, 0, 8, 8, *TERMS[1])
    sweep(level, va3, u3, upd3, 0, 8, 8, *TERMS[2], store_update=False)
    for p in range(4):
        i = 2 * p
        _, r0 = level.defect(u3, i)
        _, r1 = level.defect(u3, i + 1)
        at = slice(16 * p, 16 * p + 16)
        scr3[0, at, :] = (0.125 / 64.0) * (d3[i] * r0 + d3[i + 1] * r1)
        scr3[1, at, :] = 0.25 * cx3[i]
        scr3[2, at, :] = 0.25 * (cy3[i] + cy3[i + 1])
        scr3[3, at, :] = 0.25 * (cz3[i] + cz3[i + 1])
        total = None
        for k in (i, i + 1):
            cy, cz = cy3[k], cz3[k]
            inner = cx3[k] + cx3[(k + 1) % 8] + (cy + roll(cy, -1, 0))
            inner = inner + (cz + roll(cz, -1, 1))
            total = d3[k] - inner if total is None else total + (d3[k] - inner)
        scr3[4, at, :] = 0.25 * total
    fine = iota((128, 128), 0)
    coarse = iota((128, 128), 1) & 63
    both = jnp.where((fine >> 1) == coarse, 1.0, 0.0)
    even = jnp.where(fine == 2 * coarse, 1.0, 0.0)
    f, cx, cy, cz, e = restrict(scr3, both, even, 32)

    def cut(a, p):
        return a[8 * p : 8 * p + 8]

    fs, cxs, cys, czs = [[cut(a, p) for p in range(4)] for a in (f, cx, cy, cz)]
    invs, gs, vs, es = [], [], [], []
    for p in range(4):
        d = cxs[p] + cxs[(p + 1) % 4] + (cys[p] + roll(cys[p], -1, 0))
        d = d + (czs[p] + roll(czs[p], -1, 1)) + cut(e, p)
        invs.append(1.0 / d)
        gs.append(256.0 * fs[p] * invs[p])
        es.append(CFIRST * gs[p])
        vs.append(es[p])
    xlo = [invs[p] * cxs[p] for p in range(4)]
    xhi = [invs[p] * cxs[(p + 1) % 4] for p in range(4)]
    ylo = [invs[p] * cys[p] for p in range(4)]
    yhi = [invs[p] * roll(cys[p], -1, 0) for p in range(4)]
    zlo = [invs[p] * czs[p] for p in range(4)]
    zhi = [invs[p] * roll(czs[p], -1, 1) for p in range(4)]
    for momentum, push in CTERMS:
        momentum, push = float(np.float32(momentum)), float(np.float32(push))
        new_v, new_e = [], []
        for p in range(4):
            v = vs[p]
            total = xlo[p] * vs[(p + 3) % 4] + xhi[p] * vs[(p + 1) % 4]
            total = total + (ylo[p] * roll(v, 1, 0) + yhi[p] * roll(v, -1, 0))
            total = total + (zlo[p] * roll(v, 1, 1) + zhi[p] * roll(v, -1, 1))
            ne = momentum * es[p] + push * ((gs[p] - v) + total)
            new_e.append(ne)
            new_v.append(v + ne)
        vs, es = new_v, new_e
    w4 = jnp.concatenate(vs, axis=0)
    fine = iota((128, 128), 1)
    coarse = iota((128, 128), 0)
    m = jnp.where((fine >> 1) == coarse, 1.0, 0.0)
    wide = spread(dup2, w4, 8, m)
    for i in range(8):
        p = i // 2
        va3[i] = u3[i] + wide[16 * p : 16 * p + 16]
    post(level, va3, vb3, upd3, [(0, 8)] * 4, 8)
    for m in loads[:6]:
        m.wait()
    w3 = va3[...].reshape(128, 128)
    wide = spread(dup2, w3, 16, spread_matrix(96, 128))
    for i in range(16):
        p = i // 2
        va2[i] = u2[i] + wide[32 * p : 32 * p + 32]
    level = Level(cx2, cy2, cz2, inv2, rhs2, 16)
    post(level, va2, vb2, upd2, [(0, 16)] * 4, FULL)
    for m in loads[6:12]:
        m.wait()
    w2 = jnp.concatenate([va2[:, 0:8, :], va2[:, 24:32, :]], axis=1).reshape(256, 128)
    wide = spread(dup1, w2, 16, spread_matrix(96, 128))
    for i in range(32):
        p = i // 2
        va1[i] = u1[i] + wide[32 * p : 32 * p + 32]
    level = Level(cx1, cy1, cz1, inv1, rhs1, 32)
    post(level, va1, vb1, upd1, [(0, 32)] * 4, FULL)
    for m in loads[12:]:
        m.wait()
    rows = [
        jnp.concatenate([va1[i % 32, 0:8, :], mix_rows(va1, i % 32)], axis=0) for i in range(-4, 12)
    ]
    w1 = jnp.concatenate(rows, axis=0)
    wide = spread(dup0, w1, 16, spread_matrix(192, 256))
    for i in range(3, 29):
        p = i // 2
        va0[i] = u0[i] + wide[32 * p : 32 * p + 32]
    level = Level(cx0, cy0, cz0, inv0, rhs0, 0)
    post(level, va0, vb0, upd0, [(4, 28), (5, 27), (6, 26), (7, 25)], NEAR)

    for i in range(16):
        sol_ref[i] = va0[i + 8, 0:16, 0:128]
    ends = copies_of((sol_ref, res_ref), (sol_far, res_far), sems[19:])
    ends[0].start()

    def finish(i):
        _, d = level.defect(va0, i)
        res_ref[i - 8] = diag0[i - 8] * d[0:16, 0:128]

    loop(8, 24, 16, finish)
    ends[1].start()
    for m in ends:
        m.wait()


def mix_rows(ref, i):
    low = iota((8, 128), 0) < 4
    return jnp.where(low, ref[i, 8:16, :], ref[i, 24:32, :])


def call(body, args, outs, scratch=(), limit=16, far_in=(), far_out=(), copies=0, us=1):
    near, far = pl.BlockSpec(memory_space=pltpu.VMEM), pl.BlockSpec(memory_space=pltpu.HBM)
    return pl.pallas_call(
        body,
        out_shape=[jax.ShapeDtypeStruct(s, F32) for s in outs],
        in_specs=[far if i in far_in else near for i in range(len(args))],
        out_specs=[far if i in far_out else near for i in range(len(outs))],
        scratch_shapes=[pltpu.VMEM(s, F32) for s in scratch]
        + [pltpu.SemaphoreType.DMA] * copies,
        compiler_params=pltpu.CompilerParams(vmem_limit_bytes=limit * MIB),
        name=body.__name__,
        cost_estimate=pl.CostEstimate(
            flops=0, bytes_accessed=us * 3_000_000, transcendentals=0
        ),
    )(*args)


def move(values, axis, shift):
    size = lax.axis_size(axis)
    return lax.ppermute(values, axis, [((i + shift) % size, i) for i in range(size)])


def local(source, conductivity):
    f, b = source, conductivity
    ends = lax.optimization_barrier(jnp.concatenate([f[8:16], b[7:16], f[0:8], b[0:9]]))
    to_hi, to_lo = ends[:17], ends[17:]
    xs = [move(to_hi, "gx", -1), move(to_lo, "gx", 1)]
    to_hi, to_lo = call(packy0, [f, b] + xs, [(66, 8, 128)] * 2)
    ys = [move(to_hi, "gy", -1), move(to_lo, "gy", 1)]
    to_hi, to_lo, bw = call(
        pack0b, [b] + xs + ys, [(7, 32, 128)] * 2 + [(34, 32, 128)]
    )
    zb = [move(to_hi, "gz", -1), move(to_lo, "gz", 1)]
    to_hi, to_lo, fw = call(
        pack0f, [f] + xs + ys, [(7, 32, 128)] * 2 + [(32, 32, 128)]
    )
    zf = [move(to_hi, "gz", -1), move(to_lo, "gz", 1)]
    big = (32, 32, 256)
    cx0, cy0, cz0, inv0, d0, xpc = call(
        fine_coef,
        [bw] + [e[64:].reshape(16, 128) for e in ys] + zb,
        [big] * 5 + [(3 * TILES + 2, 16, 128)],
        [(34, 32, 256), big, big, (33, 32, 256), (4, 2, 256, 128)],
        24,
        us=20,
    )
    xpc, zf = lax.optimization_barrier((xpc, zf))
    u0, cx0, cy0, cz0, inv0, rhs0, diag0, xpf = call(
        fine_down,
        [fw] + zf + [cx0, cy0, cz0, inv0, d0],
        [big] * 6 + [(16, 16, 128), (TILES, 16, 128)],
        [big] * 5 + [(1, 2, 256, 128)],
        24,
        far_out=range(6),
        copies=6,
        us=20,
    )

    def along_x(xp):
        got = {k: move(xp, "gx", k) for k in (1, 3, 2)}
        return [xp, got[1], got[2], got[3]]

    def along_y(xs, tiles, us):
        to_hi, to_lo = call(packy1, xs, [(6 * tiles, 8, 128)] * 2, us=us)
        return xs + [move(to_hi, "gy", -1), move(to_lo, "gy", 1)]

    coarse, xpf = lax.optimization_barrier((along_x(xpc), xpf))
    coarse, right_side = along_y(coarse, 3 * TILES + 1, 20), along_y(along_x(xpf), TILES, 1)
    mid = (32, 32, 128)
    u1, cx1, cy1, cz1, inv1, rhs1, own2, ym, yp = call(
        mid_down,
        coarse + right_side,
        [mid] * 6 + [(5, 4, 16, 128), (5, 4, 8, 128), (5, 4, 8, 128)],
        [mid] * 13 + [(32, 128), (32, 128), (5, 512, 128)],
        far_out=range(6),
        copies=6,
    )
    from_hi, from_lo, far = move(ym, "gy", 2), move(yp, "gy", -2), move(ym, "gy", 4)
    up2, down2, w2 = call(
        pack2, (own2, from_hi, far, from_lo), [(8, 32, 128)] * 2 + [(5, 4, 32, 128)]
    )
    zlo, zhi = move(up2, "gz", -1), move(down2, "gz", 1)
    low = (16, 32, 128)
    u2, cx2, cy2, cz2, inv2, rhs2, own3 = call(
        low_down,
        (w2, zlo, zhi),
        [low] * 6 + [(5, 16, 128)],
        [low] * 10 + [(5, 256, 128)],
        far_out=range(6),
        copies=6,
    )
    everyone = jnp.broadcast_to(own3[None], (8, 5, 16, 128))
    gathered = lax.all_to_all(everyone, "gz", 0, 0)
    tiny = (8, 16, 128)
    return tuple(
        call(
            up,
            (
                gathered,
                u2, cx2, cy2, cz2, inv2, rhs2,
                u1, cx1, cy1, cz1, inv1, rhs1,
                u0, cx0, cy0, cz0, inv0, rhs0, diag0,
            ),
            [(16, 16, 128)] * 2,
            [(5,) + tiny] + [tiny] * 6 + [(5, 64, 128)]
            + [low] * 3 + [(256, 128)] + [mid] * 3 + [(512, 128)] + [big] * 3 + [(512, 128)]
            + [low] * 6 + [mid] * 6 + [big] * 6 + [(16, 16, 128)] * 3,
            28,
            far_in=range(1, 20),
            far_out=(0, 1),
            copies=21,
        )
    )


def solution(mesh):
    spec = P("gx", "gy", "gz")
    return jax.shard_map(
        local, mesh=mesh, in_specs=(spec, spec), out_specs=(spec, spec), check_vma=False
    )
```
